32 devices in a mesh: dp: 2 (over core), expert: 16 (over z, y, x).
Axes of the slice: x: 2, y: 2, z: 4, core: 2. Of those that a mesh axis runs over, the one named last changes fastest.
Arguments:
- hidden: bfloat16 [4096, 2048], P(('dp', 'expert')), may hold values from -6 to 6
- lengths: int32 [2, 3], P('dp'), may hold values from 1 to 1024, 2048 in all within a row
- slots: int32 [4096], P('dp'), may hold values from 0 to 2047, as said below
- routes: int32 [4096, 8], P(('dp', 'expert')), may hold values from 0 to 15, all different within a row
- order: int32 [4096, 8], P(('dp', 'expert')), may hold values from 0 to 1023, as said below
- gain_in: bfloat16 [2048], P(('dp', 'expert')), may hold values from 0.099609375 to 1.8984375
- w_query: bfloat16 [2048, 4096], P(('dp', 'expert')), may hold values from -0.125 to 0.125
- key_projection_weight: bfloat16 [2048, 512], P(('dp', 'expert')), may hold values from -0.125 to 0.125
- value_projection_weight: bfloat16 [2048, 512], P(('dp', 'expert')), may hold values from -0.125 to 0.125
- gain_q: bfloat16 [128], P(('dp', 'expert')), may hold values from 0.099609375 to 1.8984375
- gain_k: bfloat16 [128], P(('dp', 'expert')), may hold values from 0.099609375 to 1.8984375
- w_out: bfloat16 [4096, 2048], P(('dp', 'expert')), may hold values from -0.75 to 0.75
- gain_mid: bfloat16 [2048], P(('dp', 'expert')), may hold values from 0.099609375 to 1.8984375
- w_router: bfloat16 [2048, 16], P(('dp', 'expert')), may hold values from -0.0625 to 0.0625
- w_gate: bfloat16 [16, 2048, 768], P('expert', 'dp'), may hold values from -0.125 to 0.125
- w_up: bfloat16 [16, 2048, 768], P('expert', 'dp'), may hold values from -0.125 to 0.125
- w_down: bfloat16 [16, 768, 2048], P('expert', None, 'dp'), may hold values from -0.625 to 0.625
- cotangent: bfloat16 [4096, 2048], P(('dp', 'expert')), may hold values from -6 to 6
Outputs:
- result: bfloat16 [4096, 2048], P(('dp', 'expert'))
- grad_hidden: bfloat16 [4096, 2048], P(('dp', 'expert'))
- grad_gain_in: float32 [2048], P(('dp', 'expert'))
- grad_w_query: float32 [2048, 4096], P(('dp', 'expert'))
- grad_w_key: float32 [2048, 512], P(('dp', 'expert'))
- grad_w_value: float32 [2048, 512], P(('dp', 'expert'))
- grad_gain_q: float32 [128], P(('dp', 'expert'))
- grad_gain_k: float32 [128], P(('dp', 'expert'))
- grad_w_out: float32 [4096, 2048], P(('dp', 'expert'))
- grad_gain_mid: float32 [2048], P(('dp', 'expert'))
- grad_w_router: float32 [2048, 16], P(('dp', 'expert'))
- grad_w_gate: float32 [16, 2048, 768], P('expert', 'dp')
- grad_w_up: float32 [16, 2048, 768], P('expert', 'dp')
- grad_w_down: float32 [16, 768, 2048], P('expert', None, 'dp')
The draws below stay inside these ranges and needn't reach their ends.
Inputs may be any that keep to these rules, and one draw needn't show every extreme that they name: `slots`: within the 2048 rows of each index of dp, every place 0 to 2047 occurs once. `lengths`: each row sums to 2048; its largest entry is 1024. `routes`: A token's 8 experts are different. `order`: within the 128 rows of each device, every number 0 to 1023 occurs once.
All inputs are finite; a program needn't handle non-finite values.
Results may differ from the reference program's by a relative error of at most 0.017.
Values may be sent and summed in bfloat16 or wider, within the bound.
No kernel may reach another device: no remote copies, remote signals or barrier semaphores. Data moves between devices by JAX's collectives and lax.ppermute only.
A program may use at most 384 MiB of HBM per device.

```python
import math
import jax
import jax.numpy as jnp
import numpy as np
from jax import lax

MODEL_WIDTH = 2048
QUERY_HEADS = 32
KEY_VALUE_HEADS = 4
HEAD_SIZE = 128
FF = 768
TOP = 8
TOK_DEV = 128
EXPERTS = 16
GROUP_TOKENS = 2048
TOTAL_TOKENS = 4096
MOST_LEN = 1024
NSEQ = 3
CAP = 72
N_DP = 2
DEVICES = 32


def shuffled_rows(key, count, width):
    keys = jax.random.split(key, count)

    def one_row(single):
        return jax.random.permutation(single, width)
    return jax.vmap(one_row)(keys).astype(jnp.int32)


def draw_slots(key, part):
    key = jax.random.fold_in(key, 5)
    return shuffled_rows(key, N_DP, GROUP_TOKENS).reshape(TOTAL_TOKENS)


def draw_order(key, part):
    key = jax.random.fold_in(key, 9)
    return shuffled_rows(key, DEVICES, TOK_DEV * TOP).reshape(TOTAL_TOKENS, TOP)


def levels(own_key, dims, pieces, smallest, largest):
    factor_of = 1.0
    for dim, blocks in pieces:
        draws = jax.random.uniform(jax.random.fold_in(jax.random.fold_in(own_key, 6), dim), (blocks,), jnp.float32, smallest / len(pieces), largest / len(pieces))
        factor_of = factor_of * jnp.repeat(jnp.exp(draws), dims[dim] // blocks).reshape((-1,) + (1,) * (len(dims) - 1 - dim))
    return factor_of


def different_ones(key, rows, number_of, top, lift):
    order = jax.random.permutation(jax.random.fold_in(key, 1), number_of)
    favour = order
    for power in range(3):
        favour = favour * favour // number_of
    favour = favour * lift // number_of
    lots = jax.random.randint(jax.random.fold_in(key, 2), (rows, number_of), 0, 4096) + favour
    sure = jax.random.permutation(jax.random.fold_in(key, 3), rows)[jnp.arange(number_of) % rows]
    lots = jnp.where(jnp.arange(rows)[:, None] == sure[None, :], 1 << 14, lots)
    priority = lots * number_of + jnp.arange(number_of)
    return lax.top_k(priority.astype(jnp.int32), top)[1].astype(jnp.int32)


def length_profile(count, total, most, lean):
    loads = [(1 << 20) // math.isqrt(standing ** lean) + 1 for standing in range(2, count + 1)]
    surplus, given = total - most - (count - 1), [1] * (count - 1)
    while surplus > 0:
        free = [i for i in range(count - 1) if given[i] < most]
        pool, left = sum([loads[i] for i in free]), surplus
        for i in free:
            more = min(most - given[i], max(1, left * loads[i] // pool), surplus)
            given[i] = given[i] + more
            surplus = surplus - more
    return np.array([most] + given)


def ragged_sizes(stream_key, count, total, bound, skew):
    if count == 2:
        one = jax.random.randint(stream_key, (), max(1, total - bound), min(bound, total - 1) + 1)
        return jnp.stack([one, total - one])
    sizes = jnp.asarray(length_profile(count, total, bound, skew), jnp.int32)
    pairs = (count - 1) // 2
    source_of, sink = sizes[1:1 + 2 * pairs:2], sizes[2:2 + 2 * pairs:2]
    margin = jnp.minimum(source_of - 1, bound - sink)
    moved = jax.random.randint(jax.random.fold_in(stream_key, 1), (pairs,), 0, 1 << 20) % (margin + 1)
    sizes = sizes.at[1:1 + 2 * pairs:2].set(source_of - moved).at[2:2 + 2 * pairs:2].set(sink + moved)
    return sizes[jax.random.permutation(jax.random.fold_in(stream_key, 2), count)]


def scatter_about(stream_key, extent, deviation, limit, pieces=(), kind=jnp.bfloat16):
    drawn = deviation * jax.random.normal(stream_key, extent, jnp.float32)
    if pieces:
        drawn = drawn * levels(stream_key, extent, pieces, -0.22, 0.18)
    return jnp.clip(drawn, -limit, limit).astype(kind)


def setup_inputs(seed: int = 0) -> dict:
    key_list = jax.random.split(jax.random.key(seed), 19)
    return {
        "hidden": scatter_about(key_list[0], (TOTAL_TOKENS, MODEL_WIDTH), 1.0, 6.0, ((0, 32),)),
        "lengths": jax.vmap(lambda own: ragged_sizes(own, NSEQ, GROUP_TOKENS, MOST_LEN, 2))(jax.random.split(key_list[1], N_DP)).reshape((N_DP, NSEQ)).astype(jnp.int32),
        "slots": draw_slots(jax.random.fold_in(key_list[18], 71), 0),
        "routes": different_ones(key_list[3], TOTAL_TOKENS, EXPERTS, TOP, 4096),
        "order": draw_order(jax.random.fold_in(key_list[18], 71), 0),
        "gain_in": jnp.clip(1.0 + 0.18 * jax.random.normal(key_list[5], (MODEL_WIDTH,), jnp.float32), 0.099609375, 1.8984375).astype(jnp.bfloat16),
        "w_query": scatter_about(key_list[6], (MODEL_WIDTH, QUERY_HEADS * HEAD_SIZE), MODEL_WIDTH ** -0.5, 0.125, ((0, 32),)),
        "key_projection_weight": scatter_about(key_list[7], (MODEL_WIDTH, KEY_VALUE_HEADS * HEAD_SIZE), MODEL_WIDTH ** -0.5, 0.125, ((0, 32),)),
        "value_projection_weight": scatter_about(key_list[8], (MODEL_WIDTH, KEY_VALUE_HEADS * HEAD_SIZE), MODEL_WIDTH ** -0.5, 0.125, ((0, 32),)),
        "gain_q": jnp.clip(1.0 + 0.18 * jax.random.normal(key_list[9], (HEAD_SIZE,), jnp.float32), 0.099609375, 1.8984375).astype(jnp.bfloat16),
        "gain_k": jnp.clip(1.0 + 0.18 * jax.random.normal(key_list[10], (HEAD_SIZE,), jnp.float32), 0.099609375, 1.8984375).astype(jnp.bfloat16),
        "w_out": scatter_about(key_list[11], (QUERY_HEADS * HEAD_SIZE, MODEL_WIDTH), (QUERY_HEADS * HEAD_SIZE // 64) ** -0.5, 0.75, ((0, 32),)),
        "gain_mid": jnp.clip(1.0 + 0.18 * jax.random.normal(key_list[12], (MODEL_WIDTH,), jnp.float32), 0.099609375, 1.8984375).astype(jnp.bfloat16),
        "w_router": scatter_about(key_list[13], (MODEL_WIDTH, EXPERTS), (4 * MODEL_WIDTH) ** -0.5, 0.0625, ((0, 32),)),
        "w_gate": scatter_about(key_list[14], (EXPERTS, MODEL_WIDTH, FF), MODEL_WIDTH ** -0.5, 0.125, ((0, 16), (1, 2))),
        "w_up": scatter_about(key_list[15], (EXPERTS, MODEL_WIDTH, FF), MODEL_WIDTH ** -0.5, 0.125, ((0, 16), (1, 2))),
        "w_down": scatter_about(key_list[16], (EXPERTS, FF, MODEL_WIDTH), (FF // 8) ** -0.5, 0.625, ((0, 16), (2, 2))),
        "cotangent": scatter_about(key_list[17], (TOTAL_TOKENS, MODEL_WIDTH), 1.0, 6.0, ((0, 32),)),
    }


EPS = 1e-06
THETA = 1000000.0
MASKED = -1e+30

@jax.custom_vjp
def reduced_rows(v):
    return lax.optimization_barrier(v.astype(jnp.bfloat16)).astype(jnp.float32)

@jax.custom_vjp
def reduced_rows_gradient(v):
    return v

def low_keep(v):
    return (reduced_rows(v), None)

def low_pass(kept, grad):
    return (grad,)

def back_keep(v):
    return (v, None)

def back_low(kept, grad):
    return (reduced_rows(grad),)
reduced_rows.defvjp(low_keep, low_pass)
reduced_rows_gradient.defvjp(back_keep, back_low)

def matrix_product(left, right):
    return jnp.dot(left, right, precision=lax.Precision.HIGHEST)

def rms_scale(values, scaling):
    return values * lax.rsqrt(lax.optimization_barrier(jnp.mean(values * values, axis=-1, keepdims=True)) + EPS) * scaling

def rotate(values, cosine, sine_table):
    half = values.shape[-1] // 2
    turned = jnp.concatenate([-values[..., half:], values[..., :half]], axis=-1)
    return values * cosine + turned * sine_table

def rotary_tables(position, width):
    index_float = jnp.arange(width // 2, dtype=jnp.float32)
    freq = jnp.power(jnp.float32(THETA), -2.0 * index_float / width)
    angle = position.astype(jnp.float32)[:, None] * freq[None, :]
    cosine = jnp.concatenate([jnp.cos(angle), jnp.cos(angle)], axis=-1)[:, None, :]
    sine_table = jnp.concatenate([jnp.sin(angle), jnp.sin(angle)], axis=-1)[:, None, :]
    return (cosine, sine_table)

def places(slot_rows, lengths_row):
    seq_ends = jnp.cumsum(lengths_row).astype(jnp.int32)
    starts = (seq_ends - lengths_row).astype(jnp.int32)
    segment = lax.optimization_barrier(jnp.sum((slot_rows[:, None] >= seq_ends[None, :]).astype(jnp.int32), axis=1)).astype(jnp.int32)
    chosen = segment[:, None] == jnp.arange(lengths_row.shape[0], dtype=jnp.int32)[None, :]
    start_of = lax.optimization_barrier(jnp.sum(jnp.where(chosen, starts[None, :], 0), axis=1)).astype(jnp.int32)
    return (segment, (slot_rows - start_of).astype(jnp.int32))

def fill_slots(route_rows, order_rows, experts, capacity):
    pair_count = route_rows.shape[0] * route_rows.shape[1]
    expert_of = route_rows.reshape(pair_count)
    order_key = order_rows.reshape(pair_count)
    numbered = jnp.arange(pair_count, dtype=jnp.int32)
    inverse = jnp.zeros((pair_count,), jnp.int32).at[order_key].set(numbered)
    ordered = expert_of[inverse]
    onehot = (ordered[:, None] == jnp.arange(experts, dtype=jnp.int32)[None, :]).astype(jnp.int32)
    running = jnp.cumsum(onehot, axis=0).astype(jnp.int32)
    rank_of = (lax.optimization_barrier(jnp.sum(running * onehot, axis=1)).astype(jnp.int32) - 1)[order_key]
    kept_pairs = rank_of < capacity
    slot_id = jnp.where(kept_pairs, expert_of * capacity + rank_of, experts * capacity).astype(jnp.int32)
    return (kept_pairs, slot_id)

def reference(hidden, lengths, slots, routes, order, gain_in, w_query, key_projection_weight, value_projection_weight, gain_q, gain_k, w_out, gain_mid, w_router, w_gate, w_up, w_down, cotangent):
    score_scale = HEAD_SIZE ** (-0.5)
    query_heads_per_group = QUERY_HEADS // KEY_VALUE_HEADS
    query_block_rows = min(128, GROUP_TOKENS)
    segment_parts = []
    position_parts = []
    for group_index in range(N_DP):
        seg_part, pos_part = places(slots[group_index * GROUP_TOKENS:(group_index + 1) * GROUP_TOKENS], lengths[group_index])
        segment_parts.append(seg_part)
        position_parts.append(pos_part)
    segment = jnp.concatenate(segment_parts)
    position = jnp.concatenate(position_parts)
    cosine, sine_table = rotary_tables(position, HEAD_SIZE)

    def device_fill(route_rows, order_rows):
        return fill_slots(route_rows, order_rows, EXPERTS, CAP)
    kept_pairs, slot_id = jax.vmap(device_fill)(routes.reshape(DEVICES, TOK_DEV, TOP), order.reshape(DEVICES, TOK_DEV, TOP))
    pair_count = TOK_DEV * TOP
    token_local = jnp.arange(pair_count, dtype=jnp.int32) // TOP
    device_number = jnp.arange(DEVICES, dtype=jnp.int32)

    def slot_table(slot_row, device_id):
        source = jnp.zeros((EXPERTS * CAP + 1,), jnp.int32).at[slot_row].set(token_local + device_id * TOK_DEV)[:EXPERTS * CAP]
        filled = jnp.zeros((EXPERTS * CAP + 1,), jnp.int32).at[slot_row].set(1)[:EXPERTS * CAP]
        return (source, filled)
    source, filled = jax.vmap(slot_table)(slot_id, device_number)
    source = source.reshape(DEVICES, EXPERTS, CAP).transpose(1, 0, 2).reshape(EXPERTS, DEVICES * CAP)
    filled = filled.reshape(DEVICES, EXPERTS, CAP).transpose(1, 0, 2).reshape(EXPERTS, DEVICES * CAP)
    expert_of = routes.reshape(DEVICES, pair_count)
    rank_of = slot_id - expert_of * CAP
    flat_index = jnp.where(kept_pairs, expert_of * (DEVICES * CAP) + device_number[:, None] * CAP + rank_of, 0).astype(jnp.int32).reshape(TOTAL_TOKENS, TOP)
    kept_rows = kept_pairs.reshape(TOTAL_TOKENS, TOP)
    chooser = routes[:, :, None] == jnp.arange(EXPERTS, dtype=jnp.int32)[None, None, :]

    def forward(x_in, norm_in, query_w, key_weight_local, value_weight_local, norm_q, norm_k, out_w, norm_mid, router_w, gate_w, up_w, down_w):
        normalized_input_first = reduced_rows(rms_scale(x_in, norm_in))
        query_proj = reduced_rows_gradient(matrix_product(normalized_input_first, query_w)).reshape(TOTAL_TOKENS, QUERY_HEADS, HEAD_SIZE)
        key_projected = reduced_rows_gradient(matrix_product(normalized_input_first, key_weight_local)).reshape(TOTAL_TOKENS, KEY_VALUE_HEADS, HEAD_SIZE)
        value_reduced = reduced_rows(reduced_rows_gradient(matrix_product(normalized_input_first, value_weight_local))).reshape(TOTAL_TOKENS, KEY_VALUE_HEADS, HEAD_SIZE)
        query_reduced = reduced_rows(rotate(rms_scale(query_proj, norm_q), cosine, sine_table))
        key_low = reduced_rows(rotate(rms_scale(key_projected, norm_k), cosine, sine_table))
        attended_parts = []
        for group_index in range(N_DP):
            first_token = group_index * GROUP_TOKENS
            last_token = first_token + GROUP_TOKENS
            key_group = key_low[first_token:last_token]
            value_group = value_reduced[first_token:last_token]
            seg_group = segment[first_token:last_token]
            slot_group = slots[first_token:last_token]
            query_head_group = query_reduced[first_token:last_token].reshape(GROUP_TOKENS // query_block_rows, query_block_rows, KEY_VALUE_HEADS, query_heads_per_group, HEAD_SIZE)
            seg_blocks = seg_group.reshape(GROUP_TOKENS // query_block_rows, query_block_rows)
            slot_blocks = slot_group.reshape(GROUP_TOKENS // query_block_rows, query_block_rows)

            def attend(block_items):
                query_rows, seg_rows, slot_rows = block_items
                scores = jnp.einsum('qhrd,khd->hrqk', query_rows, key_group, precision=lax.Precision.HIGHEST) * score_scale
                scores = reduced_rows_gradient(scores)
                visible = (seg_rows[:, None] == seg_group[None, :]) & (slot_group[None, :] <= slot_rows[:, None])
                probs = jax.nn.softmax(jnp.where(visible[None, None], scores, MASKED), axis=-1)
                mixed_rows = jnp.einsum('hrqk,khd->qhrd', reduced_rows(probs), value_group, precision=lax.Precision.HIGHEST)
                return mixed_rows.reshape(query_block_rows, QUERY_HEADS * HEAD_SIZE)
            attended_parts.append(lax.map(jax.checkpoint(attend), (query_head_group, seg_blocks, slot_blocks)).reshape(GROUP_TOKENS, QUERY_HEADS * HEAD_SIZE))
        attended = reduced_rows(reduced_rows_gradient(jnp.concatenate(attended_parts, axis=0)))
        x_one = x_in + reduced_rows_gradient(matrix_product(attended, out_w))
        xn_two = reduced_rows(rms_scale(x_one, norm_mid))
        logits = reduced_rows_gradient(matrix_product(xn_two, router_w))
        chosen = lax.optimization_barrier(jnp.sum(jnp.where(chooser, logits[:, None, :], 0.0), axis=-1))
        gate_probs = jax.nn.softmax(chosen, axis=-1)

        def expert(expert_items):
            source_rows, filled_rows, gate_matrix, up_matrix, down_matrix = expert_items
            rows_in = reduced_rows_gradient(jnp.where(filled_rows[:, None] > 0, xn_two[source_rows], 0.0))
            gate_pre = reduced_rows_gradient(matrix_product(rows_in, gate_matrix))
            up_pre = reduced_rows_gradient(matrix_product(rows_in, up_matrix))
            activation = reduced_rows(jax.nn.silu(gate_pre) * up_pre)
            return reduced_rows(reduced_rows_gradient(matrix_product(activation, down_matrix)))
        expert_rows = lax.map(jax.checkpoint(expert), (source, filled, gate_w, up_w, down_w)).reshape(EXPERTS * DEVICES * CAP, MODEL_WIDTH)
        mixture = x_one
        for pick_index in range(TOP):
            picked = expert_rows[flat_index[:, pick_index]]
            mixture = mixture + jnp.where(kept_rows[:, pick_index:pick_index + 1], gate_probs[:, pick_index:pick_index + 1] * picked, 0.0)
        return mixture
    floats = tuple((item.astype(jnp.float32) for item in (hidden, gain_in, w_query, key_projection_weight, value_projection_weight, gain_q, gain_k, w_out, gain_mid, w_router, w_gate, w_up, w_down)))
    mixed, pullback = jax.vjp(forward, *floats)
    grads = pullback(cotangent.astype(jnp.float32))
    return (mixed.astype(jnp.bfloat16), grads[0].astype(jnp.bfloat16), grads[1], grads[2], grads[3], grads[4], grads[5], grads[6], grads[7], grads[8], grads[9], grads[10], grads[11], grads[12])
```

```python
import jax
import jax.numpy as jnp
from jax import lax
from jax.sharding import PartitionSpec as P

MODEL_WIDTH = 2048
QUERY_HEADS = 32
KEY_VALUE_HEADS = 4
HEAD_SIZE = 128
TOP = 8
PER_KV = QUERY_HEADS // KEY_VALUE_HEADS
QW = PER_KV * HEAD_SIZE

EPS = 1e-06
THETA = 1000000.0
MASKED = -1e30
BF = jnp.bfloat16
F32 = jnp.float32


def rms_scale(values, scaling):
    return values * lax.rsqrt(jnp.mean(values * values, axis=-1, keepdims=True) + EPS) * scaling


def rotate(values, cosine, sine_table):
    half = values.shape[-1] // 2
    turned = jnp.concatenate([-values[..., half:], values[..., :half]], axis=-1)
    return values * cosine + turned * sine_table


def rotary_tables(position, width):
    index_float = jnp.arange(width // 2, dtype=jnp.float32)
    freq = jnp.power(jnp.float32(THETA), -2.0 * index_float / width)
    angle = position.astype(jnp.float32)[:, None] * freq[None, :]
    cosine = jnp.concatenate([jnp.cos(angle), jnp.cos(angle)], axis=-1)[:, None, :]
    sine_table = jnp.concatenate([jnp.sin(angle), jnp.sin(angle)], axis=-1)[:, None, :]
    return (cosine, sine_table)


def places(slot_rows, lengths_row):
    seq_ends = jnp.cumsum(lengths_row)
    starts = seq_ends - lengths_row
    segment = jnp.sum((slot_rows[:, None] >= seq_ends[None, :]).astype(jnp.int32), axis=1)
    chosen = segment[:, None] == jnp.arange(lengths_row.shape[0], dtype=jnp.int32)[None, :]
    start_of = jnp.sum(jnp.where(chosen, starts[None, :], 0), axis=1)
    return (segment, slot_rows - start_of)


def pick(blocks, index):
    return lax.dynamic_index_in_dim(blocks, index, 0, keepdims=False)


def put(buffer, block, index):
    return lax.dynamic_update_index_in_dim(buffer, block, index, 0)


class Links:
    def __init__(self, n):
        self.n = n
        self.planes = n // KEY_VALUE_HEADS
        index = lax.axis_index("expert")
        self.g = lax.axis_index("dp")
        self.index = index
        self.a = index // KEY_VALUE_HEADS
        self.b = index % KEY_VALUE_HEADS

    def flip(self, value, k):
        return lax.ppermute(value, "expert", [(i, i ^ k) for i in range(self.n)])

    def onward(self, value):
        step = KEY_VALUE_HEADS
        return lax.ppermute(value, "expert", [(i, (i + step) % self.n) for i in range(self.n)])

    def twin(self, value):
        return lax.ppermute(value, "dp", [(0, 1), (1, 0)])

    def plane_gather(self, own):
        half = own.shape[0] // 2
        near_x = self.flip(own, 1)
        near_y = self.flip(own, 2)
        far_low = self.flip(near_x[:half], 2)
        far_high = self.flip(near_y[half:], 1)
        out = jnp.zeros((4,) + own.shape, own.dtype)
        out = put(out, own, self.b)
        out = put(out, near_x, self.b ^ 1)
        out = put(out, near_y, self.b ^ 2)
        return put(out, jnp.concatenate([far_low, far_high], axis=0), self.b ^ 3)

    def plane_exchange(self, blocks):
        out = jnp.zeros_like(blocks)
        out = put(out, pick(blocks, self.b), self.b)
        for k in (3, 1, 2):
            out = put(out, self.flip(pick(blocks, self.b ^ k), k), self.b ^ k)
        return out

    def plane_scatter(self, blocks):
        half = blocks.shape[1] // 2
        far = pick(blocks, self.b ^ 3)
        to_x = pick(blocks, self.b ^ 1)
        to_y = pick(blocks, self.b ^ 2)
        low = self.flip(far[:half], 2)
        high = self.flip(far[half:], 1)
        to_x = jnp.concatenate(
            [(to_x[:half].astype(F32) + low.astype(F32)).astype(BF), to_x[half:]], axis=0
        )
        to_y = jnp.concatenate(
            [to_y[:half], (to_y[half:].astype(F32) + high.astype(F32)).astype(BF)], axis=0
        )
        got_x = self.flip(to_x, 1)
        got_y = self.flip(to_y, 2)
        return pick(blocks, self.b).astype(F32) + got_x.astype(F32) + got_y.astype(F32)

    def line_gather(self, own):
        out = jnp.zeros((self.planes,) + own.shape, own.dtype)
        out = put(out, own, self.a)
        piece = own
        for step in range(1, self.planes):
            piece = self.onward(piece)
            out = put(out, piece, (self.a - step) % self.planes)
        return out

    def line_scatter(self, block_of):
        total = block_of((self.a - 1) % self.planes)
        for step in range(1, self.planes):
            came = self.onward(total.astype(BF))
            total = block_of((self.a - 1 - step) % self.planes) + came.astype(F32)
        return total

    def group_gather(self, own):
        out = jnp.zeros((self.planes, 4) + own.shape, own.dtype)
        piece = own
        for step in range(self.planes):
            if step:
                piece = self.onward(piece)
            out = put(out, self.plane_gather(piece), (self.a - step) % self.planes)
        return out

    def group_scatter(self, blocks):
        return self.line_scatter(lambda j: self.plane_scatter(pick(blocks, j)))

    def twin_gather(self, own):
        other = self.twin(own)
        first = self.g == 0
        return jnp.stack([jnp.where(first, own, other), jnp.where(first, other, own)])

    def twin_scatter(self, halves):
        return pick(halves, self.g) + self.twin(pick(halves, 1 - self.g).astype(BF)).astype(F32)


def body(
    hidden,
    lengths,
    slots,
    routes,
    order,
    gain_in,
    w_query,
    key_projection_weight,
    value_projection_weight,
    gain_q,
    gain_k,
    w_out,
    gain_mid,
    w_router,
    w_gate,
    w_up,
    w_down,
    cotangent,
):
    tokens = hidden.shape[0]
    experts = w_router.shape[1]
    links = Links(experts)
    planes = links.planes
    capacity = max(2, (tokens * TOP * 9 + 8 * experts - 1) // (8 * experts))
    score_scale = HEAD_SIZE ** (-0.5)
    block_tokens = 4 * tokens
    rows = gain_in.shape[0]
    head_part = gain_q.shape[0]
    devices = 2 * experts

    small = jnp.concatenate(
        [gain_in, gain_mid, gain_q, gain_k, w_router.reshape(rows * experts)], axis=0
    )
    small = lax.all_gather(small, ("dp", "expert"), axis=0, tiled=False)
    full_in = small[:, :rows].reshape(MODEL_WIDTH).astype(F32)
    full_mid = small[:, rows : 2 * rows].reshape(MODEL_WIDTH).astype(F32)
    at = 2 * rows
    full_qgain = small[:, at : at + head_part].reshape(HEAD_SIZE).astype(F32)
    at = at + head_part
    full_kgain = small[:, at : at + head_part].reshape(HEAD_SIZE).astype(F32)
    at = at + head_part
    full_router = small[:, at:].reshape(MODEL_WIDTH, experts)

    pairs = lax.all_gather(order * experts + routes, "expert", axis=0, tiled=True)

    block_hidden = links.plane_gather(hidden).reshape(block_tokens, MODEL_WIDTH)

    own_columns = jnp.concatenate(
        [
            w_query.reshape(rows, 4, QW),
            key_projection_weight.reshape(rows, 4, HEAD_SIZE),
            value_projection_weight.reshape(rows, 4, HEAD_SIZE),
        ],
        axis=2,
    ).transpose(1, 0, 2)
    qkv_width = QW + 2 * HEAD_SIZE
    w_qkv = links.plane_exchange(own_columns)
    w_qkv = links.line_gather(w_qkv)
    w_qkv = links.twin_gather(w_qkv).reshape(MODEL_WIDTH, qkv_width)

    head_rows = w_out.shape[0]
    to_block = []
    for g in range(2):
        for a in range(planes):
            for b in range(4):
                to_block.append(((b * 2 + g) * planes + a, g * experts + a * 4 + b))
    block_out = lax.ppermute(w_out, ("dp", "expert"), to_block)
    block_out = links.line_gather(block_out)
    block_out = links.twin_gather(block_out).reshape(QW, MODEL_WIDTH)

    gate_full = lax.all_gather(w_gate, "dp", axis=1, tiled=True)[0]
    up_full = lax.all_gather(w_up, "dp", axis=1, tiled=True)[0]
    down_full = lax.all_gather(w_down, "dp", axis=2, tiled=True)[0]

    upstream_all = links.group_gather(cotangent).reshape(experts, tokens, MODEL_WIDTH)

    block_slots = lax.dynamic_slice_in_dim(slots, links.a * block_tokens, block_tokens)
    seg_query, position = places(block_slots, lengths[0])
    seg_key, _ = places(slots, lengths[0])
    cosine, sine_table = rotary_tables(position, HEAD_SIZE)
    visible = (seg_query[:, None] == seg_key[None, :]) & (slots[None, :] <= block_slots[:, None])

    block_float = block_hidden.astype(F32)
    normalized = rms_scale(block_float, full_in).astype(BF)
    projected = jnp.dot(normalized, w_qkv, preferred_element_type=F32)
    query_proj = projected[:, :QW].reshape(block_tokens, PER_KV, HEAD_SIZE)
    key_proj = projected[:, QW : QW + HEAD_SIZE].reshape(block_tokens, 1, HEAD_SIZE)
    value_low = projected[:, QW + HEAD_SIZE :].astype(BF)

    def head_norm(values, scaling):
        return rotate(rms_scale(values, scaling), cosine, sine_table)

    query_turned, query_back = jax.vjp(head_norm, query_proj, full_qgain)
    key_turned, key_back = jax.vjp(head_norm, key_proj, full_kgain)
    key_low = key_turned.astype(BF).reshape(block_tokens, HEAD_SIZE)
    keys_values = links.line_gather(jnp.concatenate([key_low, value_low], axis=1)).reshape(
        planes * block_tokens, 2 * HEAD_SIZE
    )
    keys, values = keys_values[:, :HEAD_SIZE], keys_values[:, HEAD_SIZE:]
    query_heads = query_turned.astype(BF).transpose(1, 0, 2)

    def forward_head(query_rows):
        scores = (
            jnp.einsum("qd,kd->qk", query_rows, keys, preferred_element_type=F32) * score_scale
        )
        scores = jnp.where(visible, scores, MASKED)
        top_score = jnp.max(scores, axis=-1, keepdims=True)
        exponent = jnp.exp(scores - top_score)
        row_total = jnp.sum(exponent, axis=-1, keepdims=True)
        weights = (exponent / row_total).astype(BF)
        mixed_rows = jnp.einsum("qk,kd->qd", weights, values, preferred_element_type=F32)
        return (mixed_rows.astype(BF), top_score + jnp.log(row_total))

    attended_heads, log_sums = lax.map(forward_head, query_heads)
    attended = attended_heads.transpose(1, 0, 2).reshape(block_tokens, QW)

    branch = jnp.dot(attended, block_out, preferred_element_type=F32).astype(BF)
    branch = links.plane_scatter(branch.reshape(4, tokens, MODEL_WIDTH))
    x_float = hidden.astype(F32)
    x_one = x_float + branch
    norm_two, norm_two_back = jax.vjp(rms_scale, x_one, full_mid)
    xn_two = norm_two.astype(BF)

    rows_all = links.group_gather(xn_two).reshape(experts, tokens, MODEL_WIDTH)
    pair_routes = pairs % experts
    pair_order = pairs // experts
    hit = pair_routes == links.index
    routed = jnp.any(hit, axis=1).reshape(experts, tokens)
    place = jnp.sum(jnp.where(hit, pair_order, 0), axis=1).reshape(experts, tokens)
    before = routed[:, None, :] & (place[:, None, :] < place[:, :, None])
    rank = jnp.sum(before.astype(jnp.int32), axis=2)
    slot_numbers = jnp.arange(capacity, dtype=jnp.int32)
    select = (rank[:, None, :] == slot_numbers[None, :, None]) & routed[:, None, :]
    select_low = select.astype(BF)

    logits = jnp.dot(
        rows_all.reshape(experts * tokens, MODEL_WIDTH), full_router, preferred_element_type=F32
    )
    expert_numbers = jnp.arange(experts, dtype=jnp.int32)
    chooser = jnp.any(pair_routes[:, :, None] == expert_numbers[None, None, :], axis=1)
    chosen_top = jnp.max(jnp.where(chooser, logits, MASKED), axis=-1, keepdims=True)
    chosen_exp = jnp.where(chooser, jnp.exp(jnp.where(chooser, logits - chosen_top, 0.0)), 0.0)
    probs_all = chosen_exp / jnp.sum(chosen_exp, axis=-1, keepdims=True)
    own_probs = lax.dynamic_slice_in_dim(probs_all, links.index * tokens, tokens)
    expert_probs = jnp.sum(
        jnp.where(expert_numbers[None, :] == links.index, probs_all, 0.0), axis=1
    ).reshape(experts, tokens)
    slot_probs = jnp.sum(jnp.where(select, expert_probs[:, None, :], 0.0), axis=2)
    slot_count = experts * capacity

    def to_slots(all_rows):
        return (
            jnp.einsum("sct,std->scd", select_low, all_rows, preferred_element_type=F32)
            .astype(BF)
            .reshape(slot_count, MODEL_WIDTH)
        )

    def to_tokens(slot_rows):
        return (
            jnp.einsum(
                "sct,scd->std",
                select_low,
                slot_rows.reshape(experts, capacity, MODEL_WIDTH),
                preferred_element_type=F32,
            )
            .astype(BF)
            .reshape(planes, 4, tokens, MODEL_WIDTH)
        )

    slot_upstream = to_slots(upstream_all)
    arrived = to_slots(rows_all)
    gate_pre = jnp.dot(arrived, gate_full, preferred_element_type=F32)
    up_pre = jnp.dot(arrived, up_full, preferred_element_type=F32)
    activation = (jax.nn.silu(gate_pre) * up_pre).astype(BF)
    returned = jnp.dot(activation, down_full, preferred_element_type=F32).astype(BF)
    slot_probs_column = slot_probs.reshape(slot_count, 1)
    upstream_float = slot_upstream.astype(F32)
    out_grad = (slot_probs_column * upstream_float).astype(BF)
    act_grad = jnp.einsum("rd,fd->rf", out_grad, down_full, preferred_element_type=F32)
    logistic = jax.nn.sigmoid(gate_pre)
    gate_low = (act_grad * up_pre * logistic * (1.0 + gate_pre * (1.0 - logistic))).astype(BF)
    up_low = (act_grad * gate_pre * logistic).astype(BF)
    pair_grad = (
        jnp.einsum("rf,df->rd", gate_low, gate_full, preferred_element_type=F32)
        + jnp.einsum("rf,df->rd", up_low, up_full, preferred_element_type=F32)
    ).astype(BF)
    moe_grad = links.group_scatter(to_tokens(pair_grad))

    slot_gate_grad = jnp.sum(upstream_float * returned.astype(F32), axis=1).reshape(
        experts, capacity
    )
    gate_grads = jnp.sum(jnp.where(select, slot_gate_grad[:, :, None], 0.0), axis=1)
    gate_grads = lax.all_to_all(gate_grads, "expert", split_axis=0, concat_axis=0, tiled=True).T

    mixture = links.group_scatter(
        to_tokens((slot_probs_column * returned.astype(F32)).astype(BF))
    )
    result = (x_one + mixture).astype(BF)

    grad_down = jnp.einsum("rf,rd->fd", activation, out_grad, preferred_element_type=F32)
    grad_gate = jnp.einsum("rd,rf->df", arrived, gate_low, preferred_element_type=F32)
    grad_up = jnp.einsum("rd,rf->df", arrived, up_low, preferred_element_type=F32)
    ff = w_gate.shape[2]
    half_width = MODEL_WIDTH // 2
    grad_down = links.twin_scatter(grad_down.reshape(ff, 2, half_width).transpose(1, 0, 2))
    grad_gate = links.twin_scatter(grad_gate.reshape(2, half_width, ff))
    grad_up = links.twin_scatter(grad_up.reshape(2, half_width, ff))

    upstream = cotangent.astype(F32)
    chosen_grad = own_probs * (
        gate_grads - jnp.sum(own_probs * gate_grads, axis=-1, keepdims=True)
    )
    logit_grad = chosen_grad.astype(BF)
    grad_router = jnp.dot(xn_two.T, logit_grad, preferred_element_type=F32)
    xn_two_grad = moe_grad + jnp.dot(logit_grad, full_router.T, preferred_element_type=F32)
    x_one_norm_grad, grad_mid = norm_two_back(xn_two_grad)
    x_one_grad = upstream + x_one_norm_grad
    branch_grad = x_one_grad.astype(BF)

    block_grad = links.plane_gather(branch_grad).reshape(block_tokens, MODEL_WIDTH)
    attended_grad = jnp.einsum(
        "td,hd->th", block_grad, block_out, preferred_element_type=F32
    ).astype(BF)
    grad_heads = attended_grad.reshape(block_tokens, PER_KV, HEAD_SIZE).transpose(1, 0, 2)

    def backward_head(key_terms, head_items):
        query_rows, grad_rows, log_sum = head_items
        scores = (
            jnp.einsum("qd,kd->qk", query_rows, keys, preferred_element_type=F32) * score_scale
        )
        scores = jnp.where(visible, scores, MASKED)
        probs = jnp.exp(scores - log_sum)
        weights = probs.astype(BF)
        prob_grad = jnp.einsum("qd,kd->qk", grad_rows, values, preferred_element_type=F32)
        row_inner = jnp.sum(probs * prob_grad, axis=-1, keepdims=True)
        score_grad = (probs * (prob_grad - row_inner)).astype(BF)
        query_grad = (
            jnp.einsum("qk,kd->qd", score_grad, keys, preferred_element_type=F32) * score_scale
        )
        key_grad = (
            jnp.einsum("qk,qd->kd", score_grad, query_rows, preferred_element_type=F32)
            * score_scale
        )
        value_grad = jnp.einsum("qk,qd->kd", weights, grad_rows, preferred_element_type=F32)
        return ((key_terms[0] + key_grad, key_terms[1] + value_grad), query_grad)

    no_terms = jnp.zeros((planes * block_tokens, HEAD_SIZE), F32)
    key_terms, query_grads = lax.scan(
        backward_head, (no_terms, no_terms), (query_heads, grad_heads, log_sums)
    )
    key_terms = jnp.concatenate(key_terms, axis=1).reshape(planes, block_tokens, 2 * HEAD_SIZE)
    key_terms = links.line_scatter(lambda j: pick(key_terms, j))

    grad_out = jnp.einsum("th,td->hd", attended, block_grad, preferred_element_type=F32)
    grad_out = links.twin_scatter(grad_out.reshape(2, QW // 2, MODEL_WIDTH))
    grad_out = grad_out.astype(BF).reshape(planes, head_rows, MODEL_WIDTH)
    grad_out = links.line_scatter(lambda j: pick(grad_out, j).astype(F32)).astype(BF)
    grad_out = lax.ppermute(
        grad_out, ("dp", "expert"), [(there, here) for here, there in to_block]
    ).astype(F32)

    query_proj_grad, grad_qgain = query_back(query_grads.transpose(1, 0, 2))
    key_proj_grad, grad_kgain = key_back(key_terms[:, :HEAD_SIZE].reshape(key_proj.shape))
    proj_grad = jnp.concatenate(
        [
            query_proj_grad.reshape(block_tokens, QW).astype(BF),
            key_proj_grad.reshape(block_tokens, HEAD_SIZE).astype(BF),
            key_terms[:, HEAD_SIZE:].astype(BF),
        ],
        axis=1,
    )
    xn_one_grad = jnp.einsum("tc,dc->td", proj_grad, w_qkv, preferred_element_type=F32)
    xn_one_grad = links.plane_scatter(xn_one_grad.astype(BF).reshape(4, tokens, MODEL_WIDTH))
    _, norm_one_back = jax.vjp(rms_scale, x_float, full_in)
    x_norm_grad, grad_in = norm_one_back(xn_one_grad)
    input_grad = (x_one_grad + x_norm_grad).astype(BF)

    grad_qkv = jnp.einsum("td,tc->dc", normalized, proj_grad, preferred_element_type=F32)
    grad_qkv = links.twin_scatter(grad_qkv.reshape(2, MODEL_WIDTH // 2, qkv_width))
    grad_qkv = grad_qkv.astype(BF).reshape(planes, 4, rows, qkv_width)
    grad_qkv = links.line_scatter(lambda j: pick(grad_qkv, j).astype(F32)).astype(BF)
    grad_qkv = links.plane_exchange(grad_qkv).transpose(1, 0, 2).astype(F32)
    grad_query = grad_qkv[:, :, :QW].reshape(rows, 4 * QW)
    grad_key = grad_qkv[:, :, QW : QW + HEAD_SIZE].reshape(rows, 4 * HEAD_SIZE)
    grad_value = grad_qkv[:, :, QW + HEAD_SIZE :].reshape(rows, 4 * HEAD_SIZE)

    def sum_of(parts):
        packed = jnp.concatenate([part.reshape(devices, -1) for part in parts], axis=1)
        came = lax.all_to_all(packed, ("dp", "expert"), split_axis=0, concat_axis=0, tiled=True)
        return jnp.sum(came, axis=0)

    first = sum_of([grad_mid, grad_router])
    grad_mid = first[:rows]
    grad_router = first[rows:].reshape(rows, experts)
    last = sum_of([grad_in, grad_qgain, grad_kgain])
    grad_in = last[:rows]
    grad_qgain = last[rows : rows + head_part]
    grad_kgain = last[rows + head_part :]

    return (
        result,
        input_grad,
        grad_in,
        grad_query,
        grad_key,
        grad_value,
        grad_qgain,
        grad_kgain,
        grad_out,
        grad_mid,
        grad_router,
        grad_gate[None],
        grad_up[None],
        grad_down[None],
    )


def solution(mesh):
    every = ("dp", "expert")
    in_specs = (
        P(every, None),
        P("dp", None),
        P("dp"),
        P(every, None),
        P(every, None),
        P(every),
        P(every, None),
        P(every, None),
        P(every, None),
        P(every),
        P(every),
        P(every, None),
        P(every),
        P(every, None),
        P("expert", "dp", None),
        P("expert", "dp", None),
        P("expert", None, "dp"),
        P(every, None),
    )
    out_specs = (
        P(every, None),
        P(every, None),
        P(every),
        P(every, None),
        P(every, None),
        P(every, None),
        P(every),
        P(every),
        P(every, None),
        P(every),
        P(every, None),
        P("expert", "dp", None),
        P("expert", "dp", None),
        P("expert", None, "dp"),
    )
    return jax.shard_map(body, mesh=mesh, in_specs=in_specs, out_specs=out_specs, check_vma=False)
```

```python
import jax
import jax.numpy as jnp
from jax import lax
from jax.experimental import pallas as pl
from jax.experimental.pallas import tpu as pltpu
from jax.sharding import PartitionSpec as P

MODEL_WIDTH = 2048
QUERY_HEADS = 32
KEY_VALUE_HEADS = 4
HEAD_SIZE = 128
TOP = 8
PER_KV = QUERY_HEADS // KEY_VALUE_HEADS
QW = PER_KV * HEAD_SIZE

EPS = 1e-06
THETA = 1000000.0
MASKED = -1e30
BF = jnp.bfloat16
F32 = jnp.float32


def rms_scale(values, scaling):
    return values * lax.rsqrt(jnp.mean(values * values, axis=-1, keepdims=True) + EPS) * scaling


def rotary_tables(position):
    half = HEAD_SIZE // 2
    index_float = jnp.arange(half, dtype=jnp.float32)
    freq = jnp.power(jnp.float32(THETA), -2.0 * index_float / HEAD_SIZE)
    angle = position.astype(jnp.float32)[:, None] * freq[None, :]
    cosine, sine = jnp.cos(angle), jnp.sin(angle)
    return (
        jnp.concatenate([cosine, cosine], axis=-1),
        jnp.concatenate([-sine, sine], axis=-1),
    )


def project_kernel(planes, ids_ref, x_ref, cos_ref, sin_ref, gains_ref, *refs):
    pieces, (w_ref, proj_ref, turned_ref) = refs[: 2 * planes], refs[2 * planes :]
    mine_a, mine_b, mine_g = ids_ref[0], ids_ref[1], ids_ref[2]
    last = pl.program_id(0) == pl.num_programs(0) - 1
    rows = pieces[0].shape[0] // 4
    for number, piece in enumerate(pieces):
        g = mine_g ^ (number // planes)
        a = lax.rem(mine_a + planes - number % planes, planes)
        for k in range(4):
            at = pl.multiple_of(((g * planes + a) * 4 + (mine_b ^ k)) * rows, rows)
            w_ref[pl.ds(at, rows), :] = piece[k * rows : (k + 1) * rows, :]
    projected = jnp.dot(x_ref[...], w_ref[...], preferred_element_type=F32)
    proj_ref[...] = projected

    def turn(values, gain):
        scaled = (
            values * lax.rsqrt(jnp.mean(values * values, axis=-1, keepdims=True) + EPS) * gain
        )
        swapped = pltpu.roll(scaled, HEAD_SIZE // 2, 1)
        return scaled * cos_ref[...] + swapped * sin_ref[...]

    gain_q, gain_k = gains_ref[0:1], gains_ref[1:2]
    first, second = projected[:, :HEAD_SIZE], projected[:, HEAD_SIZE:]
    turned_ref[:, :HEAD_SIZE] = turn(first, jnp.where(last, gain_k, gain_q)).astype(BF)
    turned_ref[:, HEAD_SIZE:] = jnp.where(last, second, turn(second, gain_q)).astype(BF)


def project(ids, rows_in, cosine, sine, gains, *pieces):
    count, width = rows_in.shape
    height, columns = pieces[0].shape
    step = 2 * HEAD_SIZE
    whole = lambda array: pl.BlockSpec(array.shape, lambda i: (0, 0))
    strip = lambda height: pl.BlockSpec((height, step), lambda i: (0, i))
    return pl.pallas_call(
        lambda *refs: project_kernel(len(pieces) // 2, *refs),
        grid=(columns // step,),
        in_specs=[pl.BlockSpec(memory_space=pltpu.SMEM)]
        + [whole(rows_in), whole(cosine), whole(sine), whole(gains)]
        + [strip(height)] * len(pieces),
        out_specs=[strip(width), strip(count), strip(count)],
        out_shape=[
            jax.ShapeDtypeStruct((width, columns), BF),
            jax.ShapeDtypeStruct((count, columns), F32),
            jax.ShapeDtypeStruct((count, columns), BF),
        ],
        compiler_params=pltpu.CompilerParams(vmem_limit_bytes=32 * 2**20),
    )(ids, rows_in, cosine, sine, gains, *pieces)


def unturn_kernel(grad_ref, proj_ref, cos_ref, sin_ref, gain_ref, out_ref, gain_grad_ref):
    @pl.when(pl.program_id(0) == 0)
    def _():
        gain_grad_ref[...] = jnp.zeros_like(gain_grad_ref)

    grad, values = grad_ref[...], proj_ref[...]
    grad = grad * cos_ref[...] + pltpu.roll(grad * sin_ref[...], HEAD_SIZE // 2, 1)
    scale = lax.rsqrt(jnp.mean(values * values, axis=-1, keepdims=True) + EPS)
    gain_grad_ref[...] += jnp.sum(grad * values * scale, axis=0, keepdims=True)
    grad = grad * gain_ref[...]
    inner = jnp.mean(grad * values, axis=-1, keepdims=True)
    out_ref[...] = (scale * grad - values * (scale * scale * scale * inner)).astype(BF)


def unturn(grad, projected, first_head, cosine, sine, gain):
    count, columns = grad.shape
    block = (count, HEAD_SIZE)
    whole = lambda array: pl.BlockSpec(array.shape, lambda i: (0, 0))
    return pl.pallas_call(
        unturn_kernel,
        grid=(columns // HEAD_SIZE,),
        in_specs=[
            pl.BlockSpec(block, lambda i: (0, i)),
            pl.BlockSpec(block, lambda i: (0, i + first_head)),
            whole(cosine),
            whole(sine),
            whole(gain),
        ],
        out_specs=[pl.BlockSpec(block, lambda i: (0, i)), whole(gain)],
        out_shape=[
            jax.ShapeDtypeStruct((count, columns), BF),
            jax.ShapeDtypeStruct(gain.shape, F32),
        ],
    )(grad, projected, cosine, sine, gain)


def table_kernel(capacity, ids_ref, pairs_ref, send_ref, keep_ref, chosen_ref):
    mine_a, mine_b = ids_ref[0], ids_ref[1]
    slots, tokens = send_ref.shape[1:]
    experts = chosen_ref.shape[2]
    numbers = lax.broadcasted_iota(jnp.int32, (slots, tokens), 0).astype(F32)
    nowhere = 1e6

    def table(source, expert, k):
        hit = pairs_ref[0, source, 0] == expert.astype(F32)
        order = pairs_ref[0, source, 1] * 32.0 + pairs_ref[0, source, 2]
        place = jnp.min(jnp.where(hit, order, nowhere), axis=0, keepdims=True)
        across = jnp.broadcast_to(place, (tokens, tokens))
        before = jnp.where(across.T < across, 1.0, 0.0)
        rank = jnp.sum(before, axis=0, keepdims=True)
        inside = (place < nowhere) & (rank < capacity)
        rank = jnp.where(inside, rank + k * capacity, -1.0)
        return jnp.where(numbers == rank, 1.0, 0.0)

    send = keep = chosen = 0.0
    for k in range(4):
        send = send + table(0, mine_a * 4 + (mine_b ^ k), k)
        kept = table(k, mine_a * 4 + mine_b, k)
        keep = keep + kept
        routes = pairs_ref[0, k, 0]
        expert_rows = lax.broadcasted_iota(jnp.int32, (experts, tokens), 0).astype(F32)
        chooser = sum(
            jnp.where(routes[j : j + 1] == expert_rows, 1.0, 0.0) for j in range(TOP)
        )
        chosen = chosen + lax.dot_general(
            kept.astype(BF),
            chooser.astype(BF),
            (((1,), (1,)), ((), ())),
            preferred_element_type=F32,
        )
    send_ref[0] = send.astype(BF)
    keep_ref[0] = keep.astype(BF)
    chosen_ref[0] = chosen


def slot_tables(ids, pairs, capacity, experts):
    planes, _, _, _, tokens = pairs.shape
    slots = 4 * capacity
    block = lambda *shape: pl.BlockSpec((1,) + shape, lambda i: (i,) + (0,) * len(shape))
    return pl.pallas_call(
        lambda *refs: table_kernel(capacity, *refs),
        grid=(planes,),
        in_specs=[pl.BlockSpec(memory_space=pltpu.SMEM), block(4, 3, TOP, tokens)],
        out_specs=[block(slots, tokens), block(slots, tokens), block(slots, experts)],
        out_shape=[
            jax.ShapeDtypeStruct((planes, slots, tokens), BF),
            jax.ShapeDtypeStruct((planes, slots, tokens), BF),
            jax.ShapeDtypeStruct((planes, slots, experts), F32),
        ],
    )(ids, pairs)


def places(slot_rows, lengths_row):
    seq_ends = jnp.cumsum(lengths_row)
    starts = seq_ends - lengths_row
    segment = jnp.sum((slot_rows[:, None] >= seq_ends[None, :]).astype(jnp.int32), axis=1)
    chosen = segment[:, None] == jnp.arange(lengths_row.shape[0], dtype=jnp.int32)[None, :]
    start_of = jnp.sum(jnp.where(chosen, starts[None, :], 0), axis=1)
    return (segment, slot_rows - start_of)


def pick(blocks, index):
    return lax.dynamic_index_in_dim(blocks, index, 0, keepdims=False)


class Rounds:
    def __init__(self):
        self.active = {}
        self.asked = {}
        self.values = {}
        self.flags = set()
        self.count = 0

    def start(self, task):
        self.count += 1
        self.active[self.count] = (task, None)
        return self.count

    def wait(self, flag):
        while flag not in self.flags:
            yield None

    def until(self, *wanted):
        while True:
            for number, (task, came) in list(self.active.items()):
                if self.asked.get(number) is not None:
                    continue
                try:
                    self.asked[number] = task.send(came)
                except StopIteration as end:
                    self.values[number] = end.value
                    del self.active[number]
                    self.asked.pop(number, None)
            if all(number in self.values for number in wanted):
                break
            asked = {number: calls for number, calls in self.asked.items() if calls is not None}
            given = {number: [args for _, args in calls] for number, calls in asked.items()}
            given = lax.optimization_barrier(given)
            for number, calls in asked.items():
                came = [call(*args) for (call, _), args in zip(calls, given[number])]
                self.active[number] = (self.active[number][0], came)
            self.asked = {}
        values = [self.values[number] for number in wanted]
        return values[0] if len(values) == 1 else values

    def run(self, task):
        return self.until(self.start(task))


def later(count, task):
    for _ in range(count):
        yield []
    return (yield from task)


def work(function, *args):
    (result,) = yield [(function, args)]
    return result


class Links:
    def __init__(self, n):
        self.n = n
        self.planes = n // KEY_VALUE_HEADS
        index = lax.axis_index("expert")
        self.g = lax.axis_index("dp")
        self.index = index
        self.a = index // KEY_VALUE_HEADS
        self.b = index % KEY_VALUE_HEADS
        self.flips = [None] + [lambda v, k=k: self.flip(v, k) for k in (1, 2, 3)]
        self.shifts = [None] + [lambda v, s=s: self.shift(v, s) for s in range(1, self.planes)]
        self.backs = [None] + [lambda v, s=s: self.shift(v, -s) for s in range(1, self.planes)]

    def flip(self, value, k):
        return lax.ppermute(value, "expert", [(i, i ^ k) for i in range(self.n)])

    def shift(self, value, step):
        step = step * KEY_VALUE_HEADS
        return lax.ppermute(value, "expert", [(i, (i + step) % self.n) for i in range(self.n)])

    def onward(self, value):
        return self.shift(value, 1)

    def twin(self, value):
        return lax.ppermute(value, "dp", [(0, 1), (1, 0)])

    def behind(self, step):
        return (self.a - step) % self.planes

    def natural(self, blocks):
        odd, high = self.b % 2 == 1, self.b >= 2
        pair = [jnp.where(odd, blocks[q ^ 1], blocks[q]) for q in range(4)]
        return [jnp.where(high, pair[q ^ 2], pair[q]) for q in range(4)]

    def natural_line(self, blocks):
        twice = jnp.concatenate([blocks[::-1], blocks[::-1]], axis=0)
        return lax.dynamic_slice_in_dim(twice, self.planes - 1 - self.a, self.planes, 0)

    def plane_gather(self, own):
        half = own.shape[0] // 2
        near_x, near_y = yield [(self.flips[1], (own,)), (self.flips[2], (own,))]
        low, high = yield [(self.flips[2], (near_x[:half],)), (self.flips[1], (near_y[half:],))]
        return jnp.concatenate([own, near_x, near_y, low, high], axis=0)

    def plane_exchange(self, blocks):
        came = yield [(self.flips[k], (blocks[k],)) for k in (3, 1, 2)]
        return [blocks[0], came[1], came[2], came[0]]

    def plane_scatter(self, total):
        count = total.shape[0] // 4
        half = count // 2
        cut = lambda k, low, high: total[k * count + low : k * count + high]
        low, high = yield [
            (self.flips[2], (cut(3, 0, half).astype(BF),)),
            (self.flips[1], (cut(3, half, count).astype(BF),)),
        ]
        to_x = jnp.concatenate([cut(1, 0, half) + low.astype(F32), cut(1, half, count)], axis=0)
        to_y = jnp.concatenate([cut(2, 0, half), cut(2, half, count) + high.astype(F32)], axis=0)
        got_x, got_y = yield [
            (self.flips[1], (to_x.astype(BF),)),
            (self.flips[2], (to_y.astype(BF),)),
        ]
        return cut(0, 0, count) + got_x.astype(F32) + got_y.astype(F32)

    def line_scatter(self, blocks):
        total = blocks[1]
        for step in range(1, self.planes):
            (came,) = yield [(self.onward, (total.astype(BF),))]
            total = blocks[(1 + step) % self.planes] + came.astype(F32)
        return total

    def line_scatter_direct(self, blocks):
        steps = range(1, self.planes)
        came = yield [(self.backs[s], (blocks[s].astype(BF),)) for s in steps]
        return sum((block.astype(F32) for block in came), blocks[0])

    def small_scatter(self, blocks):
        blocks = blocks.reshape(2, self.planes, 4, -1)
        (came,) = yield [(self.twin, (pick(blocks, 1 - self.g),))]
        blocks = pick(blocks, self.g) + came
        came = yield [
            (self.shifts[step], (pick(blocks, (self.a + step) % self.planes),))
            for step in range(1, self.planes)
        ]
        total = sum(came, pick(blocks, self.a))
        came = yield [(self.flips[k], (pick(total, self.b ^ k),)) for k in (3, 1, 2)]
        return sum(came, pick(total, self.b))

    def twin_scatter(self, own, other):
        (came,) = yield [(self.twin, (other.astype(BF),))]
        return own + came.astype(F32)


def body(
    hidden,
    lengths,
    slots,
    routes,
    order,
    gain_in,
    w_query,
    key_projection_weight,
    value_projection_weight,
    gain_q,
    gain_k,
    w_out,
    gain_mid,
    w_router,
    w_gate,
    w_up,
    w_down,
    cotangent,
):
    tokens = hidden.shape[0]
    experts = w_router.shape[1]
    links = Links(experts)
    planes = links.planes
    capacity = max(2, (tokens * TOP * 9 + 8 * experts - 1) // (8 * experts))
    score_scale = HEAD_SIZE ** (-0.5)
    block_tokens = 4 * tokens
    rows = gain_in.shape[0]
    head_part = gain_q.shape[0]
    devices = 2 * experts

    rounds = Rounds()
    spread = rounds.start
    slot_count = 4 * capacity

    gate_full = lax.all_gather(w_gate, "dp", axis=1, tiled=True)[0]
    up_full = lax.all_gather(w_up, "dp", axis=1, tiled=True)[0]
    down_full = lax.all_gather(w_down, "dp", axis=2, tiled=True)[0]

    lanes = 128
    gains = jnp.concatenate([gain_in, gain_mid, gain_q, gain_k], axis=0)
    gain_count = gains.shape[0]
    gains = jnp.pad(gains, (0, -gain_count % lanes)).reshape(-1, lanes)
    router_rows = rows * experts // lanes
    small = jnp.concatenate([w_router.reshape(-1, lanes), gains], axis=0)
    small = jnp.pad(small, ((0, -small.shape[0] % 8), (0, 0)))
    small_rows = small.shape[0]
    pairs = jnp.concatenate([part.T.astype(BF) for part in (routes, order // 32, order % 32)])
    expert_numbers = jnp.arange(experts, dtype=jnp.int32)
    ids = jnp.stack([links.a, links.b, links.g]).astype(jnp.int32)
    tables = {}

    def gather_small():
        (other,) = yield [(links.twin, (small,))]
        piece = jnp.concatenate([small, other, pairs], axis=0)
        blocks = yield from links.plane_exchange([piece] * 4)
        line = jnp.concatenate(blocks, axis=0)
        came = yield [(links.shifts[s], (line,)) for s in range(1, planes)]
        line = jnp.stack([line] + came).reshape(planes, 4, piece.shape[0], lanes)
        all_pairs = line[:, :, 2 * small_rows :].astype(F32)
        all_pairs = all_pairs.reshape(planes, 4, 3, TOP, tokens)
        tables["send"], tables["keep"], tables["keep_chooser"] = slot_tables(
            ids, all_pairs, capacity, experts
        )
        line = links.natural_line(line[:, :, : 2 * small_rows])
        line = jnp.stack(links.natural([line[:, k] for k in range(4)]), axis=1)
        line = line.reshape(experts, 2, small_rows, lanes)
        first, second = line[:, 0], line[:, 1]
        swap = links.g == 1
        return jnp.concatenate(
            [jnp.where(swap, second, first), jnp.where(swap, first, second)], axis=0
        )

    small_task = spread(gather_small())

    qkv_width = QW + 2 * HEAD_SIZE

    def own_columns(b):
        cut = lambda array, width: lax.dynamic_slice_in_dim(array, b * width, width, 1)
        return jnp.concatenate(
            [
                cut(w_query, QW),
                cut(key_projection_weight, HEAD_SIZE),
                cut(value_projection_weight, HEAD_SIZE),
            ],
            axis=1,
        )

    def gather_qkv():
        blocks = yield from links.plane_exchange([own_columns(links.b ^ k) for k in range(4)])
        pieces, others = [jnp.concatenate(blocks, axis=0)], []
        for _ in range(1, planes):
            came = yield [(links.onward, (pieces[-1],)), (links.twin, (pieces[-1],))]
            pieces.append(came[0])
            others.append(came[1])
        others += yield [(links.twin, (pieces[-1],))]
        return pieces + others

    qkv_task = spread(gather_qkv())
    hidden_task = spread(later(1, links.plane_gather(hidden)))

    def choose(piece, step):
        rows_out = jnp.dot(tables["send"][step], piece, preferred_element_type=F32).astype(BF)
        return by_place(rows_out)

    def by_place(slot_rows):
        return [slot_rows[k * capacity : (k + 1) * capacity] for k in range(4)]

    def gather_upstream():
        pieces, out = [cotangent], []
        plan = [(0, True, None), (3, True, 0), (0, False, 1), (0, False, 2)]
        plan += [(2, True, None), (0, False, 3)]
        if planes != 4:
            plan = [(4, True, None)] + [(0, s < planes - 2, s) for s in range(planes)]
        for idle, hop, step in plan:
            for _ in range(idle):
                yield []
            asks = [(links.onward, (pieces[-1],))] if hop else []
            if step is not None:
                blocks = choose(pieces[step], step)
                asks += [(links.flips[k], (blocks[k],)) for k in (1, 2, 3)]
            came = yield asks
            if hop:
                pieces.append(came[0])
            if step is not None:
                out.append(jnp.concatenate([blocks[0]] + came[-3:], axis=0))
        return out

    upstream_task = spread(gather_upstream())

    head_rows = w_out.shape[0]
    to_block = [
        ((b * 2 + g) * planes + a, g * experts + a * 4 + b)
        for g in range(2)
        for a in range(planes)
        for b in range(4)
    ]
    from_block = [(there, here) for here, there in to_block]
    to_blocks = lambda value: lax.ppermute(value, ("dp", "expert"), to_block)
    from_blocks = lambda value: lax.ppermute(value, ("dp", "expert"), from_block)

    def gather_out():
        yield from rounds.wait("project")
        pieces, others = [], []
        pieces += yield [(to_blocks, (w_out,))]
        yield from rounds.wait("attend")
        for step in range(1, planes):
            if step == planes - 1:
                yield []
            came = yield [(links.onward, (pieces[-1],)), (links.twin, (pieces[-1],))]
            pieces.append(came[0])
            others.append(came[1])
        others += yield [(links.twin, (pieces[-1],))]
        return jnp.concatenate(pieces + others, axis=0)

    out_task = spread(gather_out())

    device_of = jnp.stack(
        [links.behind(s) * 4 + (links.b ^ k) for s in range(planes) for k in range(4)]
    )
    all_slots = slots.reshape(experts, tokens)[device_of].reshape(experts * tokens)
    block_slots = all_slots[:block_tokens]
    seg_key, key_position = places(all_slots, lengths[0])
    seg_query, position = seg_key[:block_tokens], key_position[:block_tokens]
    cosine, sine = rotary_tables(position)
    visible = (seg_query[:, None] == seg_key[None, :]) & (
        all_slots[None, :] <= block_slots[:, None]
    )

    small_all, block_hidden = rounds.until(small_task, hidden_task)
    full_router = small_all[:, :router_rows].reshape(MODEL_WIDTH, experts)
    gains = small_all[:, router_rows:].reshape(devices, -1)
    full_in = gains[:, :rows].reshape(MODEL_WIDTH).astype(F32)
    full_mid = gains[:, rows : 2 * rows].reshape(MODEL_WIDTH).astype(F32)
    head_gains = gains[:, 2 * rows : gain_count].reshape(devices, 2, head_part).swapaxes(0, 1)
    head_gains = head_gains.reshape(2, HEAD_SIZE).astype(F32)

    block_float = block_hidden.astype(F32)
    normalized = rms_scale(block_float, full_in).astype(BF)
    qkv_pieces = rounds.until(qkv_task)

    rounds.flags.add("project")
    w_qkv, projected, turned = rounds.run(
        work(project, ids, normalized, cosine, sine, head_gains, *qkv_pieces)
    )

    def gather_keys(own):
        came = yield [(links.shifts[s], (own,)) for s in range(1, planes)]
        return jnp.concatenate([own] + came, axis=0)

    keys_values = rounds.run(gather_keys(turned[:, QW:]))
    keys, values = keys_values[:, :HEAD_SIZE], keys_values[:, HEAD_SIZE:]

    def forward_head(query_rows, keys, values):
        scores = (
            jnp.einsum("qd,kd->qk", query_rows, keys, preferred_element_type=F32) * score_scale
        )
        scores = jnp.where(visible, scores, MASKED)
        top_score = jnp.max(scores, axis=-1, keepdims=True)
        exponent = jnp.exp(scores - top_score)
        row_total = jnp.sum(exponent, axis=-1, keepdims=True)
        weights = (exponent / row_total).astype(BF)
        mixed_rows = jnp.einsum("qk,kd->qd", weights, values, preferred_element_type=F32)
        return (mixed_rows.astype(BF), top_score + jnp.log(row_total))

    part_heads = 2
    parts = PER_KV // part_heads
    part_width = part_heads * HEAD_SIZE

    def head_of(array, head):
        return array[:, head * HEAD_SIZE : (head + 1) * HEAD_SIZE]

    def part_of(array, part):
        return array[:, part * part_width : (part + 1) * part_width]

    def forward_part(query_rows, keys, values):
        came = [forward_head(head_of(query_rows, h), keys, values) for h in range(part_heads)]
        return (jnp.concatenate([c[0] for c in came], axis=1), [c[1] for c in came])

    rounds.flags.add("attend")
    attended, log_sums = [], []
    for part in range(parts):
        got = rounds.run(work(forward_part, part_of(turned, part), keys, values))
        attended.append(got[0])
        log_sums.append(got[1])
    attended = jnp.concatenate(attended, axis=1)
    order_of = [(t, s) for t in range(2) for s in range(planes)]
    attended = jnp.concatenate(
        [
            lax.dynamic_slice_in_dim(
                attended, ((links.g ^ t) * planes + links.behind(s)) * head_rows, head_rows, 1
            )
            for t, s in order_of
        ],
        axis=1,
    )
    block_out = rounds.until(out_task)

    branch = jnp.dot(attended, block_out, preferred_element_type=F32)
    branch = rounds.run(links.plane_scatter(branch))
    x_float = hidden.astype(F32)
    x_one = x_float + branch
    norm_two, norm_two_back = jax.vjp(rms_scale, x_one, full_mid)
    xn_two = norm_two.astype(BF)

    own_chooser = jnp.any(routes[:, :, None] == expert_numbers, axis=1)

    def masked_softmax(logits, chooser):
        top = jnp.max(jnp.where(chooser, logits, MASKED), axis=-1, keepdims=True)
        exponent = jnp.where(chooser, jnp.exp(jnp.where(chooser, logits - top, 0.0)), 0.0)
        total = jnp.sum(exponent, axis=-1, keepdims=True)
        return exponent / jnp.where(total > 0.0, total, 1.0)

    upstream_slots = rounds.until(upstream_task)

    def expert_step(arrived, slot_upstream, keep_chooser):
        logits = jnp.dot(arrived, full_router, preferred_element_type=F32)
        probs = masked_softmax(logits, keep_chooser > 0.0)
        slot_probs = jnp.sum(
            jnp.where(expert_numbers == links.index, probs, 0.0), axis=1, keepdims=True
        )
        gate_pre = jnp.dot(arrived, gate_full, preferred_element_type=F32)
        up_pre = jnp.dot(arrived, up_full, preferred_element_type=F32)
        logistic = jax.nn.sigmoid(gate_pre)
        activation = (gate_pre * logistic * up_pre).astype(BF)
        returned = jnp.dot(activation, down_full, preferred_element_type=F32).astype(BF)
        upstream_float = slot_upstream.astype(F32)
        out_grad = (slot_probs * upstream_float).astype(BF)
        act_grad = jnp.einsum("rd,fd->rf", out_grad, down_full, preferred_element_type=F32)
        gate_low = (act_grad * up_pre * logistic * (1.0 + gate_pre * (1.0 - logistic))).astype(BF)
        up_low = (act_grad * gate_pre * logistic).astype(BF)
        pair_grad = (
            jnp.einsum("rf,df->rd", gate_low, gate_full, preferred_element_type=F32)
            + jnp.einsum("rf,df->rd", up_low, up_full, preferred_element_type=F32)
        ).astype(BF)
        returned_float = returned.astype(F32)
        gate_grad = jnp.sum(upstream_float * returned_float, axis=1)
        mixed = (slot_probs * returned_float).astype(BF)
        return (pair_grad, gate_grad, mixed, arrived, activation, out_grad, gate_low, up_low)

    def sum_slots(blocks, step):
        return jnp.einsum(
            "ct,cd->td",
            tables["send"][step],
            jnp.concatenate(blocks, axis=0),
            preferred_element_type=F32,
        )

    made = []

    def return_gates():
        slot_grads = jnp.stack([piece[1] for piece in made]).reshape(planes, 4, capacity, 1)
        keep = tables["keep"].reshape(planes, 4, capacity, tokens) > 0.0
        grads = jnp.sum(jnp.where(keep, slot_grads, 0.0), axis=2)
        came = yield [(links.backs[s], (grads[s],)) for s in range(1, planes)]
        line = jnp.stack([grads[0]] + came)
        blocks = yield from links.plane_exchange([line[:, k] for k in range(4)])
        line = jnp.stack(links.natural(blocks), axis=1)
        twice = jnp.concatenate([line, line], axis=0)
        line = lax.dynamic_slice_in_dim(twice, (planes - links.a) % planes, planes, 0)
        return line.reshape(experts, tokens)

    def return_mixture():
        sums, total = {}, None
        for step in range(planes):
            place = (step + 1) % planes
            blocks = by_place(made[place][2])
            asks = [(links.flips[k], (blocks[k],)) for k in (1, 2, 3)]
            if step > 1:
                asks += [(links.onward, (total.astype(BF),))]
            came = yield asks
            sums[step] = sum_slots([blocks[0]] + came[:3], place)
            if step == 0:
                total = sums[0]
            elif step > 1:
                total = came[3].astype(F32) + sums[step - 1]
        (came,) = yield [(links.onward, (total.astype(BF),))]
        return came.astype(F32) + sums[planes - 1]

    def experts_there_and_back():
        piece, ready, sums, total = xn_two, None, {}, None
        for step in range(planes + 3):
            asks = []
            if step < planes:
                blocks = choose(piece, step)
                asks += [(links.flips[k], (blocks[k],)) for k in (1, 2, 3)]
            if 2 <= step < planes + 2:
                back = by_place(made[step - 2][0])
                asks += [(links.flips[k], (back[k],)) for k in (1, 2, 3)]
            if step < planes - 1:
                asks += [(links.onward, (piece,))]
            if step >= 4:
                asks += [(links.onward, (total.astype(BF),))]
            if 1 <= step <= planes:
                args = (ready, upstream_slots[step - 1], tables["keep_chooser"][step - 1])
                asks += [(expert_step, args)]
            if step == planes + 1:
                tables["gates"] = spread(return_gates())
                tables["mixture"] = spread(return_mixture())
            came = yield asks
            if step < planes:
                ready = jnp.concatenate([blocks[0]] + came[:3], axis=0)
                came = came[3:]
            if 2 <= step < planes + 2:
                sums[step - 2] = sum_slots([back[0]] + came[:3], step - 2)
                came = came[3:]
            if step < planes - 1:
                piece, came = came[0], came[1:]
            if step >= 4:
                total, came = came[0].astype(F32) + sums[(step - 2) % planes], came[1:]
            elif step == 3:
                total = sums[1]
            if 1 <= step <= planes:
                made.append(came[0])
        return total

    moe_grad = rounds.run(experts_there_and_back())
    stacked = lambda place: jnp.concatenate([piece[place] for piece in made], axis=0)

    def by_rows(rows_in, grads_in):
        return jnp.einsum("rd,rf->df", rows_in, grads_in, preferred_element_type=F32)

    half_width = MODEL_WIDTH // 2

    def half_of(array, which):
        return lax.dynamic_slice_in_dim(array, which * half_width, half_width, 1)

    def gate_up_gradient(place):
        rows_in, grads_in = stacked(3), stacked(place)
        other, own = yield [
            (by_rows, (half_of(rows_in, 1 - links.g), grads_in)),
            (by_rows, (half_of(rows_in, links.g), grads_in)),
        ]
        return (yield from links.twin_scatter(own, other))

    def down_gradient():
        rows_in, grads_in = stacked(4), stacked(5)
        other, own = yield [
            (by_rows, (rows_in, half_of(grads_in, 1 - links.g))),
            (by_rows, (rows_in, half_of(grads_in, links.g))),
        ]
        return (yield from links.twin_scatter(own, other))

    gate_task = spread(gate_up_gradient(6))
    up_task = spread(later(1, gate_up_gradient(7)))
    down_task = spread(later(2, down_gradient()))
    own_logits = jnp.dot(xn_two, full_router, preferred_element_type=F32)
    own_probs = masked_softmax(own_logits, own_chooser)
    gate_grads = rounds.until(tables["gates"]).T

    upstream = cotangent.astype(F32)
    chosen_grad = own_probs * (
        gate_grads - jnp.sum(own_probs * gate_grads, axis=-1, keepdims=True)
    )
    logit_grad = chosen_grad.astype(BF)
    xn_two_grad = moe_grad + jnp.dot(logit_grad, full_router.T, preferred_element_type=F32)
    x_one_norm_grad, grad_mid = norm_two_back(xn_two_grad)
    x_one_grad = upstream + x_one_norm_grad
    branch_grad = x_one_grad.astype(BF)

    block_grad = rounds.run(links.plane_gather(branch_grad))
    attended_grad = jnp.einsum(
        "td,hd->th", block_grad, block_out, preferred_element_type=F32
    ).astype(BF)
    attended_grad = jnp.concatenate(
        [
            lax.dynamic_slice_in_dim(
                attended_grad,
                ((links.g ^ (h // planes)) * planes + links.behind(h % planes)) * head_rows,
                head_rows,
                1,
            )
            for h in range(2 * planes)
        ],
        axis=1,
    )

    def scatter_out():
        grad = yield from work(
            lambda rows_in, grads_in: jnp.einsum(
                "th,td->hd", rows_in, grads_in, preferred_element_type=F32
            ),
            attended,
            block_grad,
        )
        grad = yield from links.twin_scatter(grad[: QW // 2], grad[QW // 2 :])
        blocks = [grad[s * head_rows : (s + 1) * head_rows] for s in range(planes)]
        grad = yield from links.line_scatter(blocks)
        grad = yield from work(from_blocks, grad.astype(BF))
        return grad.astype(F32)

    grad_out_task = spread(scatter_out())

    def sum_of(parts):
        return links.small_scatter(
            jnp.concatenate([part.reshape(devices, -1) for part in parts], axis=1)
        )

    grad_router = jnp.dot(xn_two.T, logit_grad, preferred_element_type=F32)
    first_task = spread(sum_of([grad_mid, grad_router]))

    def backward_head(query_rows, grad_rows, log_sum, keys, values):
        scores = (
            jnp.einsum("qd,kd->qk", query_rows, keys, preferred_element_type=F32) * score_scale
        )
        scores = jnp.where(visible, scores, MASKED)
        probs = jnp.exp(scores - log_sum)
        weights = probs.astype(BF)
        prob_grad = jnp.einsum("qd,kd->qk", grad_rows, values, preferred_element_type=F32)
        row_inner = jnp.sum(probs * prob_grad, axis=-1, keepdims=True)
        score_grad = (probs * (prob_grad - row_inner)).astype(BF)
        query_grad = (
            jnp.einsum("qk,kd->qd", score_grad, keys, preferred_element_type=F32) * score_scale
        )
        key_grad = (
            jnp.einsum("qk,qd->kd", score_grad, query_rows, preferred_element_type=F32)
            * score_scale
        )
        value_grad = jnp.einsum("qk,qd->kd", weights, grad_rows, preferred_element_type=F32)
        return (query_grad, key_grad, value_grad)

    def backward_part(query_rows, grad_rows, log_sum, keys, values):
        came = [
            backward_head(head_of(query_rows, h), head_of(grad_rows, h), log_sum[h], keys, values)
            for h in range(part_heads)
        ]
        query_grad = jnp.concatenate([c[0] for c in came], axis=1)
        key_terms = jnp.concatenate([sum(c[1] for c in came), sum(c[2] for c in came)], axis=1)
        return (query_grad, key_terms)

    def to_owners(grads_in, scatter):
        other, own = yield [
            (by_rows, (half_of(normalized, 1 - links.g), grads_in)),
            (by_rows, (half_of(normalized, links.g), grads_in)),
        ]
        grad = yield from links.twin_scatter(own, other)
        grad = grad.reshape(planes, 4 * rows, grads_in.shape[1])
        grad = yield from scatter([pick(grad, links.behind(s)) for s in range(planes)])
        grad = grad.astype(BF).reshape(4, rows, grads_in.shape[1])
        blocks = yield from links.plane_exchange([pick(grad, links.b ^ k) for k in range(4)])
        return links.natural(blocks)

    query_low_grads, query_tasks, key_terms, grad_qgain = [], [], None, None
    for part in range(parts):
        got = rounds.run(
            work(
                backward_part,
                part_of(turned, part),
                part_of(attended_grad, part),
                log_sums[part],
                keys,
                values,
            )
        )
        key_terms = got[1] if part == 0 else key_terms + got[1]
        proj_grad, gain_grad = unturn(
            got[0], projected, part * part_heads, cosine, sine, head_gains[0:1]
        )
        grad_qgain = gain_grad if part == 0 else grad_qgain + gain_grad
        query_low_grads.append(proj_grad)
        if part % 2:
            low_grads = jnp.concatenate(query_low_grads[-2:], axis=1)
            task = to_owners(low_grads, links.line_scatter)
            if part == parts - 1:
                task = later(1, task)
            query_tasks.append(spread(task))
    key_terms = rounds.run(
        links.line_scatter_direct(
            [key_terms[s * block_tokens : (s + 1) * block_tokens] for s in range(planes)]
        )
    )

    key_proj_grad, grad_kgain = unturn(
        key_terms[:, :HEAD_SIZE], projected, PER_KV, cosine, sine, head_gains[1:2]
    )
    key_value_grad = jnp.concatenate([key_proj_grad, key_terms[:, HEAD_SIZE:].astype(BF)], axis=1)
    key_value_task = spread(to_owners(key_value_grad, links.line_scatter_direct))
    proj_grad = jnp.concatenate(query_low_grads + [key_value_grad], axis=1)
    xn_one_grad = jnp.einsum("tc,dc->td", proj_grad, w_qkv, preferred_element_type=F32)
    _, block_back = jax.vjp(lambda gain: rms_scale(block_float, gain), full_in)
    (grad_in,) = block_back(xn_one_grad)
    last_task = spread(sum_of([grad_in, grad_qgain, grad_kgain]))
    xn_one_grad = rounds.run(links.plane_scatter(xn_one_grad))
    _, norm_one_back = jax.vjp(lambda values: rms_scale(values, full_in), x_float)
    (x_norm_grad,) = norm_one_back(xn_one_grad)
    input_grad = (x_one_grad + x_norm_grad).astype(BF)

    grad_gate, grad_up, grad_down, mixture, grad_out = rounds.until(
        gate_task, up_task, down_task, tables["mixture"], grad_out_task
    )
    first, last, grad_kv, *grad_query = rounds.until(
        first_task, last_task, key_value_task, *query_tasks
    )
    result = (x_one + mixture).astype(BF)
    whole = lambda blocks: jnp.concatenate(blocks, axis=1).astype(F32)
    grad_query = whole([half[b] for b in range(4) for half in grad_query])
    grad_key = whole([block[:, :HEAD_SIZE] for block in grad_kv])
    grad_value = whole([block[:, HEAD_SIZE:] for block in grad_kv])
    grad_mid = first[:rows]
    grad_router = first[rows:].reshape(rows, experts)
    grad_in = last[:rows]
    grad_qgain = last[rows : rows + head_part]
    grad_kgain = last[rows + head_part :]

    return (
        result,
        input_grad,
        grad_in,
        grad_query,
        grad_key,
        grad_value,
        grad_qgain,
        grad_kgain,
        grad_out,
        grad_mid,
        grad_router,
        grad_gate[None],
        grad_up[None],
        grad_down[None],
    )


def solution(mesh):
    every = ("dp", "expert")
    in_specs = (
        P(every, None),
        P("dp", None),
        P("dp"),
        P(every, None),
        P(every, None),
        P(every),
        P(every, None),
        P(every, None),
        P(every, None),
        P(every),
        P(every),
        P(every, None),
        P(every),
        P(every, None),
        P("expert", "dp", None),
        P("expert", "dp", None),
        P("expert", None, "dp"),
        P(every, None),
    )
    out_specs = (
        P(every, None),
        P(every, None),
        P(every),
        P(every, None),
        P(every, None),
        P(every, None),
        P(every),
        P(every),
        P(every, None),
        P(every),
        P(every, None),
        P("expert", "dp", None),
        P("expert", "dp", None),
        P("expert", None, "dp"),
    )
    return jax.shard_map(body, mesh=mesh, in_specs=in_specs, out_specs=out_specs, check_vma=False)
```

```python
import jax
import jax.numpy as jnp
from jax import lax
from jax.experimental import pallas as pl
from jax.experimental.pallas import tpu as pltpu
from jax.sharding import PartitionSpec as P

MODEL_WIDTH = 2048
QUERY_HEADS = 32
KEY_VALUE_HEADS = 4
HEAD_SIZE = 128
TOP = 8
PER_KV = QUERY_HEADS // KEY_VALUE_HEADS
QW = PER_KV * HEAD_SIZE

EPS = 1e-06
THETA = 1000000.0
MASKED = -1e30
BF = jnp.bfloat16
F32 = jnp.float32


def rms_scale(values, scaling):
    return values * lax.rsqrt(jnp.mean(values * values, axis=-1, keepdims=True) + EPS) * scaling


def rotary_tables(position):
    half = HEAD_SIZE // 2
    index_float = jnp.arange(half, dtype=jnp.float32)
    freq = jnp.power(jnp.float32(THETA), -2.0 * index_float / HEAD_SIZE)
    angle = position.astype(jnp.float32)[:, None] * freq[None, :]
    cosine, sine = jnp.cos(angle), jnp.sin(angle)
    return (
        jnp.concatenate([cosine, cosine], axis=-1),
        jnp.concatenate([-sine, sine], axis=-1),
    )


def project_kernel(starts_ref, x_ref, cos_ref, sin_ref, gains_ref, *refs):
    pieces, (w_ref, proj_ref, turned_ref) = refs[:-3], refs[-3:]
    last = pl.program_id(0) == pl.num_programs(0) - 1
    rows = pieces[0].shape[0] // 4
    for number, piece in enumerate(pieces):
        for k in range(4):
            at = pl.multiple_of(starts_ref[number * 4 + k], rows)
            w_ref[pl.ds(at, rows), :] = piece[k * rows : (k + 1) * rows, :]
    projected = jnp.dot(x_ref[...], w_ref[...], preferred_element_type=F32)
    proj_ref[...] = projected

    def turn(values, gain):
        scaled = (
            values * lax.rsqrt(jnp.mean(values * values, axis=-1, keepdims=True) + EPS) * gain
        )
        swapped = pltpu.roll(scaled, HEAD_SIZE // 2, 1)
        return scaled * cos_ref[...] + swapped * sin_ref[...]

    gain_q, gain_k = gains_ref[0:1], gains_ref[1:2]
    first, second = projected[:, :HEAD_SIZE], projected[:, HEAD_SIZE:]
    turned_ref[:, :HEAD_SIZE] = turn(first, jnp.where(last, gain_k, gain_q)).astype(BF)
    turned_ref[:, HEAD_SIZE:] = jnp.where(last, second, turn(second, gain_q)).astype(BF)


def project(starts, rows_in, cosine, sine, gains, *pieces):
    count, width = rows_in.shape
    height, columns = pieces[0].shape
    step = 2 * HEAD_SIZE
    whole = lambda array: pl.BlockSpec(array.shape, lambda i: (0, 0))
    strip = lambda height: pl.BlockSpec((height, step), lambda i: (0, i))
    return pl.pallas_call(
        project_kernel,
        grid=(columns // step,),
        in_specs=[pl.BlockSpec(memory_space=pltpu.SMEM)]
        + [whole(rows_in), whole(cosine), whole(sine), whole(gains)]
        + [strip(height)] * len(pieces),
        out_specs=[strip(width), strip(count), strip(count)],
        out_shape=[
            jax.ShapeDtypeStruct((width, columns), BF),
            jax.ShapeDtypeStruct((count, columns), F32),
            jax.ShapeDtypeStruct((count, columns), BF),
        ],
        cost_estimate=pl.CostEstimate(
            flops=2 * count * width * columns,
            bytes_accessed=2 * (count + columns) * width,
            transcendentals=0,
        ),
        compiler_params=pltpu.CompilerParams(vmem_limit_bytes=60 * 2**20),
    )(starts, rows_in, cosine, sine, gains, *pieces)


def unturned(grad, values, cosine, sine, gain):
    grad = grad * cosine + pltpu.roll(grad * sine, HEAD_SIZE // 2, 1)
    scale = lax.rsqrt(jnp.mean(values * values, axis=-1, keepdims=True) + EPS)
    gain_grad = jnp.sum(grad * values * scale, axis=0, keepdims=True)
    grad = grad * gain
    inner = jnp.mean(grad * values, axis=-1, keepdims=True)
    return (scale * grad - values * (scale * scale * scale * inner)).astype(BF), gain_grad


def unturn_kernel(grad_ref, proj_ref, cos_ref, sin_ref, gain_ref, out_ref, gain_grad_ref):
    out_ref[...], gain_grad_ref[...] = unturned(
        grad_ref[...], proj_ref[...], cos_ref[...], sin_ref[...], gain_ref[...]
    )


def unturn(grad, projected, cosine, sine, gain):
    return pl.pallas_call(
        unturn_kernel,
        out_shape=[
            jax.ShapeDtypeStruct(grad.shape, BF),
            jax.ShapeDtypeStruct(gain.shape, F32),
        ],
    )(grad, projected, cosine, sine, gain)


def input_kernel(grad_ref, w_ref, hidden_ref, scale_ref, out_ref, gain_grad_ref):
    dims = (((1,), (1,)), ((), ()))
    out = lax.dot_general(grad_ref[...], w_ref[...], dims, preferred_element_type=F32)
    out_ref[...] = out
    gain_grad_ref[...] = jnp.sum(
        out * hidden_ref[...].astype(F32) * scale_ref[...], axis=0, keepdims=True
    )


def input_gradient(proj_grad, weights, hidden, scale):
    count, columns = proj_grad.shape
    width = weights.shape[0]
    step = 256
    whole = lambda array: pl.BlockSpec(array.shape, lambda i: (0, 0))
    strip = lambda height: pl.BlockSpec((height, step), lambda i: (0, i))
    return pl.pallas_call(
        input_kernel,
        grid=(width // step,),
        in_specs=[
            whole(proj_grad),
            pl.BlockSpec((step, columns), lambda i: (i, 0)),
            strip(count),
            whole(scale),
        ],
        out_specs=[strip(count), strip(1)],
        out_shape=[
            jax.ShapeDtypeStruct((count, width), F32),
            jax.ShapeDtypeStruct((1, width), F32),
        ],
        cost_estimate=pl.CostEstimate(
            flops=2 * count * width * columns,
            bytes_accessed=6 * (count + columns) * width,
            transcendentals=0,
        ),
        compiler_params=pltpu.CompilerParams(vmem_limit_bytes=24 * 2**20),
    )(proj_grad, weights, hidden, scale)


def forward_kernel(q_ref, kv_ref, vt_ref, place_ref, low_ref, high_ref, out_ref, p_ref):
    count, queries = p_ref.shape
    step = min(512, count)
    chunks = [slice(at, at + step) for at in range(0, count, step)]
    q, low, high = q_ref[...], low_ref[...], high_ref[...]
    top = jnp.full((1, queries), MASKED, F32)
    for chunk in chunks:
        place = place_ref[chunk, :]
        seen = (place >= low) & (place <= high)
        scores = lax.dot_general(
            kv_ref[chunk, :HEAD_SIZE], q, (((1,), (1,)), ((), ())), preferred_element_type=F32
        )
        scores = jnp.where(seen, scores * HEAD_SIZE**-0.5, MASKED)
        p_ref[chunk, :] = scores
        top = jnp.maximum(top, jnp.max(scores, axis=0, keepdims=True))
    total = jnp.zeros((1, queries), F32)
    for chunk in chunks:
        exponent = jnp.exp(p_ref[chunk, :] - top)
        p_ref[chunk, :] = exponent
        total = total + jnp.sum(exponent, axis=0, keepdims=True)
    share = 1.0 / total
    out = jnp.zeros((HEAD_SIZE, queries), F32)
    for chunk in chunks:
        probs = (p_ref[chunk, :] * share).astype(BF)
        out = out + jnp.dot(vt_ref[:, chunk], probs, preferred_element_type=F32)
    out_ref[...] = out.T.astype(BF)


def attention_blocks(rows, count):
    step = min(rows, 512 * 2048 // count)
    whole = lambda array: pl.BlockSpec(array.shape, lambda i, j: (0, 0))
    head = pl.BlockSpec((step, HEAD_SIZE), lambda i, j: (j, i))
    along = pl.BlockSpec((1, step), lambda i, j: (0, j))
    down = pl.BlockSpec((step, HEAD_SIZE), lambda i, j: (j, 0))
    limit = (32 if count <= 2048 else 60) * 2**20
    return step, whole, head, along, down, limit


def attention_forward(q, keys_values, values_turned, place, low, high):
    rows, columns = q.shape
    count = keys_values.shape[0]
    step, whole, head, along, _, limit = attention_blocks(rows, count)
    return pl.pallas_call(
        forward_kernel,
        grid=(columns // HEAD_SIZE, rows // step),
        in_specs=[head, whole(keys_values), whole(values_turned), whole(place), along, along],
        out_specs=head,
        out_shape=jax.ShapeDtypeStruct(q.shape, BF),
        scratch_shapes=[pltpu.VMEM((count, step), F32)],
        cost_estimate=pl.CostEstimate(
            flops=8 * rows * columns * count, bytes_accessed=4 * rows * columns, transcendentals=0
        ),
        compiler_params=pltpu.CompilerParams(vmem_limit_bytes=limit),
    )(q, keys_values, values_turned, place, low, high)


def backward_kernel(
    q_ref, grad_ref, proj_ref, kv_ref, kt_ref, place_ref, low_ref, high_ref, cos_ref, sin_ref,
    gain_ref, out_ref, dkv_ref, gain_grad_ref, p_ref, dp_ref,
):
    @pl.when((pl.program_id(0) == 0) & (pl.program_id(1) == 0))
    def _():
        dkv_ref[...] = jnp.zeros_like(dkv_ref)
        gain_grad_ref[...] = jnp.zeros_like(gain_grad_ref)

    count, queries = p_ref.shape
    step = min(512, count)
    chunks = [slice(at, at + step) for at in range(0, count, step)]
    scale = HEAD_SIZE**-0.5
    q, grad = q_ref[...], grad_ref[...]
    low, high = low_ref[...], high_ref[...]

    def across(left, right):
        dims = (((1,), (1,)), ((), ()))
        return lax.dot_general(left, right, dims, preferred_element_type=F32)

    top = jnp.full((1, queries), MASKED, F32)
    for chunk in chunks:
        place = place_ref[chunk, :]
        seen = (place >= low) & (place <= high)
        scores = jnp.where(seen, across(kv_ref[chunk, :HEAD_SIZE], q) * scale, MASKED)
        p_ref[chunk, :] = scores
        top = jnp.maximum(top, jnp.max(scores, axis=0, keepdims=True))
    total = inner = jnp.zeros((1, queries), F32)
    for chunk in chunks:
        exponent = jnp.exp(p_ref[chunk, :] - top)
        p_ref[chunk, :] = exponent
        total = total + jnp.sum(exponent, axis=0, keepdims=True)
        prob_grad = across(kv_ref[chunk, HEAD_SIZE:], grad)
        dp_ref[chunk, :] = prob_grad
        inner = inner + jnp.sum(exponent * prob_grad, axis=0, keepdims=True)
    share = 1.0 / total
    inner = inner * share
    dq = jnp.zeros((HEAD_SIZE, queries), F32)
    for chunk in chunks:
        probs = p_ref[chunk, :] * share
        score_grad = (probs * (dp_ref[chunk, :] - inner)).astype(BF)
        dkv_ref[chunk, HEAD_SIZE:] += jnp.dot(probs.astype(BF), grad, preferred_element_type=F32)
        dkv_ref[chunk, :HEAD_SIZE] += (
            jnp.dot(score_grad, q, preferred_element_type=F32) * scale
        )
        dq = dq + jnp.dot(kt_ref[:, chunk], score_grad, preferred_element_type=F32)
    out_ref[...], gain_grad = unturned(
        dq.T * scale, proj_ref[...], cos_ref[...], sin_ref[...], gain_ref[...]
    )
    gain_grad_ref[...] += gain_grad


def attention_backward(
    q, grad, projected, keys_values, keys_turned, place, low, high, cosine, sine, gain
):
    rows, columns = q.shape
    count = keys_values.shape[0]
    step, whole, head, along, down, limit = attention_blocks(rows, count)
    return pl.pallas_call(
        backward_kernel,
        grid=(columns // HEAD_SIZE, rows // step),
        in_specs=[head, head, head, whole(keys_values), whole(keys_turned), whole(place)]
        + [along, along, down, down, whole(gain)],
        out_specs=[head, whole(keys_values), whole(gain)],
        out_shape=[
            jax.ShapeDtypeStruct(q.shape, BF),
            jax.ShapeDtypeStruct(keys_values.shape, F32),
            jax.ShapeDtypeStruct(gain.shape, F32),
        ],
        scratch_shapes=[pltpu.VMEM((count, step), F32)] * 2,
        cost_estimate=pl.CostEstimate(
            flops=10 * rows * columns * count, bytes_accessed=8 * rows * columns, transcendentals=0
        ),
        compiler_params=pltpu.CompilerParams(vmem_limit_bytes=limit),
    )(q, grad, projected, keys_values, keys_turned, place, low, high, cosine, sine, gain)


def choose_kernel(blocks, table_ref, piece_ref, *refs):
    chosen = jnp.dot(table_ref[...], piece_ref[...], preferred_element_type=F32)
    back_refs, out_refs = refs[:-blocks], refs[-blocks:]
    count = out_refs[0].shape[0]
    width = piece_ref.shape[1]
    for k, out_ref in enumerate(out_refs):
        part = chosen[k * count : (k + 1) * count].astype(BF)
        if back_refs:
            out_ref[:, :width] = part
            out_ref[:, width:] = back_refs[k][...]
        else:
            out_ref[...] = part


def choose_rows(table, piece, blocks, backs=()):
    width = piece.shape[1] + (backs[0].shape[1] if backs else 0)
    shape = (table.shape[0] // blocks, width)
    return pl.pallas_call(
        lambda *refs: choose_kernel(blocks, *refs),
        out_shape=[jax.ShapeDtypeStruct(shape, BF)] * blocks,
        compiler_params=pltpu.CompilerParams(vmem_limit_bytes=16 * 2**20),
    )(table, piece, *backs)


def collect_kernel(blocks, table_ref, *refs):
    width = refs[-1].shape[1]
    rows_in = [ref[:, ref.shape[1] - width :].astype(F32) for ref in refs[:blocks]]
    stack = jnp.concatenate(rows_in, axis=0).astype(BF)
    total = jnp.dot(table_ref[...], stack, preferred_element_type=F32)
    if len(refs) > blocks + 1:
        total = total + refs[blocks][...].astype(F32)
    refs[-1][...] = total.astype(refs[-1].dtype)


def collect_rows(table, blocks, width, more=None, kind=BF):
    extra = [] if more is None else [more]
    return pl.pallas_call(
        lambda *refs: collect_kernel(len(blocks), *refs),
        out_shape=jax.ShapeDtypeStruct((table.shape[0], width), kind),
        compiler_params=pltpu.CompilerParams(vmem_limit_bytes=24 * 2**20),
    )(table, *blocks, *extra)


def expert_kernel(blocks, me_ref, *refs):
    rows_refs, upstream_refs = refs[:blocks], refs[blocks : 2 * blocks]
    refs = refs[2 * blocks :]
    chooser_ref, router_ref, gate_ref, up_ref, down_ref = refs[:5]
    back_refs, mixed_refs = refs[5 : 5 + blocks], refs[5 + blocks : 5 + 2 * blocks]
    refs = refs[5 + 2 * blocks :]
    rows_ref, act_ref, out_grad_ref, gate_low_ref, up_low_ref = refs[:5]
    upstream_ref, share_ref, returned_ref, pair_ref = refs[5:]
    step = pl.program_id(0)
    across = (((1,), (1,)), ((), ()))

    @pl.when(step == 0)
    def _():
        whole = lambda parts: jnp.concatenate([ref[...].astype(F32) for ref in parts], axis=0)
        rows_in = whole(rows_refs).astype(BF)
        upstream = whole(upstream_refs)
        logits = jnp.dot(rows_in, router_ref[...], preferred_element_type=F32)
        chosen = chooser_ref[...] > 0.0
        top = jnp.max(jnp.where(chosen, logits, MASKED), axis=1, keepdims=True)
        exponent = jnp.where(chosen, jnp.exp(jnp.where(chosen, logits - top, 0.0)), 0.0)
        total = jnp.sum(exponent, axis=1, keepdims=True)
        number = lax.broadcasted_iota(jnp.int32, exponent.shape, 1)
        mine = jnp.sum(jnp.where(number == me_ref[0], exponent, 0.0), axis=1, keepdims=True)
        share = mine / jnp.where(total > 0.0, total, 1.0)
        rows_ref[...] = rows_in
        upstream_ref[...] = upstream
        out_grad_ref[...] = (share * upstream).astype(BF)
        share_ref[...] = jnp.broadcast_to(share, share_ref.shape)
        returned_ref[...] = jnp.zeros_like(returned_ref)
        pair_ref[...] = jnp.zeros_like(pair_ref)

    rows_in, out_grad = rows_ref[...], out_grad_ref[...]
    gate, up, down = gate_ref[...], up_ref[...], down_ref[...]
    gate_pre = jnp.dot(rows_in, gate, preferred_element_type=F32)
    up_pre = jnp.dot(rows_in, up, preferred_element_type=F32)
    act_grad = lax.dot_general(out_grad, down, across, preferred_element_type=F32)
    logistic = jax.nn.sigmoid(gate_pre)
    silu = gate_pre * logistic
    act = (silu * up_pre).astype(BF)
    gate_low = (act_grad * up_pre * logistic * (1.0 + gate_pre * (1.0 - logistic))).astype(BF)
    up_low = (act_grad * silu).astype(BF)
    act_ref[...], gate_low_ref[...], up_low_ref[...] = act, gate_low, up_low
    returned_ref[...] += jnp.dot(act, down, preferred_element_type=F32)
    pair_ref[...] += lax.dot_general(
        gate_low, gate, across, preferred_element_type=F32
    ) + lax.dot_general(up_low, up, across, preferred_element_type=F32)

    @pl.when(step == pl.num_programs(0) - 1)
    def _():
        returned = returned_ref[...].astype(BF).astype(F32)
        gate_grad = jnp.sum(upstream_ref[...] * returned, axis=1, keepdims=True)
        mixed = share_ref[:, :1] * returned
        pair = pair_ref[...]
        count = rows_refs[0].shape[0]
        width = pair.shape[1]
        number = lax.broadcasted_iota(jnp.int32, share_ref.shape, 1)
        gates = jnp.where(number == me_ref[0], gate_grad, 0.0)
        for k in range(blocks):
            part = slice(k * count, (k + 1) * count)
            back_refs[k][:, :width] = pair[part].astype(BF)
            back_refs[k][:, width:] = gates[part].astype(BF)
            mixed_refs[k][...] = mixed[part].astype(BF)


def expert_rows(me, rows_in, upstream, chooser, router, gate, up, down):
    blocks = len(rows_in)
    block = upstream[0].shape
    slots, width = blocks * block[0], block[1]
    ff = gate.shape[1]
    step = 256
    lanes = 128
    whole = lambda shape: pl.BlockSpec(shape, lambda i: (0, 0))
    columns = lambda height: pl.BlockSpec((height, step), lambda i: (0, i))
    shape = jax.ShapeDtypeStruct
    out = [((block[0], width + lanes), BF)] * blocks + [(block, BF)] * blocks
    out_specs = [whole(dims) for dims, _ in out]
    out_specs += [whole((slots, width)), columns(slots), whole((slots, width))]
    out_specs += [columns(slots)] * 2
    out += [((slots, width), BF), ((slots, ff), BF), ((slots, width), BF)]
    out += [((slots, ff), BF)] * 2
    return pl.pallas_call(
        lambda *refs: expert_kernel(blocks, *refs),
        grid=(ff // step,),
        in_specs=[pl.BlockSpec(memory_space=pltpu.SMEM)]
        + [whole(block)] * (2 * blocks)
        + [whole(chooser.shape), whole(router.shape)]
        + [columns(width), columns(width), pl.BlockSpec((step, width), lambda i: (i, 0))],
        out_specs=out_specs,
        out_shape=[shape(dims, kind) for dims, kind in out],
        scratch_shapes=[
            pltpu.VMEM((slots, width), F32),
            pltpu.VMEM((slots, lanes), F32),
            pltpu.VMEM((slots, width), F32),
            pltpu.VMEM((slots, width), F32),
        ],
        cost_estimate=pl.CostEstimate(
            flops=12 * slots * width * ff, bytes_accessed=6 * width * ff, transcendentals=0
        ),
        compiler_params=pltpu.CompilerParams(vmem_limit_bytes=44 * 2**20),
    )(me, *rows_in, *upstream, chooser, router, gate, up, down)


def table_kernel(capacity, ids_ref, pairs_ref, send_ref, back_ref, chosen_ref):
    mine_a, mine_b = ids_ref[0], ids_ref[1]
    slots, tokens = send_ref.shape[1:]
    experts = chosen_ref.shape[2]
    numbers = lax.broadcasted_iota(jnp.int32, (slots, tokens), 0).astype(F32)
    nowhere = 1e6

    def table(source, expert, k):
        hit = pairs_ref[0, source, 0] == expert.astype(F32)
        order = pairs_ref[0, source, 1] * 32.0 + pairs_ref[0, source, 2]
        place = jnp.min(jnp.where(hit, order, nowhere), axis=0, keepdims=True)
        across = jnp.broadcast_to(place, (tokens, tokens))
        before = jnp.where(across.T < across, 1.0, 0.0)
        rank = jnp.sum(before, axis=0, keepdims=True)
        inside = (place < nowhere) & (rank < capacity)
        rank = jnp.where(inside, rank + k * capacity, -1.0)
        return jnp.where(numbers == rank, 1.0, 0.0)

    send = chosen = 0.0
    for k in range(4):
        send = send + table(0, mine_a * 4 + (mine_b ^ k), k)
        kept = table(k, mine_a * 4 + mine_b, k)
        routes = pairs_ref[0, k, 0]
        expert_rows = lax.broadcasted_iota(jnp.int32, (experts, tokens), 0).astype(F32)
        chooser = sum(
            jnp.where(routes[j : j + 1] == expert_rows, 1.0, 0.0) for j in range(TOP)
        )
        chosen = chosen + lax.dot_general(
            kept.astype(BF),
            chooser.astype(BF),
            (((1,), (1,)), ((), ())),
            preferred_element_type=F32,
        )
    send_ref[0] = send.astype(BF)
    back_ref[0] = send.T.astype(BF)
    chosen_ref[0] = chosen


def slot_tables(ids, pairs, capacity, experts):
    planes, _, _, _, tokens = pairs.shape
    slots = 4 * capacity
    block = lambda *shape: pl.BlockSpec((1,) + shape, lambda i: (i,) + (0,) * len(shape))
    return pl.pallas_call(
        lambda *refs: table_kernel(capacity, *refs),
        grid=(planes,),
        in_specs=[pl.BlockSpec(memory_space=pltpu.SMEM), block(4, 3, TOP, tokens)],
        out_specs=[block(slots, tokens), block(tokens, slots), block(slots, experts)],
        out_shape=[
            jax.ShapeDtypeStruct((planes, slots, tokens), BF),
            jax.ShapeDtypeStruct((planes, tokens, slots), BF),
            jax.ShapeDtypeStruct((planes, slots, experts), F32),
        ],
    )(ids, pairs)


def places(slot_rows, lengths_row):
    seq_ends = jnp.cumsum(lengths_row)
    starts = seq_ends - lengths_row
    segment = jnp.sum((slot_rows[:, None] >= seq_ends[None, :]).astype(jnp.int32), axis=1)
    chosen = segment[:, None] == jnp.arange(lengths_row.shape[0], dtype=jnp.int32)[None, :]
    start_of = jnp.sum(jnp.where(chosen, starts[None, :], 0), axis=1)
    return (segment, slot_rows - start_of)


def pick(blocks, index):
    return lax.dynamic_index_in_dim(blocks, index, 0, keepdims=False)


class Rounds:
    def __init__(self):
        self.active = {}
        self.asked = {}
        self.values = {}
        self.count = 0

    def start(self, task):
        self.count += 1
        self.active[self.count] = (task, None)
        return self.count

    def until(self, *wanted):
        while True:
            while waiting := [number for number in self.active if number not in self.asked]:
                for number in waiting:
                    task, came = self.active[number]
                    try:
                        self.asked[number] = task.send(came)
                    except StopIteration as end:
                        self.values[number] = end.value
                        del self.active[number]
            if all(number in self.values for number in wanted):
                break
            asked = self.asked
            given = {number: [args for _, args in calls] for number, calls in asked.items()}
            given = lax.optimization_barrier(given)
            came = {
                number: [call(*args) for (call, _), args in zip(calls, given[number])]
                for number, calls in asked.items()
            }
            came = lax.optimization_barrier(came)
            for number, results in came.items():
                self.active[number] = (self.active[number][0], results)
            self.asked = {}
        values = [self.values[number] for number in wanted]
        return values[0] if len(values) == 1 else values

    def run(self, task):
        return self.until(self.start(task))


def hold(count, *values):
    for _ in range(count):
        (values,) = yield [(lambda *v: v, values)]
    return values


def later(count, task):
    yield from hold(count)
    return (yield from task)


def work(function, *args):
    (result,) = yield [(function, args)]
    return result


class Links:
    def __init__(self, n):
        self.n = n
        self.planes = n // 4
        index = lax.axis_index("expert")
        self.g = lax.axis_index("dp")
        self.index = index
        self.p = index % 4
        self.l = index // 4
        self.square = n == 16
        if self.square:
            self.a = index % 2 + index // 8 * 2
            self.b = index // 2 % 4
        else:
            self.a, self.b = self.l, self.p
        masks = (0, 2, 4, 6) if self.square else (0, 1, 2, 3)
        self.places = [lambda v, k=k: self.flip(v, k) for k in range(4)]
        self.heads = [lambda v, m=m: self.flip(v, m) for m in masks]
        self.shifts = [lambda v, s=s: self.shift(v, s) for s in range(self.planes)]
        self.backs = [lambda v, s=s: self.shift(v, -s) for s in range(self.planes)]

    def device(self, a, b):
        return a % 2 + b * 2 + a // 2 * 8 if self.square else a * 4 + b

    def block(self, r):
        return self.a ^ r if self.square else (self.a - r) % self.planes

    def flip(self, value, mask):
        return lax.ppermute(value, "expert", [(i, i ^ mask) for i in range(self.n)])

    def shift(self, value, step):
        return lax.ppermute(
            value, "expert", [(i, (i + step * 4) % self.n) for i in range(self.n)]
        )

    def onward(self, value):
        return self.shift(value, 1)

    def twin(self, value):
        return lax.ppermute(value, "dp", [(0, 1), (1, 0)])

    def natural(self, blocks, mine):
        odd, high = mine % 2 == 1, mine >= 2
        pair = [jnp.where(odd, blocks[q ^ 1], blocks[q]) for q in range(4)]
        return [jnp.where(high, pair[q ^ 2], pair[q]) for q in range(4)]

    def turned_line(self, blocks):
        twice = jnp.concatenate([blocks[::-1], blocks[::-1]], axis=0)
        return lax.dynamic_slice_in_dim(twice, self.planes - 1 - self.l, self.planes, 0)

    def head_gather(self, own):
        half = own.shape[0] // 2
        near_x, near_y = yield [(self.heads[1], (own,)), (self.heads[2], (own,))]
        low, high = yield [(self.heads[2], (near_x[:half],)), (self.heads[1], (near_y[half:],))]
        return jnp.concatenate([own, near_x, near_y, low, high], axis=0)

    def exchange(self, flips, blocks):
        came = yield [(flips[k], (blocks[k],)) for k in (3, 1, 2)]
        return [blocks[0], came[1], came[2], came[0]]

    def head_scatter(self, total):
        count = total.shape[0] // 4
        half = count // 2
        cut = lambda k, low, high: total[k * count + low : k * count + high]
        low, high = yield [
            (self.heads[2], (cut(3, 0, half).astype(BF),)),
            (self.heads[1], (cut(3, half, count).astype(BF),)),
        ]
        to_x = jnp.concatenate([cut(1, 0, half) + low.astype(F32), cut(1, half, count)], axis=0)
        to_y = jnp.concatenate([cut(2, 0, half), cut(2, half, count) + high.astype(F32)], axis=0)
        got_x, got_y = yield [
            (self.heads[1], (to_x.astype(BF),)),
            (self.heads[2], (to_y.astype(BF),)),
        ]
        return cut(0, 0, count) + got_x.astype(F32) + got_y.astype(F32)

    def block_gather(self, own, idle=(0, 0)):
        if not self.square:
            came = yield [(shift, (own,)) for shift in self.shifts[1:]]
            return [own] + came
        x, z = (lambda v: self.flip(v, 1)), (lambda v: self.flip(v, 8))
        half = own.shape[0] // 2
        near, low = yield [(x, (own,)), (z, (own[:half],))]
        near, low = yield from hold(idle[0], near, low)
        high, far_low = yield [(z, (own[half:],)), (x, (low,))]
        high, far_low = yield from hold(idle[1], high, far_low)
        (far_high,) = yield [(x, (high,))]
        return [
            own,
            near,
            jnp.concatenate([low, high], axis=0),
            jnp.concatenate([far_low, far_high], axis=0),
        ]

    def block_gather_short(self, own):
        if not self.square:
            came = yield [(shift, (own,)) for shift in self.shifts[1:]]
            return [own] + came
        x, z = (lambda v: self.flip(v, 1)), (lambda v: self.flip(v, 8))
        near, across = yield [(x, (own,)), (z, (own,))]
        (far,) = yield [(x, (across,))]
        return [own, near, across, far]

    def block_scatter(self, blocks, split=False, idle=0):
        if not self.square:
            came = yield [
                (back, (block.astype(BF),)) for back, block in zip(self.backs[1:], blocks[1:])
            ]
            return sum((block.astype(F32) for block in came), blocks[0].astype(F32))
        x, z = (lambda v: self.flip(v, 1)), (lambda v: self.flip(v, 8))
        (came,) = yield [(x, (blocks[3].astype(BF),))]
        (came,) = yield from hold(idle, came)
        across = (blocks[2].astype(F32) + came.astype(F32)).astype(BF)
        half = across.shape[0] // 2 if split else across.shape[0]
        near, got = yield [(x, (blocks[1].astype(BF),)), (z, (across[:half],))]
        if split:
            (more,) = yield [(z, (across[half:],))]
            got = jnp.concatenate([got, more], axis=0)
        return blocks[0].astype(F32) + near.astype(F32) + got.astype(F32)

    def twin_scatter(self, make, own, other, idle=None):
        low = lambda *args: make(*args).astype(BF)
        (block,) = yield [(low, other)]
        (came,) = yield [(self.twin, (block,))]
        if idle is None:
            return make(*own) + came.astype(F32)
        (came,) = yield from hold(idle, came)
        (total,) = yield [(lambda came, *args: make(*args) + came.astype(F32), (came, *own))]
        return total


def body(
    hidden,
    lengths,
    slots,
    routes,
    order,
    gain_in,
    w_query,
    key_projection_weight,
    value_projection_weight,
    gain_q,
    gain_k,
    w_out,
    gain_mid,
    w_router,
    w_gate,
    w_up,
    w_down,
    cotangent,
):
    tokens = hidden.shape[0]
    experts = w_router.shape[1]
    links = Links(experts)
    planes = links.planes
    capacity = max(2, (tokens * TOP * 9 + 8 * experts - 1) // (8 * experts))
    block_tokens = 4 * tokens
    rows = gain_in.shape[0]
    head_part = gain_q.shape[0]
    devices = 2 * experts

    rounds = Rounds()
    spread = rounds.start
    slot_count = 4 * capacity

    gate_full = lax.all_gather(w_gate, "dp", axis=1, tiled=True)[0]
    up_full = lax.all_gather(w_up, "dp", axis=1, tiled=True)[0]
    down_full = lax.all_gather(w_down, "dp", axis=2, tiled=True)[0]

    lanes = 128
    gains = jnp.concatenate([gain_in, gain_mid, gain_q, gain_k], axis=0)
    gain_count = gains.shape[0]
    gains = jnp.pad(gains, (0, -gain_count % lanes)).reshape(-1, lanes)
    router_rows = rows * experts // lanes
    small = jnp.concatenate([w_router.reshape(-1, lanes), gains], axis=0)
    small = jnp.pad(small, ((0, -small.shape[0] % 8), (0, 0)))
    small_rows = small.shape[0]
    pairs = jnp.concatenate([part.T.astype(BF) for part in (routes, order // 32, order % 32)])
    expert_numbers = jnp.arange(experts, dtype=jnp.int32)
    ids = jnp.stack([links.l, links.p]).astype(jnp.int32)
    tables = {}

    def gather_small():
        piece = jnp.concatenate([small, pairs], axis=0)
        blocks = yield from links.exchange(links.places, [piece] * 4)
        line = jnp.stack(blocks)
        if links.square:
            low, high = (lambda v: links.flip(v, 4)), (lambda v: links.flip(v, 8))
            (near,) = yield [(low, (line,))]
            line = jnp.stack([line, near])
            (across,) = yield [(high, (line,))]
            line = jnp.stack([line[0], line[1], across[0], across[1]])
        else:
            came = yield [(shift, (line,)) for shift in links.shifts[1:]]
            line = jnp.stack([line] + came)
            yield from hold(1)
        own_small = line[:, :, :small_rows]
        (other_small,) = yield [(links.twin, (own_small,))]
        return (yield from work(sort_small, line, other_small, rounds.values[hidden_task]))

    def sort_small(line, other_small, block_hidden):
        if links.square:
            line = jnp.stack(links.natural([line[r] for r in range(4)], links.l))
            other_small = jnp.stack(links.natural([other_small[r] for r in range(4)], links.l))
        else:
            line, other_small = links.turned_line(line), links.turned_line(other_small)
        all_pairs = links.turned_line(line[:, :, small_rows:]).astype(F32)
        all_pairs = all_pairs.reshape(planes, 4, 3, TOP, tokens)
        found = slot_tables(ids, all_pairs, capacity, experts)
        tables["send"], tables["back"], tables["chooser"] = found
        line = jnp.stack([line[:, :, :small_rows], other_small], axis=2)
        line = jnp.stack(links.natural([line[:, k] for k in range(4)], links.p), axis=1)
        line = line.reshape(experts, 2, small_rows, lanes)
        first, second = line[:, 0], line[:, 1]
        swap = links.g == 1
        small_all = jnp.concatenate(
            [jnp.where(swap, second, first), jnp.where(swap, first, second)], axis=0
        )
        gains = small_all[:, router_rows:].reshape(devices, -1)
        head_gains = gains[:, 2 * rows : gain_count].reshape(devices, 2, head_part)
        values = block_hidden.astype(F32)
        scale = lax.rsqrt(jnp.mean(values * values, axis=-1, keepdims=True) + EPS)
        full_in = gains[:, :rows].reshape(MODEL_WIDTH).astype(F32)
        return (
            (values * scale * full_in).astype(BF),
            scale,
            small_all[:, :router_rows].reshape(MODEL_WIDTH, experts),
            full_in,
            gains[:, rows : 2 * rows].reshape(MODEL_WIDTH).astype(F32),
            head_gains.swapaxes(0, 1).reshape(2, HEAD_SIZE).astype(F32),
        )

    small_task = spread(gather_small())

    qkv_width = QW + 2 * HEAD_SIZE

    def own_columns(b):
        cut = lambda array, width: lax.dynamic_slice_in_dim(array, b * width, width, 1)
        return jnp.concatenate(
            [
                cut(w_query, QW),
                cut(key_projection_weight, HEAD_SIZE),
                cut(value_projection_weight, HEAD_SIZE),
            ],
            axis=1,
        )

    def gather_qkv():
        blocks = [own_columns(links.b ^ k) for k in range(4)]
        blocks = yield from links.exchange(links.heads, blocks)
        pieces = yield from links.block_gather(jnp.concatenate(blocks, axis=0))
        others = yield [(links.twin, (piece,)) for piece in pieces]
        return pieces + others

    qkv_task = spread(gather_qkv())
    hidden_task = spread(later(1, links.head_gather(hidden)))

    aligned = capacity % 8 == 0

    def choose(piece, step, backs=()):
        found = choose_rows(tables["send"][step], piece, 4 if aligned else 1, as_blocks(backs))
        return found if aligned else by_place(found[0])

    def by_place(slot_rows):
        return [slot_rows[k * capacity : (k + 1) * capacity] for k in range(4)]

    def as_blocks(blocks):
        return blocks if aligned or not blocks else [jnp.concatenate(blocks, axis=0)]

    def collect(blocks, step, width, more=None, kind=BF):
        return collect_rows(tables["back"][step], as_blocks(blocks), width, more, kind)

    def in_places(own, came):
        return [own, came[0], came[1], came[2]]

    def to_places(blocks):
        return [(links.places[k], (blocks[k],)) for k in (1, 2, 3)]

    def gather_upstream():
        pieces, out = [cotangent], []
        plan = [(8, True, 0)] + [(0, s < planes - 1, s) for s in range(1, planes)]
        for idle, hop, step in plan:
            yield from hold(idle)
            asks = [(links.onward, (pieces[-1],))] if hop else []
            if step is not None:
                blocks = choose(pieces[step], step)
                asks += to_places(blocks)
            came = yield asks
            if hop:
                pieces.append(came[0])
            if step is not None:
                out.append(in_places(blocks[0], came[-3:]))
        return out

    upstream_task = spread(gather_upstream())

    head_rows = w_out.shape[0]
    to_block = [
        ((b * 2 + g) * planes + a, g * experts + links.device(a, b))
        for g in range(2)
        for a in range(planes)
        for b in range(4)
    ]
    from_block = [(there, here) for here, there in to_block]
    to_blocks = lambda value: lax.ppermute(value, ("dp", "expert"), to_block)
    from_blocks = lambda value: lax.ppermute(value, ("dp", "expert"), from_block)

    def gather_out():
        (own,) = yield [(to_blocks, (w_out,))]
        (own,) = yield from hold(1, own)
        pieces = yield from links.block_gather(own, (1, 0))
        pieces = jnp.concatenate(pieces, axis=0)
        (others,) = yield [(links.twin, (pieces,))]
        return jnp.concatenate([pieces, others], axis=0)

    out_task = spread(later(3, gather_out()))

    device_of = jnp.stack(
        [links.device(links.block(r), links.b ^ k) for r in range(planes) for k in range(4)]
    )
    starts = jnp.concatenate([(links.g ^ t) * experts + device_of for t in range(2)]) * rows
    all_slots = slots.reshape(experts, tokens)[device_of].reshape(experts * tokens)
    _, position = places(all_slots[:block_tokens], lengths[0])
    cosine, sine = rotary_tables(position)
    high = all_slots[:block_tokens]
    low = high - position

    found, block_hidden, qkv_pieces = rounds.until(small_task, hidden_task, qkv_task)
    normalized, block_scale, full_router, full_in, full_mid, head_gains = found
    w_qkv, projected, turned = rounds.run(
        work(project, starts, normalized, cosine, sine, head_gains, *qkv_pieces)
    )
    keys_values = jnp.concatenate(
        rounds.run(links.block_gather_short(turned[:, QW:])), axis=0
    )
    keys_turned = keys_values[:, :HEAD_SIZE].T
    values_turned = keys_values[:, HEAD_SIZE:].T
    place_column = all_slots[:, None]
    low, high = low[None, :], high[None, :]

    def part_of(array, part, parts):
        width = array.shape[1] // parts
        return array[:, part * width : (part + 1) * width]

    def forward_part(query_rows):
        return attention_forward(query_rows, keys_values, values_turned, place_column, low, high)

    attended = [
        rounds.run(work(forward_part, part_of(turned[:, :QW], part, 4)))
        for part in range(4)
    ]
    attended = jnp.concatenate(attended, axis=1)
    attended = jnp.concatenate(
        [
            lax.dynamic_slice_in_dim(
                attended, ((links.g ^ t) * planes + links.block(r)) * head_rows, head_rows, 1
            )
            for t in range(2)
            for r in range(planes)
        ],
        axis=1,
    )
    block_out = rounds.until(out_task)

    branch = jnp.dot(attended, block_out, preferred_element_type=F32)
    branch = rounds.run(links.head_scatter(branch))
    x_float = hidden.astype(F32)
    x_one = x_float + branch
    norm_two, norm_two_back = jax.vjp(rms_scale, x_one, full_mid)
    xn_two = norm_two.astype(BF)

    own_chooser = jnp.any(routes[:, :, None] == expert_numbers, axis=1)

    def masked_softmax(logits, chooser):
        top = jnp.max(jnp.where(chooser, logits, MASKED), axis=-1, keepdims=True)
        exponent = jnp.where(chooser, jnp.exp(jnp.where(chooser, logits - top, 0.0)), 0.0)
        total = jnp.sum(exponent, axis=-1, keepdims=True)
        return exponent / jnp.where(total > 0.0, total, 1.0)

    upstream_slots = rounds.until(upstream_task)
    me = links.index.astype(jnp.int32)[None]
    made = []

    def expert_step(step, *rows_in):
        found = expert_rows(
            me,
            as_blocks(list(rows_in)),
            as_blocks(upstream_slots[step]),
            tables["chooser"][step],
            full_router,
            gate_full,
            up_full,
            down_full,
        )
        if aligned:
            return (found[:4], found[4:8], found[8:])
        return (by_place(found[0]), by_place(found[1]), found[2:])

    def return_mixture():
        blocks = made[1][1]
        back = yield to_places(blocks)
        total = collect(in_places(blocks[0], back), 1, MODEL_WIDTH)
        yield from hold(2)
        (came,) = yield [(links.onward, (total,))]
        blocks = made[2][1]
        back = yield to_places(blocks)
        total = collect(in_places(blocks[0], back), 2, MODEL_WIDTH, came)
        for step in range(3, planes):
            blocks = made[step][1]
            came, *back = yield [(links.onward, (total,))] + to_places(blocks)
            total = collect(in_places(blocks[0], back), step, MODEL_WIDTH, came)
        (came,) = yield [(links.onward, (total,))]
        blocks = made[0][1]
        back = yield to_places(blocks)
        return collect(in_places(blocks[0], back), 0, MODEL_WIDTH, came, F32)

    def experts_there_and_back():
        piece, ready, own_plane, total = xn_two, None, None, None
        wide = MODEL_WIDTH + lanes
        for step in range(planes + 3):
            asks = []
            back = made[step - 2][0] if 2 <= step < planes + 2 else []
            blocks = back
            if step < planes:
                blocks = choose(piece, step, back)
            if blocks:
                asks += to_places(blocks)
            if step < planes - 1:
                asks += [(links.onward, (piece,))]
            if step >= 4:
                asks += [(links.onward, (total,))]
            if 1 <= step <= planes:
                asks += [(lambda *v, s=step - 1: expert_step(s, *v), tuple(ready))]
            if step == planes + 2:
                tables["mixture"] = spread(return_mixture())
            came = yield asks
            if blocks:
                ready, came = in_places(blocks[0], came[:3]), came[3:]
            if step < planes - 1:
                piece, came = came[0], came[1:]
            if step >= 4:
                hop, came = came[0], came[1:]
            if 1 <= step <= planes:
                made.append(came[0])
            if step == 2:
                own_plane = collect(ready, 0, wide, None, F32)
            elif step == 3:
                total = collect(ready, 1, wide)
            elif step >= 4 and step < planes + 2:
                total = collect(ready, step - 2, wide, hop)
        return own_plane + hop.astype(F32)

    moe_grad = rounds.run(experts_there_and_back())
    gate_grads = moe_grad[:, MODEL_WIDTH : MODEL_WIDTH + experts]
    moe_grad = moe_grad[:, :MODEL_WIDTH]
    stacked = lambda place: jnp.concatenate([piece[2][place] for piece in made], axis=0)

    def by_rows(rows_in, grads_in):
        return jnp.einsum("rd,rf->df", rows_in, grads_in, preferred_element_type=F32)

    half_width = MODEL_WIDTH // 2

    def half_of(array, which):
        return lax.dynamic_slice_in_dim(array, which * half_width, half_width, 1)

    def gate_up_gradient(place):
        rows_in, grads_in = stacked(0), stacked(place)
        return links.twin_scatter(
            by_rows,
            (half_of(rows_in, links.g), grads_in),
            (half_of(rows_in, 1 - links.g), grads_in),
            idle=8,
        )

    def down_gradient():
        rows_in, grads_in = stacked(1), stacked(2)
        return links.twin_scatter(
            by_rows,
            (rows_in, half_of(grads_in, links.g)),
            (rows_in, half_of(grads_in, 1 - links.g)),
            idle=3,
        )

    gate_task = spread(gate_up_gradient(3))
    up_task = spread(later(1, gate_up_gradient(4)))
    down_task = spread(later(7, down_gradient()))
    own_logits = jnp.dot(xn_two, full_router, preferred_element_type=F32)
    own_probs = masked_softmax(own_logits, own_chooser)

    upstream = cotangent.astype(F32)
    chosen_grad = own_probs * (
        gate_grads - jnp.sum(own_probs * gate_grads, axis=-1, keepdims=True)
    )
    logit_grad = chosen_grad.astype(BF)
    xn_two_grad = moe_grad + jnp.dot(logit_grad, full_router.T, preferred_element_type=F32)
    x_one_norm_grad, grad_mid = norm_two_back(xn_two_grad)
    x_one_grad = upstream + x_one_norm_grad
    branch_grad = x_one_grad.astype(BF)

    block_grad = rounds.run(links.head_gather(branch_grad))

    def head_gradients(block_grad, block_out):
        grad = jnp.einsum("td,hd->th", block_grad, block_out, preferred_element_type=F32)
        grad = grad.astype(BF)
        parts = []
        for head in range(2 * planes):
            twin, place = links.g ^ (head // planes), links.block(head % planes)
            if links.square:
                place = links.a ^ (head % planes)
            at = (twin * planes + place) * head_rows
            parts.append(lax.dynamic_slice_in_dim(grad, at, head_rows, 1))
        return jnp.concatenate(parts, axis=1)

    heads_task = spread(work(head_gradients, block_grad, block_out))

    def scatter_out():
        half = QW // 2
        grad = yield from links.twin_scatter(
            lambda rows_in, grads_in: jnp.einsum(
                "th,td->hd", rows_in, grads_in, preferred_element_type=F32
            ),
            (attended[:, :half], block_grad),
            (attended[:, half:], block_grad),
        )
        grad = grad.astype(BF)
        blocks = [grad[r * head_rows : (r + 1) * head_rows] for r in range(planes)]
        grad = yield from links.block_scatter(blocks, split=True)
        (grad,) = yield from hold(2, grad.astype(BF))
        grad = yield from work(from_blocks, grad)
        return grad.astype(F32)

    grad_out_task = spread(scatter_out())

    def owners_blocks(grad):
        blocks = []
        for r in range(planes):
            owners = [links.device(links.block(r), links.b ^ k) for k in range(4)]
            parts = [lax.dynamic_slice_in_dim(grad, owner * rows, rows, 0) for owner in owners]
            blocks.append(jnp.concatenate(parts, axis=0))
        return blocks

    def half_rows(array, which):
        return lax.dynamic_slice_in_dim(array, which * (MODEL_WIDTH // 2), MODEL_WIDTH // 2, 0)

    def query_gradient(grads_in, extra, idle):
        def make(which):
            grad = by_rows(half_of(normalized, which), grads_in)
            if extra is not None:
                grad = jnp.concatenate([grad, half_rows(extra, which)], axis=1)
            return grad

        grad = yield from links.twin_scatter(make, (links.g,), (1 - links.g,))
        blocks = yield from hold(idle[0], *owners_blocks(grad.astype(BF)))
        grad = yield from links.block_scatter(blocks, idle=idle[1])
        return grad.astype(BF)

    def exchange_owners(grad):
        grad = grad.reshape(4, rows, grad.shape[1])
        return links.exchange(links.heads, [grad[k] for k in range(4)])

    def key_value_gradient(key_value_grad, proj_grad):
        half = lambda which: by_rows(half_of(normalized, which), key_value_grad)
        found, other, own = yield [
            (input_gradient, (proj_grad, w_qkv, block_hidden, block_scale)),
            (half, (1 - links.g,)),
            (half, (links.g,)),
        ]
        xn_one_grad, grad_in = found
        tables["scatter"] = spread(links.head_scatter(xn_one_grad))
        sums = jnp.concatenate([grad_qgain, grad_kgain]).reshape(2, devices, head_part)
        sums = jnp.pad(sums, ((0, 0), (0, 0), (0, rows - head_part)))
        sums = jnp.concatenate([grad_in, sums.reshape(2, MODEL_WIDTH)], axis=0).T
        sums = jnp.pad(sums, ((0, 0), (0, lanes - sums.shape[1])))
        both = lambda grad, which: jnp.concatenate([grad, half_rows(sums, which)], axis=1)
        (came,) = yield [(links.twin, (both(other, 1 - links.g).astype(BF),))]
        grad = (both(own, links.g) + came.astype(F32)).astype(BF)
        grad = yield from links.block_scatter(owners_blocks(grad))
        return (yield from exchange_owners(grad.astype(BF)))

    attended_grad = rounds.until(heads_task)
    grad_router = jnp.dot(xn_two.T, logit_grad, preferred_element_type=F32)
    first = jnp.concatenate([grad_router, grad_mid[:, None]], axis=1)
    first = jnp.pad(first, ((0, 0), (0, lanes - first.shape[1])))
    query_low_grads, query_tasks, key_terms, grad_qgain = [], [], None, None
    parts = 4
    for part in range(parts):
        got = rounds.run(
            work(
                lambda *args: attention_backward(
                    *args,
                    keys_values,
                    keys_turned,
                    place_column,
                    low,
                    high,
                    cosine,
                    sine,
                    head_gains[0:1],
                ),
                part_of(turned[:, :QW], part, parts),
                part_of(attended_grad, part, parts),
                part_of(projected[:, :QW], part, parts),
            )
        )
        query_low_grads.append(got[0])
        key_terms = got[1] if part == 0 else key_terms + got[1]
        grad_qgain = got[2] if part == 0 else grad_qgain + got[2]
        if part % 2:
            low_grads = jnp.concatenate(query_low_grads[-2:], axis=1)
            more, idle = (None, (1, 0)) if query_tasks else (first, (0, 1))
            query_tasks.append(spread(query_gradient(low_grads, more, idle)))
    key_terms = rounds.run(
        links.block_scatter(
            [key_terms[r * block_tokens : (r + 1) * block_tokens] for r in range(planes)]
        )
    )

    key_proj_grad, grad_kgain = unturn(
        key_terms[:, :HEAD_SIZE],
        projected[:, QW : QW + HEAD_SIZE],
        cosine,
        sine,
        head_gains[1:2],
    )
    key_value_grad = jnp.concatenate([key_proj_grad, key_terms[:, HEAD_SIZE:].astype(BF)], axis=1)
    proj_grad = jnp.concatenate(query_low_grads + [key_value_grad], axis=1)
    key_value_task = spread(key_value_gradient(key_value_grad, proj_grad))
    one, two = rounds.until(*query_tasks)
    query_task = spread(exchange_owners(jnp.concatenate([one, two], axis=1)))
    xn_one_grad = rounds.until(tables["scatter"])
    _, norm_one_back = jax.vjp(lambda values: rms_scale(values, full_in), x_float)
    (x_norm_grad,) = norm_one_back(xn_one_grad)
    input_grad = (x_one_grad + x_norm_grad).astype(BF)

    grad_gate, grad_up, grad_down, mixture, grad_out, grad_query, grad_kv = rounds.until(
        gate_task,
        up_task,
        down_task,
        tables["mixture"],
        grad_out_task,
        query_task,
        key_value_task,
    )
    result = (x_one + mixture).astype(BF)
    half = QW // 2
    first = sum(block[:, half : half + lanes].astype(F32) for block in grad_query)
    last = sum(block[:, 2 * HEAD_SIZE :].astype(F32) for block in grad_kv)

    def whole(blocks):
        return jnp.concatenate(links.natural(blocks, links.b), axis=1).astype(F32)

    grad_query = whole(
        [
            jnp.concatenate([block[:, :half], block[:, half + lanes :]], axis=1)
            for block in grad_query
        ]
    )
    grad_key = whole([block[:, :HEAD_SIZE] for block in grad_kv])
    grad_value = whole([block[:, HEAD_SIZE : 2 * HEAD_SIZE] for block in grad_kv])
    grad_router, grad_mid = first[:, :experts], first[:, experts]
    grad_in = last[:, 0]
    grad_qgain, grad_kgain = last[:head_part, 1], last[:head_part, 2]

    return (
        result,
        input_grad,
        grad_in,
        grad_query,
        grad_key,
        grad_value,
        grad_qgain,
        grad_kgain,
        grad_out,
        grad_mid,
        grad_router,
        grad_gate[None],
        grad_up[None],
        grad_down[None],
    )


def solution(mesh):
    every = ("dp", "expert")
    in_specs = (
        P(every, None),
        P("dp", None),
        P("dp"),
        P(every, None),
        P(every, None),
        P(every),
        P(every, None),
        P(every, None),
        P(every, None),
        P(every),
        P(every),
        P(every, None),
        P(every),
        P(every, None),
        P("expert", "dp", None),
        P("expert", "dp", None),
        P("expert", None, "dp"),
        P(every, None),
    )
    out_specs = (
        P(every, None),
        P(every, None),
        P(every),
        P(every, None),
        P(every, None),
        P(every, None),
        P(every),
        P(every),
        P(every, None),
        P(every),
        P(every, None),
        P("expert", "dp", None),
        P("expert", "dp", None),
        P("expert", None, "dp"),
    )
    return jax.shard_map(body, mesh=mesh, in_specs=in_specs, out_specs=out_specs, check_vma=False)
```

```python
import jax
import jax.numpy as jnp
from jax import lax
from jax.experimental import pallas as pl
from jax.experimental.pallas import tpu as pltpu
from jax.sharding import PartitionSpec as P

MODEL_WIDTH = 2048
QUERY_HEADS = 32
KEY_VALUE_HEADS = 4
HEAD_SIZE = 128
TOP = 8
PER_KV = QUERY_HEADS // KEY_VALUE_HEADS
QW = PER_KV * HEAD_SIZE

EPS = 1e-06
THETA = 1000000.0
MASKED = -1e30
BF = jnp.bfloat16
F32 = jnp.float32


def rms_scale(values, scaling):
    return values * lax.rsqrt(jnp.mean(values * values, axis=-1, keepdims=True) + EPS) * scaling


def rotary_tables(position):
    half = HEAD_SIZE // 2
    index_float = jnp.arange(half, dtype=jnp.float32)
    freq = jnp.power(jnp.float32(THETA), -2.0 * index_float / HEAD_SIZE)
    angle = position.astype(jnp.float32)[:, None] * freq[None, :]
    cosine, sine = jnp.cos(angle), jnp.sin(angle)
    return (
        jnp.concatenate([cosine, cosine], axis=-1),
        jnp.concatenate([-sine, sine], axis=-1),
    )


def stack_kernel(rows, *refs):
    *block_refs, out_ref = refs
    blocks = [ref[...].astype(F32) for ref in block_refs]
    stack = [block[:rows] for block in blocks] + [block[rows:] for block in blocks]
    out_ref[...] = jnp.concatenate(stack, axis=0).astype(BF)


def stack_rows(blocks, rows):
    height, width = blocks[0].shape
    return pl.pallas_call(
        lambda *refs: stack_kernel(rows, *refs),
        out_shape=jax.ShapeDtypeStruct((height * len(blocks), width), BF),
    )(*blocks)


def project_kernel(starts_ref, x_ref, cos_ref, sin_ref, gains_ref, *refs):
    pieces, (w_ref, proj_ref, turned_ref) = refs[:-3], refs[-3:]
    last = pl.program_id(0) == pl.num_programs(0) - 1
    rows = pieces[0].shape[0] // 4
    for number, piece in enumerate(pieces):
        for k in range(4):
            at = pl.multiple_of(starts_ref[number * 4 + k], rows)
            w_ref[pl.ds(at, rows), :] = piece[k * rows : (k + 1) * rows, :]
    projected = jnp.dot(x_ref[...], w_ref[...], preferred_element_type=F32)
    proj_ref[...] = projected

    def turn(values, gain):
        scaled = (
            values * lax.rsqrt(jnp.mean(values * values, axis=-1, keepdims=True) + EPS) * gain
        )
        swapped = pltpu.roll(scaled, HEAD_SIZE // 2, 1)
        return scaled * cos_ref[...] + swapped * sin_ref[...]

    gain_q, gain_k = gains_ref[0:1], gains_ref[1:2]
    first, second = projected[:, :HEAD_SIZE], projected[:, HEAD_SIZE:]
    turned_ref[:, :HEAD_SIZE] = turn(first, jnp.where(last, gain_k, gain_q)).astype(BF)
    turned_ref[:, HEAD_SIZE:] = jnp.where(last, second, turn(second, gain_q)).astype(BF)


def project(rows, starts, rows_in, cosine, sine, gains, *pieces):
    count, width = rows_in.shape
    height, columns = 4 * rows, pieces[0].shape[1]
    step = 2 * HEAD_SIZE
    whole = lambda array: pl.BlockSpec(array.shape, lambda i: (0, 0))
    strip = lambda height: pl.BlockSpec((height, step), lambda i: (0, i))
    return pl.pallas_call(
        project_kernel,
        grid=(columns // step,),
        in_specs=[pl.BlockSpec(memory_space=pltpu.SMEM)]
        + [whole(rows_in), whole(cosine), whole(sine), whole(gains)]
        + [strip(height)] * len(pieces),
        out_specs=[strip(width), strip(count), strip(count)],
        out_shape=[
            jax.ShapeDtypeStruct((width, columns), BF),
            jax.ShapeDtypeStruct((count, columns), F32),
            jax.ShapeDtypeStruct((count, columns), BF),
        ],
        cost_estimate=pl.CostEstimate(
            flops=2 * count * width * columns,
            bytes_accessed=2 * (count + columns) * width,
            transcendentals=0,
        ),
        compiler_params=pltpu.CompilerParams(vmem_limit_bytes=60 * 2**20),
    )(starts, rows_in, cosine, sine, gains, *pieces)


def unturned(grad, values, cosine, sine, gain):
    grad = grad * cosine + pltpu.roll(grad * sine, HEAD_SIZE // 2, 1)
    scale = lax.rsqrt(jnp.mean(values * values, axis=-1, keepdims=True) + EPS)
    gain_grad = jnp.sum(grad * values * scale, axis=0, keepdims=True)
    grad = grad * gain
    inner = jnp.mean(grad * values, axis=-1, keepdims=True)
    return (scale * grad - values * (scale * scale * scale * inner)).astype(BF), gain_grad


def unturn_kernel(grad_ref, proj_ref, cos_ref, sin_ref, gain_ref, out_ref, gain_grad_ref):
    out_ref[...], gain_grad_ref[...] = unturned(
        grad_ref[...], proj_ref[...], cos_ref[...], sin_ref[...], gain_ref[...]
    )


def unturn(grad, projected, cosine, sine, gain):
    return pl.pallas_call(
        unturn_kernel,
        out_shape=[
            jax.ShapeDtypeStruct(grad.shape, BF),
            jax.ShapeDtypeStruct(gain.shape, F32),
        ],
    )(grad, projected, cosine, sine, gain)


def input_kernel(grad_ref, w_ref, out_ref):
    dims = (((1,), (1,)), ((), ()))
    out_ref[...] = lax.dot_general(grad_ref[...], w_ref[...], dims, preferred_element_type=F32)


def input_gradient(proj_grad, weights):
    count, columns = proj_grad.shape
    width = weights.shape[0]
    step = 256
    return pl.pallas_call(
        input_kernel,
        grid=(width // step,),
        in_specs=[
            pl.BlockSpec((count, columns), lambda i: (0, 0)),
            pl.BlockSpec((step, columns), lambda i: (i, 0)),
        ],
        out_specs=pl.BlockSpec((count, step), lambda i: (0, i)),
        out_shape=jax.ShapeDtypeStruct((count, width), F32),
        cost_estimate=pl.CostEstimate(
            flops=2 * count * width * columns,
            bytes_accessed=6 * (count + columns) * width,
            transcendentals=0,
        ),
        compiler_params=pltpu.CompilerParams(vmem_limit_bytes=24 * 2**20),
    )(proj_grad, weights)


def output_kernel(order_ref, *refs):
    *part_refs, own_ref, other_ref, out_ref, rows_ref, natural_ref = refs
    half = own_ref.shape[0]

    @pl.when(pl.program_id(0) == 0)
    def _():
        at = 0
        for part_ref in part_refs:
            width = part_ref.shape[1]
            natural_ref[:, at : at + width] = part_ref[...]
            at += width
        for head in range(at // HEAD_SIZE):
            start = pl.multiple_of(order_ref[head] * HEAD_SIZE, HEAD_SIZE)
            here = slice(head * HEAD_SIZE, (head + 1) * HEAD_SIZE)
            rows_ref[:, here] = natural_ref[:, pl.ds(start, HEAD_SIZE)]

    out_ref[...] = jnp.dot(
        rows_ref[:, :half], own_ref[...], preferred_element_type=F32
    ) + jnp.dot(rows_ref[:, half:], other_ref[...], preferred_element_type=F32)


def output_projection(order, parts, own, other):
    count = parts[0].shape[0]
    half, width = own.shape
    columns = 2 * half
    step = 256
    strip = lambda height: pl.BlockSpec((height, step), lambda i: (0, i))
    whole = lambda shape: pl.BlockSpec(shape, lambda i: (0, 0))
    return pl.pallas_call(
        output_kernel,
        grid=(width // step,),
        in_specs=[pl.BlockSpec(memory_space=pltpu.SMEM)]
        + [whole(part.shape) for part in parts]
        + [strip(half), strip(half)],
        out_specs=[strip(count), whole((count, columns))],
        out_shape=[
            jax.ShapeDtypeStruct((count, width), F32),
            jax.ShapeDtypeStruct((count, columns), BF),
        ],
        scratch_shapes=[pltpu.VMEM((count, columns), BF)],
        cost_estimate=pl.CostEstimate(
            flops=2 * count * width * columns,
            bytes_accessed=4 * (count + columns) * width,
            transcendentals=0,
        ),
        compiler_params=pltpu.CompilerParams(vmem_limit_bytes=24 * 2**20),
    )(order, *parts, own, other)


def forward_kernel(q_ref, kv_ref, vt_ref, place_ref, low_ref, high_ref, out_ref, p_ref):
    count, queries = p_ref.shape
    step = min(512, count)
    chunks = [slice(at, at + step) for at in range(0, count, step)]
    q, low, high = q_ref[...], low_ref[...], high_ref[...]
    top = jnp.full((1, queries), MASKED, F32)
    for chunk in chunks:
        place = place_ref[chunk, :]
        seen = (place >= low) & (place <= high)
        scores = lax.dot_general(
            kv_ref[chunk, :HEAD_SIZE], q, (((1,), (1,)), ((), ())), preferred_element_type=F32
        )
        scores = jnp.where(seen, scores * HEAD_SIZE**-0.5, MASKED)
        p_ref[chunk, :] = scores
        top = jnp.maximum(top, jnp.max(scores, axis=0, keepdims=True))
    total = jnp.zeros((1, queries), F32)
    for chunk in chunks:
        exponent = jnp.exp(p_ref[chunk, :] - top)
        p_ref[chunk, :] = exponent
        total = total + jnp.sum(exponent, axis=0, keepdims=True)
    share = 1.0 / total
    out = jnp.zeros((HEAD_SIZE, queries), F32)
    for chunk in chunks:
        probs = (p_ref[chunk, :] * share).astype(BF)
        out = out + jnp.dot(vt_ref[:, chunk], probs, preferred_element_type=F32)
    out_ref[...] = out.T.astype(BF)


def attention_blocks(rows, count):
    step = min(rows, 512 * 2048 // count)
    whole = lambda array: pl.BlockSpec(array.shape, lambda i, j: (0, 0))
    head = pl.BlockSpec((step, HEAD_SIZE), lambda i, j: (j, i))
    along = pl.BlockSpec((1, step), lambda i, j: (0, j))
    down = pl.BlockSpec((step, HEAD_SIZE), lambda i, j: (j, 0))
    limit = (32 if count <= 2048 else 60) * 2**20
    return step, whole, head, along, down, limit


def attention_forward(q, keys_values, values_turned, place, low, high):
    rows, columns = q.shape
    count = keys_values.shape[0]
    step, whole, head, along, _, limit = attention_blocks(rows, count)
    return pl.pallas_call(
        forward_kernel,
        grid=(columns // HEAD_SIZE, rows // step),
        in_specs=[head, whole(keys_values), whole(values_turned), whole(place), along, along],
        out_specs=head,
        out_shape=jax.ShapeDtypeStruct(q.shape, BF),
        scratch_shapes=[pltpu.VMEM((count, step), F32)],
        cost_estimate=pl.CostEstimate(
            flops=8 * rows * columns * count, bytes_accessed=4 * rows * columns, transcendentals=0
        ),
        compiler_params=pltpu.CompilerParams(vmem_limit_bytes=limit),
    )(q, keys_values, values_turned, place, low, high)


def backward_kernel(
    q_ref, grad_ref, proj_ref, kv_ref, kt_ref, place_ref, low_ref, high_ref, cos_ref, sin_ref,
    gain_ref, out_ref, dkv_ref, gain_grad_ref, p_ref, dp_ref,
):
    @pl.when((pl.program_id(0) == 0) & (pl.program_id(1) == 0))
    def _():
        dkv_ref[...] = jnp.zeros_like(dkv_ref)
        gain_grad_ref[...] = jnp.zeros_like(gain_grad_ref)

    count, queries = p_ref.shape
    step = min(512, count)
    chunks = [slice(at, at + step) for at in range(0, count, step)]
    scale = HEAD_SIZE**-0.5
    q, grad = q_ref[...], grad_ref[...]
    low, high = low_ref[...], high_ref[...]

    def across(left, right):
        dims = (((1,), (1,)), ((), ()))
        return lax.dot_general(left, right, dims, preferred_element_type=F32)

    top = jnp.full((1, queries), MASKED, F32)
    for chunk in chunks:
        place = place_ref[chunk, :]
        seen = (place >= low) & (place <= high)
        scores = jnp.where(seen, across(kv_ref[chunk, :HEAD_SIZE], q) * scale, MASKED)
        p_ref[chunk, :] = scores
        top = jnp.maximum(top, jnp.max(scores, axis=0, keepdims=True))
    total = inner = jnp.zeros((1, queries), F32)
    for chunk in chunks:
        exponent = jnp.exp(p_ref[chunk, :] - top)
        p_ref[chunk, :] = exponent
        total = total + jnp.sum(exponent, axis=0, keepdims=True)
        prob_grad = across(kv_ref[chunk, HEAD_SIZE:], grad)
        dp_ref[chunk, :] = prob_grad
        inner = inner + jnp.sum(exponent * prob_grad, axis=0, keepdims=True)
    share = 1.0 / total
    inner = inner * share
    dq = jnp.zeros((HEAD_SIZE, queries), F32)
    for chunk in chunks:
        probs = p_ref[chunk, :] * share
        score_grad = (probs * (dp_ref[chunk, :] - inner)).astype(BF)
        dkv_ref[chunk, HEAD_SIZE:] += jnp.dot(probs.astype(BF), grad, preferred_element_type=F32)
        dkv_ref[chunk, :HEAD_SIZE] += (
            jnp.dot(score_grad, q, preferred_element_type=F32) * scale
        )
        dq = dq + jnp.dot(kt_ref[:, chunk], score_grad, preferred_element_type=F32)
    out_ref[...], gain_grad = unturned(
        dq.T * scale, proj_ref[...], cos_ref[...], sin_ref[...], gain_ref[...]
    )
    gain_grad_ref[...] += gain_grad


def attention_backward(
    q, grad, projected, keys_values, keys_turned, place, low, high, cosine, sine, gain
):
    rows, columns = q.shape
    count = keys_values.shape[0]
    step, whole, head, along, down, limit = attention_blocks(rows, count)
    return pl.pallas_call(
        backward_kernel,
        grid=(columns // HEAD_SIZE, rows // step),
        in_specs=[head, head, head, whole(keys_values), whole(keys_turned), whole(place)]
        + [along, along, down, down, whole(gain)],
        out_specs=[head, whole(keys_values), whole(gain)],
        out_shape=[
            jax.ShapeDtypeStruct(q.shape, BF),
            jax.ShapeDtypeStruct(keys_values.shape, F32),
            jax.ShapeDtypeStruct(gain.shape, F32),
        ],
        scratch_shapes=[pltpu.VMEM((count, step), F32)] * 2,
        cost_estimate=pl.CostEstimate(
            flops=10 * rows * columns * count, bytes_accessed=8 * rows * columns, transcendentals=0
        ),
        compiler_params=pltpu.CompilerParams(vmem_limit_bytes=limit),
    )(q, grad, projected, keys_values, keys_turned, place, low, high, cosine, sine, gain)


def choose_kernel(blocks, table_ref, piece_ref, *refs):
    chosen = jnp.dot(table_ref[...], piece_ref[...], preferred_element_type=F32)
    back_refs, out_refs = refs[:-blocks], refs[-blocks:]
    count = out_refs[0].shape[0]
    width = piece_ref.shape[1]
    for k, out_ref in enumerate(out_refs):
        part = chosen[k * count : (k + 1) * count].astype(BF)
        if back_refs:
            out_ref[:, :width] = part
            out_ref[:, width:] = back_refs[k][...]
        else:
            out_ref[...] = part


def choose_rows(table, piece, blocks, backs=()):
    width = piece.shape[1] + (backs[0].shape[1] if backs else 0)
    shape = (table.shape[0] // blocks, width)
    return pl.pallas_call(
        lambda *refs: choose_kernel(blocks, *refs),
        out_shape=[jax.ShapeDtypeStruct(shape, BF)] * blocks,
        compiler_params=pltpu.CompilerParams(vmem_limit_bytes=16 * 2**20),
    )(table, piece, *backs)


def collect_kernel(blocks, table_ref, *refs):
    width = refs[-1].shape[1]
    rows_in = [ref[:, ref.shape[1] - width :].astype(F32) for ref in refs[:blocks]]
    stack = jnp.concatenate(rows_in, axis=0).astype(BF)
    total = jnp.dot(table_ref[...], stack, preferred_element_type=F32)
    if len(refs) > blocks + 1:
        total = total + refs[blocks][...].astype(F32)
    refs[-1][...] = total.astype(refs[-1].dtype)


def collect_rows(table, blocks, width, more=None, kind=BF):
    extra = [] if more is None else [more]
    return pl.pallas_call(
        lambda *refs: collect_kernel(len(blocks), *refs),
        out_shape=jax.ShapeDtypeStruct((table.shape[0], width), kind),
        compiler_params=pltpu.CompilerParams(vmem_limit_bytes=24 * 2**20),
    )(table, *blocks, *extra)


def expert_kernel(blocks, me_ref, *refs):
    rows_refs, refs = refs[:blocks], refs[blocks:]
    upstream_ref, chooser_ref, router_ref, gate_ref, up_ref, down_ref = refs[:6]
    back_refs, mixed_refs = refs[6 : 6 + blocks], refs[6 + blocks : 6 + 2 * blocks]
    refs = refs[6 + 2 * blocks :]
    rows_ref, act_ref, out_grad_ref, gate_low_ref, up_low_ref = refs[:5]
    share_ref, returned_ref, pair_ref = refs[5:]
    step = pl.program_id(0)
    across = (((1,), (1,)), ((), ()))

    @pl.when(step == 0)
    def _():
        rows_in = jnp.concatenate([ref[...].astype(F32) for ref in rows_refs], axis=0).astype(BF)
        upstream = upstream_ref[...].astype(F32)
        logits = jnp.dot(rows_in, router_ref[...], preferred_element_type=F32)
        chosen = chooser_ref[...] > 0.0
        top = jnp.max(jnp.where(chosen, logits, MASKED), axis=1, keepdims=True)
        exponent = jnp.where(chosen, jnp.exp(jnp.where(chosen, logits - top, 0.0)), 0.0)
        total = jnp.sum(exponent, axis=1, keepdims=True)
        number = lax.broadcasted_iota(jnp.int32, exponent.shape, 1)
        mine = jnp.sum(jnp.where(number == me_ref[0], exponent, 0.0), axis=1, keepdims=True)
        share = mine / jnp.where(total > 0.0, total, 1.0)
        rows_ref[...] = rows_in
        out_grad_ref[...] = (share * upstream).astype(BF)
        share_ref[...] = jnp.broadcast_to(share, share_ref.shape)
        returned_ref[...] = jnp.zeros_like(returned_ref)
        pair_ref[...] = jnp.zeros_like(pair_ref)

    rows_in, out_grad = rows_ref[...], out_grad_ref[...]
    gate, up, down = gate_ref[...], up_ref[...], down_ref[...]
    gate_pre = jnp.dot(rows_in, gate, preferred_element_type=F32)
    up_pre = jnp.dot(rows_in, up, preferred_element_type=F32)
    act_grad = lax.dot_general(out_grad, down, across, preferred_element_type=F32)
    logistic = jax.nn.sigmoid(gate_pre)
    silu = gate_pre * logistic
    act = (silu * up_pre).astype(BF)
    gate_low = (act_grad * up_pre * logistic * (1.0 + gate_pre * (1.0 - logistic))).astype(BF)
    up_low = (act_grad * silu).astype(BF)
    act_ref[...], gate_low_ref[...], up_low_ref[...] = act, gate_low, up_low
    returned_ref[...] += jnp.dot(act, down, preferred_element_type=F32)
    pair_ref[...] += lax.dot_general(
        gate_low, gate, across, preferred_element_type=F32
    ) + lax.dot_general(up_low, up, across, preferred_element_type=F32)

    @pl.when(step == pl.num_programs(0) - 1)
    def _():
        returned = returned_ref[...].astype(BF).astype(F32)
        upstream = upstream_ref[...].astype(F32)
        gate_grad = jnp.sum(upstream * returned, axis=1, keepdims=True)
        mixed = share_ref[:, :1] * returned
        pair = pair_ref[...]
        count = rows_refs[0].shape[0]
        width = pair.shape[1]
        number = lax.broadcasted_iota(jnp.int32, share_ref.shape, 1)
        gates = jnp.where(number == me_ref[0], gate_grad, 0.0)
        for k in range(blocks):
            part = slice(k * count, (k + 1) * count)
            back_refs[k][:, :width] = pair[part].astype(BF)
            back_refs[k][:, width:] = gates[part].astype(BF)
            mixed_refs[k][...] = mixed[part].astype(BF)


def expert_rows(me, rows_in, upstream, chooser, router, gate, up, down):
    blocks = len(rows_in)
    slots, width = upstream.shape
    block = (slots // blocks, width)
    ff = gate.shape[1]
    step = 256
    lanes = 128
    whole = lambda shape: pl.BlockSpec(shape, lambda i: (0, 0))
    columns = lambda height: pl.BlockSpec((height, step), lambda i: (0, i))
    shape = jax.ShapeDtypeStruct
    out = [((block[0], width + lanes), BF)] * blocks + [(block, BF)] * blocks
    out_specs = [whole(dims) for dims, _ in out]
    out_specs += [whole((slots, width)), columns(slots), whole((slots, width))]
    out_specs += [columns(slots)] * 2
    out += [((slots, width), BF), ((slots, ff), BF), ((slots, width), BF)]
    out += [((slots, ff), BF)] * 2
    return pl.pallas_call(
        lambda *refs: expert_kernel(blocks, *refs),
        grid=(ff // step,),
        in_specs=[pl.BlockSpec(memory_space=pltpu.SMEM)]
        + [whole(block)] * blocks
        + [whole(upstream.shape), whole(chooser.shape), whole(router.shape)]
        + [columns(width), columns(width), pl.BlockSpec((step, width), lambda i: (i, 0))],
        out_specs=out_specs,
        out_shape=[shape(dims, kind) for dims, kind in out],
        scratch_shapes=[
            pltpu.VMEM((slots, lanes), F32),
            pltpu.VMEM((slots, width), F32),
            pltpu.VMEM((slots, width), F32),
        ],
        cost_estimate=pl.CostEstimate(
            flops=12 * slots * width * ff, bytes_accessed=6 * width * ff, transcendentals=0
        ),
        compiler_params=pltpu.CompilerParams(vmem_limit_bytes=44 * 2**20),
    )(me, *rows_in, upstream, chooser, router, gate, up, down)


def table_kernel(capacity, ids_ref, pairs_ref, send_ref, back_ref, chosen_ref):
    mine_a, mine_b = ids_ref[0], ids_ref[1]
    slots, tokens = send_ref.shape[1:]
    experts = chosen_ref.shape[2]
    numbers = lax.broadcasted_iota(jnp.int32, (slots, tokens), 0).astype(F32)
    nowhere = 1e6

    def table(source, expert, k):
        hit = pairs_ref[0, source, 0] == expert.astype(F32)
        order = pairs_ref[0, source, 1] * 32.0 + pairs_ref[0, source, 2]
        place = jnp.min(jnp.where(hit, order, nowhere), axis=0, keepdims=True)
        across = jnp.broadcast_to(place, (tokens, tokens))
        before = jnp.where(across.T < across, 1.0, 0.0)
        rank = jnp.sum(before, axis=0, keepdims=True)
        inside = (place < nowhere) & (rank < capacity)
        rank = jnp.where(inside, rank + k * capacity, -1.0)
        return jnp.where(numbers == rank, 1.0, 0.0)

    send = chosen = 0.0
    for k in range(4):
        send = send + table(0, mine_a * 4 + (mine_b ^ k), k)
        kept = table(k, mine_a * 4 + mine_b, k)
        routes = pairs_ref[0, k, 0]
        expert_rows = lax.broadcasted_iota(jnp.int32, (experts, tokens), 0).astype(F32)
        chooser = sum(
            jnp.where(routes[j : j + 1] == expert_rows, 1.0, 0.0) for j in range(TOP)
        )
        chosen = chosen + lax.dot_general(
            kept.astype(BF),
            chooser.astype(BF),
            (((1,), (1,)), ((), ())),
            preferred_element_type=F32,
        )
    send_ref[0] = send.astype(BF)
    back_ref[0] = send.T.astype(BF)
    chosen_ref[0] = chosen


def slot_tables(ids, pairs, capacity, experts):
    planes, _, _, _, tokens = pairs.shape
    slots = 4 * capacity
    block = lambda *shape: pl.BlockSpec((1,) + shape, lambda i: (i,) + (0,) * len(shape))
    return pl.pallas_call(
        lambda *refs: table_kernel(capacity, *refs),
        grid=(planes,),
        in_specs=[pl.BlockSpec(memory_space=pltpu.SMEM), block(4, 3, TOP, tokens)],
        out_specs=[block(slots, tokens), block(tokens, slots), block(slots, experts)],
        out_shape=[
            jax.ShapeDtypeStruct((planes, slots, tokens), BF),
            jax.ShapeDtypeStruct((planes, tokens, slots), BF),
            jax.ShapeDtypeStruct((planes, slots, experts), F32),
        ],
    )(ids, pairs)


def places(slot_rows, lengths_row):
    seq_ends = jnp.cumsum(lengths_row)
    starts = seq_ends - lengths_row
    segment = jnp.sum((slot_rows[:, None] >= seq_ends[None, :]).astype(jnp.int32), axis=1)
    chosen = segment[:, None] == jnp.arange(lengths_row.shape[0], dtype=jnp.int32)[None, :]
    start_of = jnp.sum(jnp.where(chosen, starts[None, :], 0), axis=1)
    return (segment, slot_rows - start_of)


def pick(blocks, index):
    return lax.dynamic_index_in_dim(blocks, index, 0, keepdims=False)


class Rounds:
    def __init__(self):
        self.active = {}
        self.asked = {}
        self.values = {}
        self.count = 0
        self.strict = True
        self.alone = False

    def start(self, task):
        self.count += 1
        self.active[self.count] = (task, None)
        return self.count

    def until(self, *wanted):
        def waiting_now():
            ready = [n for n in self.active if n in wanted] if self.alone else self.active
            return [number for number in ready if number not in self.asked]

        while True:
            while waiting := waiting_now():
                for number in waiting:
                    task, came = self.active[number]
                    try:
                        self.asked[number] = task.send(came)
                    except StopIteration as end:
                        self.values[number] = end.value
                        del self.active[number]
            if all(number in self.values for number in wanted):
                break
            asked = {n: c for n, c in self.asked.items() if n in wanted or not self.alone}
            given = {number: [args for _, args in calls] for number, calls in asked.items()}
            if self.strict:
                given = lax.optimization_barrier(given)
            came = {
                number: [call(*args) for (call, _), args in zip(calls, given[number])]
                for number, calls in asked.items()
            }
            if self.strict:
                came = lax.optimization_barrier(came)
            for number, results in came.items():
                self.active[number] = (self.active[number][0], results)
            self.asked = {n: calls for n, calls in self.asked.items() if n not in asked}
        values = [self.values[number] for number in wanted]
        return values[0] if len(values) == 1 else values

    def run(self, task):
        return self.until(self.start(task))

    def loosely(self, *wanted, alone=False):
        self.strict, self.alone = False, alone
        values = self.until(*wanted)
        self.strict, self.alone = True, False
        return values


def hold(count, *values):
    for _ in range(count):
        (values,) = yield [(lambda *v: v, values)]
    return values


def later(count, task):
    yield from hold(count)
    return (yield from task)


def work(function, *args):
    (result,) = yield [(function, args)]
    return result


class Links:
    def __init__(self, n):
        self.n = n
        self.planes = n // 4
        index = lax.axis_index("expert")
        self.g = lax.axis_index("dp")
        self.index = index
        self.p = index % 4
        self.l = index // 4
        self.square = n == 16
        if self.square:
            self.a = index % 2 + index // 8 * 2
            self.b = index // 2 % 2 * 2 + index // 4 % 2
        else:
            self.a, self.b = self.l, self.p
        masks = (0, 4, 2, 6) if self.square else (0, 1, 2, 3)
        self.places = [lambda v, k=k: self.flip(v, k) for k in range(4)]
        self.heads = [lambda v, m=m: self.flip(v, m) for m in masks]
        self.shifts = [lambda v, s=s: self.shift(v, s) for s in range(self.planes)]
        self.backs = [lambda v, s=s: self.shift(v, -s) for s in range(self.planes)]

    def device(self, a, b):
        if not self.square:
            return a * 4 + b
        return a % 2 + b // 2 * 2 + b % 2 * 4 + a // 2 * 8

    def row_block(self, g, a):
        return a % 2 + g * 2 + a // 2 * 4 if self.square else g * self.planes + a

    def block(self, r):
        return self.a ^ r if self.square else (self.a - r) % self.planes

    def flip(self, value, mask):
        return lax.ppermute(value, "expert", [(i, i ^ mask) for i in range(self.n)])

    def shift(self, value, step):
        return lax.ppermute(
            value, "expert", [(i, (i + step * 4) % self.n) for i in range(self.n)]
        )

    def onward(self, value):
        return self.shift(value, 1)

    def twin(self, value):
        return lax.ppermute(value, "dp", [(0, 1), (1, 0)])

    def natural(self, blocks, mine):
        odd, high = mine % 2 == 1, mine >= 2
        pair = [jnp.where(odd, blocks[q ^ 1], blocks[q]) for q in range(4)]
        return [jnp.where(high, pair[q ^ 2], pair[q]) for q in range(4)]

    def turned_line(self, blocks):
        twice = jnp.concatenate([blocks[::-1], blocks[::-1]], axis=0)
        return lax.dynamic_slice_in_dim(twice, self.planes - 1 - self.l, self.planes, 0)

    def head_gather(self, own):
        half = own.shape[0] // 2
        near_x, near_y = yield [(self.heads[1], (own,)), (self.heads[2], (own,))]
        low, high = yield [(self.heads[2], (near_x[:half],)), (self.heads[1], (near_y[half:],))]
        return jnp.concatenate([own, near_x, near_y, low, high], axis=0)

    def exchange(self, flips, blocks):
        came = yield [(flips[k], (blocks[k],)) for k in (3, 1, 2)]
        return [blocks[0], came[1], came[2], came[0]]

    def head_scatter(self, total):
        count = total.shape[0] // 4
        half = count // 2
        cut = lambda k, low, high: total[k * count + low : k * count + high]
        low, high = yield [
            (self.heads[2], (cut(3, 0, half).astype(BF),)),
            (self.heads[1], (cut(3, half, count).astype(BF),)),
        ]
        to_x = jnp.concatenate([cut(1, 0, half) + low.astype(F32), cut(1, half, count)], axis=0)
        to_y = jnp.concatenate([cut(2, 0, half), cut(2, half, count) + high.astype(F32)], axis=0)
        got_x, got_y = yield [
            (self.heads[1], (to_x.astype(BF),)),
            (self.heads[2], (to_y.astype(BF),)),
        ]
        return cut(0, 0, count) + got_x.astype(F32) + got_y.astype(F32)

    def block_gather(self, own, idle=(0, 0), count=None, give=None):
        if not self.square:
            came = yield [(shift, (own,)) for shift in self.shifts[1:]]
            return [own] + came
        x, z = (lambda v: self.flip(v, 1)), (lambda v: self.flip(v, 8))
        count = count or own.shape[0]
        half = count // 2 + own.shape[0] - count
        near, low = yield [(x, (own,)), (z, (own[:half],))]
        near, low = yield from hold(idle[0], near, low)
        rest = count - half
        more = [own[half:]] if give is None else [own[half:], near[count:]]
        high, far_low = yield [(z, (jnp.concatenate(more),)), (x, (low,))]
        high, far_low = yield from hold(idle[1], high, far_low)
        if give is not None:
            give(jnp.concatenate([own[count:], near[count:], high[rest:]]))
        (far_high,) = yield [(x, (high[:rest],))]
        return [
            own,
            near,
            jnp.concatenate([low, high[:rest]], axis=0),
            jnp.concatenate([far_low, far_high], axis=0),
        ]

    def block_gather_short(self, own):
        if not self.square:
            came = yield [(shift, (own,)) for shift in self.shifts[1:]]
            return [own] + came
        x, z = (lambda v: self.flip(v, 1)), (lambda v: self.flip(v, 8))
        near, across = yield [(x, (own,)), (z, (own,))]
        (far,) = yield [(x, (across,))]
        return [own, near, across, far]

    def block_scatter(self, blocks, split=False, idle=0):
        if not self.square:
            came = yield [
                (back, (block.astype(BF),)) for back, block in zip(self.backs[1:], blocks[1:])
            ]
            return sum((block.astype(F32) for block in came), blocks[0].astype(F32))
        x, z = (lambda v: self.flip(v, 1)), (lambda v: self.flip(v, 8))
        (came,) = yield [(x, (blocks[3].astype(BF),))]
        (came,) = yield from hold(idle, came)
        across = (blocks[2].astype(F32) + came.astype(F32)).astype(BF)
        if split:
            half = across.shape[0] // 2
            (got,) = yield [(z, (across[:half],))]
            near, more = yield [(x, (blocks[1].astype(BF),)), (z, (across[half:],))]
            got = jnp.concatenate([got, more], axis=0)
        else:
            near, got = yield [(x, (blocks[1].astype(BF),)), (z, (across,))]
        return blocks[0].astype(F32) + near.astype(F32) + got.astype(F32)

    def twin_scatter(self, make, own, other, idle=None, now=False):
        low = lambda *args: make(*args).astype(BF)
        if now:
            block = low(*other)
        else:
            (block,) = yield [(low, other)]
        if idle is None:
            came, total = yield [(self.twin, (block,)), (make, own)]
            return total + came.astype(F32)
        (came,) = yield [(self.twin, (block,))]
        (came,) = yield from hold(idle, came)
        (total,) = yield [(lambda came, *args: make(*args) + came.astype(F32), (came, *own))]
        return total


def body(
    hidden,
    lengths,
    slots,
    routes,
    order,
    gain_in,
    w_query,
    key_projection_weight,
    value_projection_weight,
    gain_q,
    gain_k,
    w_out,
    gain_mid,
    w_router,
    w_gate,
    w_up,
    w_down,
    cotangent,
):
    tokens = hidden.shape[0]
    experts = w_router.shape[1]
    links = Links(experts)
    planes = links.planes
    capacity = max(2, (tokens * TOP * 9 + 8 * experts - 1) // (8 * experts))
    block_tokens = 4 * tokens
    rows = gain_in.shape[0]
    head_part = gain_q.shape[0]
    devices = 2 * experts

    rounds = Rounds()
    spread = rounds.start
    slot_count = 4 * capacity

    gate_full = lax.all_gather(w_gate, "dp", axis=1, tiled=True)[0]
    up_full = lax.all_gather(w_up, "dp", axis=1, tiled=True)[0]
    down_full = lax.all_gather(w_down, "dp", axis=2, tiled=True)[0]

    lanes = 128
    gains = jnp.concatenate([gain_in, gain_mid, gain_q, gain_k], axis=0)
    gain_count = gains.shape[0]
    gains = jnp.pad(gains, (0, -gain_count % lanes)).reshape(-1, lanes)
    router_rows = rows * experts // lanes
    small = jnp.concatenate([w_router.reshape(-1, lanes), gains], axis=0)
    small = jnp.pad(small, ((0, -small.shape[0] % 8), (0, 0)))
    small_rows = small.shape[0]
    pairs = jnp.concatenate([part.T.astype(BF) for part in (routes, order // 32, order % 32)])
    expert_numbers = jnp.arange(experts, dtype=jnp.int32)
    ids = jnp.stack([links.l, links.p]).astype(jnp.int32)
    tables = {}

    qkv_width = QW + 2 * HEAD_SIZE
    rider = jnp.concatenate([small, pairs], axis=0)
    rider_rows = rider.shape[0]

    def own_columns(b):
        cut = lambda array, width: lax.dynamic_slice_in_dim(array, b * width, width, 1)
        return jnp.concatenate(
            [
                cut(w_query, QW),
                cut(key_projection_weight, HEAD_SIZE),
                cut(value_projection_weight, HEAD_SIZE),
            ],
            axis=1,
        )

    def gather_qkv():
        blocks = [own_columns(links.b ^ k) for k in range(4)]
        if not links.square:
            blocks = yield from links.exchange(links.heads, blocks)
            pieces = yield from links.block_gather(jnp.concatenate(blocks, axis=0))
            others = yield [(links.twin, (piece,)) for piece in pieces]
            return pieces + others
        more = rider.reshape(-1, qkv_width)
        held = more.shape[0]
        more = jnp.pad(more, ((0, -held % 8), (0, 0)))
        blocks = [jnp.concatenate([block, more], axis=0) for block in blocks]
        blocks = yield from links.exchange(links.heads, blocks)
        wide = stack_rows(blocks, rows)

        def give(found):
            found = found.reshape(4, 4, -1, qkv_width)[:, :, :held]
            tables["riders"] = found.reshape(4, 4, rider_rows, lanes)

        pieces = yield from links.block_gather(wide, count=4 * rows, give=give)
        others = yield [(links.twin, (piece,)) for piece in pieces]
        return pieces + others

    def gather_small():
        if links.square:
            yield from hold(3)
            parts = tables["riders"]
            parts = jnp.stack(links.natural([parts[r] for r in range(4)], links.a))
            parts = jnp.stack(links.natural([parts[:, k] for k in range(4)], links.b), axis=1)
            parts = parts.reshape(2, 2, 2, 2, rider_rows, lanes).transpose(0, 3, 2, 1, 4, 5)
            parts = parts.reshape(experts, rider_rows, lanes)
        else:
            blocks = yield from links.exchange(links.places, [rider] * 4)
            line = jnp.stack(links.natural(blocks, links.p))
            came = yield [(shift, (line,)) for shift in links.shifts[1:]]
            parts = links.turned_line(jnp.stack([line] + came))
            parts = parts.reshape(experts, rider_rows, lanes)
            yield from hold(1)
        own_small = parts[:, :small_rows]
        (other_small,) = yield [(links.twin, (own_small,))]
        tables["pairs"] = parts[:, small_rows:]
        return (yield from work(sort_small, own_small, other_small, rounds.values[hidden_task]))

    def sort_small(own_small, other_small, block_hidden):
        swap = links.g == 1
        small_all = jnp.concatenate(
            [jnp.where(swap, other_small, own_small), jnp.where(swap, own_small, other_small)]
        )
        gains = small_all[:, router_rows:].reshape(devices, -1)
        head_gains = gains[:, 2 * rows : gain_count].reshape(devices, 2, head_part)
        values = block_hidden.astype(F32)
        scale = lax.rsqrt(jnp.mean(values * values, axis=-1, keepdims=True) + EPS)
        full_in = gains[:, :rows].reshape(MODEL_WIDTH).astype(F32)
        return (
            (values * scale * full_in).astype(BF),
            small_all[:, :router_rows].reshape(MODEL_WIDTH, experts),
            full_in,
            gains[:, rows : 2 * rows].reshape(MODEL_WIDTH).astype(F32),
            head_gains.swapaxes(0, 1).reshape(2, HEAD_SIZE).astype(F32),
        )

    def make_tables(pairs):
        pairs = pairs.astype(F32).reshape(planes, 4, 3, TOP, tokens)
        pairs = links.turned_line(pairs)
        near = [lax.dynamic_index_in_dim(pairs, links.p ^ k, 1, keepdims=False) for k in range(4)]
        return slot_tables(ids, jnp.stack(near, axis=1), capacity, experts)

    exchange_task = spread(hold(1))
    qkv_task = spread(gather_qkv())

    def gather_hidden():
        (value,) = yield from hold(1, hidden)
        return (yield from links.head_gather(value))

    hidden_task = spread(gather_hidden())
    small_task = spread(gather_small())

    aligned = capacity % 8 == 0

    def choose(piece, step, backs=()):
        found = choose_rows(tables["send"][step], piece, 4 if aligned else 1, as_blocks(backs))
        return found if aligned else by_place(found[0])

    def by_place(slot_rows):
        return [slot_rows[k * capacity : (k + 1) * capacity] for k in range(4)]

    def as_blocks(blocks):
        return blocks if aligned or not blocks else [jnp.concatenate(blocks, axis=0)]

    def collect(blocks, step, width, more=None, kind=BF):
        return collect_rows(tables["back"][step], as_blocks(blocks), width, more, kind)

    def in_places(own, came):
        return [own, came[0], came[1], came[2]]

    def to_places(blocks):
        return [(links.places[k], (blocks[k],)) for k in (1, 2, 3)]

    def gather_upstream():
        pieces, out = [cotangent], []
        yield from hold(2)
        found = yield from work(make_tables, tables["pairs"])
        tables["send"], tables["back"], tables["chooser"] = found
        plan = [(1, True, 0)] + [(0, s < planes - 1, s) for s in range(1, planes)]
        for idle, hop, step in plan:
            yield from hold(idle)
            asks = [(links.onward, (pieces[-1],))] if hop else []
            if step is not None:
                blocks = choose(pieces[step], step)
                asks += to_places(blocks)
            came = yield asks
            if hop:
                pieces.append(came[0])
            if step is not None:
                out.append(jnp.concatenate([blocks[0]] + came[-3:], axis=0))
        return out

    upstream_task = spread(gather_upstream())

    head_rows = w_out.shape[0]
    if links.square:
        pairs_of = [(g, i) for g in range(2) for i in range(experts)]
        line = lambda i: i & 3 | (i >> 3 & 1) << 2 | (i >> 2 & 1) << 3
        swap_line = [(g * experts + i, g * experts + line(i)) for g, i in pairs_of]
        swap_core = [
            (g * experts + i, (i >> 1 & 1) * experts + (i & 13 | g << 1)) for g, i in pairs_of
        ]
        there = back = (swap_line, swap_core)
    else:
        to_block = [
            (b * 2 * planes + links.row_block(g, a), g * experts + links.device(a, b))
            for g in range(2)
            for a in range(planes)
            for b in range(4)
        ]
        there = (to_block, None)
        back = ([(to, of) for of, to in to_block], None)

    def moved(value, pairs_of):
        return value if pairs_of is None else lax.ppermute(value, ("dp", "expert"), pairs_of)

    def gather_out():
        pieces = yield from links.block_gather(rounds.values[move_task], (1, 0))
        pieces = jnp.concatenate(pieces, axis=0)
        (others,) = yield [(links.twin, (pieces,))]
        return pieces, others

    def move_out():
        value = yield from work(lambda value: moved(value, there[0]), w_out)
        return (yield from work(lambda value: moved(value, there[1]), value))

    move_task = spread(move_out())

    device_of = jnp.stack(
        [links.device(links.block(r), links.b ^ k) for r in range(planes) for k in range(4)]
    )
    starts = jnp.concatenate([(links.g ^ t) * experts + device_of for t in range(2)]) * rows
    all_slots = slots.reshape(experts, tokens)[device_of].reshape(experts * tokens)
    _, position = places(all_slots[:block_tokens], lengths[0])
    cosine, sine = rotary_tables(position)
    high = all_slots[:block_tokens]
    low = high - position

    rounds.until(exchange_task)
    found, block_hidden, qkv_pieces, _ = rounds.loosely(
        small_task, hidden_task, qkv_task, move_task, alone=True
    )
    out_task = spread(gather_out())
    normalized, full_router, full_in, full_mid, head_gains = found
    w_qkv, projected, turned = rounds.run(
        work(
            lambda *args: project(rows, *args),
            starts,
            normalized,
            cosine,
            sine,
            head_gains,
            *qkv_pieces,
        )
    )
    keys_values = jnp.concatenate(
        rounds.run(links.block_gather_short(turned[:, QW:])), axis=0
    )
    keys_turned = keys_values[:, :HEAD_SIZE].T
    values_turned = keys_values[:, HEAD_SIZE:].T
    place_column = all_slots[:, None]
    low, high = low[None, :], high[None, :]

    def part_of(array, part, parts):
        width = array.shape[1] // parts
        return array[:, part * width : (part + 1) * width]

    def forward_part(query_rows):
        return attention_forward(query_rows, keys_values, values_turned, place_column, low, high)

    bounds = [0, PER_KV // 2, PER_KV]
    attended = [
        rounds.run(work(forward_part, turned[:, low_head * HEAD_SIZE : high_head * HEAD_SIZE]))
        for low_head, high_head in zip(bounds, bounds[1:])
    ]
    block_out = rounds.until(out_task)
    if head_rows == HEAD_SIZE:
        order_of = [
            links.row_block(links.g ^ t, links.block(r)) for t in range(2) for r in range(planes)
        ]
        order_of = jnp.stack(order_of).astype(jnp.int32)
    else:
        attended = jnp.concatenate(attended, axis=1)
        attended = [
            lax.dynamic_slice_in_dim(
                attended, links.row_block(links.g ^ t, links.block(r)) * head_rows, head_rows, 1
            )
            for t in range(2)
            for r in range(planes)
        ]
        attended = [jnp.concatenate(attended, axis=1)]
        order_of = jnp.arange(PER_KV, dtype=jnp.int32)
    branch, attended = rounds.run(
        work(lambda *parts: output_projection(order_of, parts, *block_out), *attended)
    )
    branch = rounds.loosely(spread(links.head_scatter(branch)))
    x_float = hidden.astype(F32)
    x_one = x_float + branch
    norm_two, norm_two_back = jax.vjp(rms_scale, x_one, full_mid)
    xn_two = norm_two.astype(BF)

    own_chooser = jnp.any(routes[:, :, None] == expert_numbers, axis=1)

    def masked_softmax(logits, chooser):
        top = jnp.max(jnp.where(chooser, logits, MASKED), axis=-1, keepdims=True)
        exponent = jnp.where(chooser, jnp.exp(jnp.where(chooser, logits - top, 0.0)), 0.0)
        total = jnp.sum(exponent, axis=-1, keepdims=True)
        return exponent / jnp.where(total > 0.0, total, 1.0)

    upstream_slots = rounds.until(upstream_task)
    me = links.index.astype(jnp.int32)[None]
    made = []

    def expert_step(step, *rows_in):
        found = expert_rows(
            me,
            as_blocks(list(rows_in)),
            upstream_slots[step],
            tables["chooser"][step],
            full_router,
            gate_full,
            up_full,
            down_full,
        )
        if aligned:
            return (found[:4], found[4:8], found[8:])
        return (by_place(found[0]), by_place(found[1]), found[2:])

    def return_mixture():
        def add(step, came, back, kind=BF):
            blocks = in_places(made[step][1][0], back)
            return collect(blocks, step, MODEL_WIDTH, came, kind)

        back = yield to_places(made[1][1])
        total = add(1, None, back)
        yield from hold(2)
        came, *back = yield [(links.onward, (total,))] + to_places(made[2][1])
        total = add(2, came, back)
        for step in range(3, planes):
            came, *back = yield [(links.onward, (total,))] + to_places(made[step][1])
            total = add(step, came, back)
        came, *back = yield [(links.onward, (total,))] + to_places(made[0][1])
        return add(0, came, back, F32)

    def experts_there_and_back():
        piece, ready, own_plane, total = xn_two, None, None, None
        wide = MODEL_WIDTH + lanes
        for step in range(planes + 3):
            asks = []
            back = made[step - 2][0] if 2 <= step < planes + 2 else []
            blocks = back
            if step < planes:
                blocks = choose(piece, step, back)
            if blocks:
                asks += to_places(blocks)
            if step < planes - 1:
                asks += [(links.onward, (piece,))]
            if step >= 4:
                asks += [(links.onward, (total,))]
            if 1 <= step <= planes:
                asks += [(lambda *v, s=step - 1: expert_step(s, *v), tuple(ready))]
            if step == planes + 2:
                tables["mixture"] = spread(return_mixture())
            came = yield asks
            if blocks:
                ready, came = in_places(blocks[0], came[:3]), came[3:]
            if step < planes - 1:
                piece, came = came[0], came[1:]
            if step >= 4:
                hop, came = came[0], came[1:]
            if 1 <= step <= planes:
                made.append(came[0])
            if step == 2:
                own_plane = collect(ready, 0, wide, None, F32)
            elif step == 3:
                total = collect(ready, 1, wide)
            elif step >= 4 and step < planes + 2:
                total = collect(ready, step - 2, wide, hop)
        return own_plane + hop.astype(F32)

    moe_grad = rounds.run(experts_there_and_back())
    gate_grads = moe_grad[:, MODEL_WIDTH : MODEL_WIDTH + experts]
    moe_grad = moe_grad[:, :MODEL_WIDTH]
    stacked = lambda place: jnp.concatenate([piece[2][place] for piece in made], axis=0)

    def by_rows(rows_in, grads_in):
        return jnp.einsum("rd,rf->df", rows_in, grads_in, preferred_element_type=F32)

    half_width = MODEL_WIDTH // 2

    def half_of(array, which):
        return lax.dynamic_slice_in_dim(array, which * half_width, half_width, 1)

    def gate_up_gradient(place):
        rows_in, grads_in = stacked(0), stacked(place)
        return links.twin_scatter(
            by_rows,
            (half_of(rows_in, links.g), grads_in),
            (half_of(rows_in, 1 - links.g), grads_in),
            idle=5,
        )

    def down_gradient():
        rows_in, grads_in = stacked(1), stacked(2)
        return links.twin_scatter(
            by_rows,
            (rows_in, half_of(grads_in, links.g)),
            (rows_in, half_of(grads_in, 1 - links.g)),
            idle=2,
        )

    gate_task = spread(gate_up_gradient(3))
    up_task = spread(later(1, gate_up_gradient(4)))
    down_task = spread(later(5, down_gradient()))
    own_logits = jnp.dot(xn_two, full_router, preferred_element_type=F32)
    own_probs = masked_softmax(own_logits, own_chooser)

    upstream = cotangent.astype(F32)
    chosen_grad = own_probs * (
        gate_grads - jnp.sum(own_probs * gate_grads, axis=-1, keepdims=True)
    )
    logit_grad = chosen_grad.astype(BF)
    xn_two_grad = moe_grad + jnp.dot(logit_grad, full_router.T, preferred_element_type=F32)
    x_one_norm_grad, grad_mid = norm_two_back(xn_two_grad)
    x_one_grad = upstream + x_one_norm_grad
    branch_grad = x_one_grad.astype(BF)

    block_grad = rounds.loosely(spread(links.head_gather(branch_grad)))

    def head_gradients(block_grad):
        grad = [
            jnp.einsum("td,hd->th", block_grad, part, preferred_element_type=F32).astype(BF)
            for part in block_out
        ]
        grad = jnp.concatenate(grad, axis=1)
        parts = []
        where = {links.row_block(g, a): (g, a) for g in range(2) for a in range(planes)}
        for head in range(2 * planes):
            g, a = where[head]
            at = ((links.g ^ g) * planes + links.block(a)) * head_rows
            parts.append(lax.dynamic_slice_in_dim(grad, at, head_rows, 1))
        return jnp.concatenate(parts, axis=1)

    heads_task = spread(work(head_gradients, block_grad))

    def scatter_out():
        half = QW // 2
        grad = yield from links.twin_scatter(
            lambda rows_in, grads_in: jnp.einsum(
                "th,td->hd", rows_in, grads_in, preferred_element_type=F32
            ),
            (attended[:, :half], block_grad),
            (attended[:, half:], block_grad),
            now=True,
        )
        grad = grad.astype(BF)
        blocks = [grad[r * head_rows : (r + 1) * head_rows] for r in range(planes)]
        grad = yield from links.block_scatter(blocks, split=True)
        (grad,) = yield from hold(2, grad.astype(BF))
        grad = yield from work(lambda value: moved(value, back[1]), grad)
        (grad,) = yield from hold(1, grad)
        grad = yield from work(lambda value: moved(value, back[0]), grad)
        return grad.astype(F32)

    grad_out_task = spread(scatter_out())

    def owners_blocks(grad):
        blocks = []
        for r in range(planes):
            owners = [links.device(links.block(r), links.b ^ k) for k in range(4)]
            parts = [lax.dynamic_slice_in_dim(grad, owner * rows, rows, 0) for owner in owners]
            blocks.append(jnp.concatenate(parts, axis=0))
        return blocks

    def half_rows(array, which):
        return lax.dynamic_slice_in_dim(array, which * (MODEL_WIDTH // 2), MODEL_WIDTH // 2, 0)

    def query_gradient(grads_in, extra):
        def make(which):
            grad = by_rows(half_of(normalized, which), grads_in)
            if extra is not None:
                grad = jnp.concatenate([grad, half_rows(extra, which)], axis=1)
            return grad

        grad = yield from links.twin_scatter(make, (links.g,), (1 - links.g,))
        grad = yield from links.block_scatter(owners_blocks(grad.astype(BF)))
        return grad.astype(BF)

    def exchange_owners(grad):
        grad = grad.reshape(4, rows, grad.shape[1])
        return links.exchange(links.heads, [grad[k] for k in range(4)])

    def key_value_gradient(key_value_grad, proj_grad):
        sums = jnp.concatenate([grad_qgain, grad_kgain]).reshape(2, devices, head_part)
        sums = jnp.pad(sums, ((0, 0), (0, 0), (0, rows - head_part))).reshape(2, MODEL_WIDTH).T
        sums = jnp.pad(sums, ((0, 0), (0, lanes - sums.shape[1])))

        def half(which):
            grad = by_rows(half_of(normalized, which), key_value_grad)
            return jnp.concatenate([grad, half_rows(sums, which)], axis=1)

        came, xn_one_grad = yield [
            (links.twin, (half(1 - links.g).astype(BF),)),
            (input_gradient, (proj_grad, w_qkv)),
        ]
        tables["scatter"] = spread(links.head_scatter(xn_one_grad))
        grad = (half(links.g) + came.astype(F32)).astype(BF)
        grad = yield from links.block_scatter(owners_blocks(grad))
        return grad.astype(BF)

    attended_grad = rounds.until(heads_task)
    grad_router = jnp.dot(xn_two.T, logit_grad, preferred_element_type=F32)
    first = jnp.concatenate([grad_router, grad_mid[:, None]], axis=1)
    first = jnp.pad(first, ((0, 0), (0, lanes - first.shape[1])))
    query_low_grads, query_tasks, key_terms, grad_qgain = [], [], None, None
    parts = 2
    for part in range(parts):
        got = rounds.run(
            work(
                lambda *args: attention_backward(
                    *args,
                    keys_values,
                    keys_turned,
                    place_column,
                    low,
                    high,
                    cosine,
                    sine,
                    head_gains[0:1],
                ),
                part_of(turned[:, :QW], part, parts),
                part_of(attended_grad, part, parts),
                part_of(projected[:, :QW], part, parts),
            )
        )
        query_low_grads.append(got[0])
        key_terms = got[1] if part == 0 else key_terms + got[1]
        grad_qgain = got[2] if part == 0 else grad_qgain + got[2]
        query_tasks.append(spread(query_gradient(got[0], None if part else first)))
    key_terms = rounds.run(
        links.block_scatter(
            [key_terms[r * block_tokens : (r + 1) * block_tokens] for r in range(planes)]
        )
    )

    key_proj_grad, grad_kgain = unturn(
        key_terms[:, :HEAD_SIZE],
        projected[:, QW : QW + HEAD_SIZE],
        cosine,
        sine,
        head_gains[1:2],
    )
    key_value_grad = jnp.concatenate([key_proj_grad, key_terms[:, HEAD_SIZE:].astype(BF)], axis=1)
    proj_grad = jnp.concatenate(query_low_grads + [key_value_grad], axis=1)
    key_value_task = spread(key_value_gradient(key_value_grad, proj_grad))
    one, two, three = rounds.until(*query_tasks, key_value_task)
    xn_one_grad = rounds.until(tables["scatter"])
    query_task = spread(exchange_owners(jnp.concatenate([one, two, three], axis=1)))
    _, norm_one_back = jax.vjp(lambda values: rms_scale(values, full_in), x_float)
    (x_norm_grad,) = norm_one_back(xn_one_grad)
    input_grad = (x_one_grad + x_norm_grad).astype(BF)

    grad_gate, grad_up, grad_down, mixture, grad_out, owned = rounds.until(
        gate_task, up_task, down_task, tables["mixture"], grad_out_task, query_task
    )
    result = (x_one + mixture).astype(BF)
    half = QW // 2
    at = QW + lanes
    first = sum(block[:, half : half + lanes].astype(F32) for block in owned)
    last = sum(block[:, at + 2 * HEAD_SIZE :].astype(F32) for block in owned)
    owned = [block.astype(F32) for block in links.natural(owned, links.b)]
    grad_query = jnp.concatenate(
        [part for block in owned for part in (block[:, :half], block[:, half + lanes : at])], axis=1
    )
    grad_key = jnp.concatenate([block[:, at : at + HEAD_SIZE] for block in owned], axis=1)
    grad_value = jnp.concatenate(
        [block[:, at + HEAD_SIZE : at + 2 * HEAD_SIZE] for block in owned], axis=1
    )
    grad_router, grad_mid = first[:, :experts], first[:, experts]
    grad_qgain, grad_kgain = last[:head_part, 0], last[:head_part, 1]
    grad_in = (
        jnp.sum(w_query.astype(F32) * grad_query, axis=1)
        + jnp.sum(key_projection_weight.astype(F32) * grad_key, axis=1)
        + jnp.sum(value_projection_weight.astype(F32) * grad_value, axis=1)
    ) / gain_in.astype(F32)

    return (
        result,
        input_grad,
        grad_in,
        grad_query,
        grad_key,
        grad_value,
        grad_qgain,
        grad_kgain,
        grad_out,
        grad_mid,
        grad_router,
        grad_gate[None],
        grad_up[None],
        grad_down[None],
    )


def solution(mesh):
    every = ("dp", "expert")
    in_specs = (
        P(every, None),
        P("dp", None),
        P("dp"),
        P(every, None),
        P(every, None),
        P(every),
        P(every, None),
        P(every, None),
        P(every, None),
        P(every),
        P(every),
        P(every, None),
        P(every),
        P(every, None),
        P("expert", "dp", None),
        P("expert", "dp", None),
        P("expert", None, "dp"),
        P(every, None),
    )
    out_specs = (
        P(every, None),
        P(every, None),
        P(every),
        P(every, None),
        P(every, None),
        P(every, None),
        P(every),
        P(every),
        P(every, None),
        P(every),
        P(every, None),
        P("expert", "dp", None),
        P("expert", "dp", None),
        P("expert", None, "dp"),
    )
    return jax.shard_map(body, mesh=mesh, in_specs=in_specs, out_specs=out_specs, check_vma=False)
```

```python
import jax
import jax.numpy as jnp
from jax import lax
from jax.experimental import pallas as pl
from jax.experimental.pallas import tpu as pltpu
from jax.sharding import PartitionSpec as P

MODEL_WIDTH = 2048
QUERY_HEADS = 32
KEY_VALUE_HEADS = 4
HEAD_SIZE = 128
TOP = 8
PER_KV = QUERY_HEADS // KEY_VALUE_HEADS
QW = PER_KV * HEAD_SIZE

EPS = 1e-06
THETA = 1000000.0
MASKED = -1e30
KEY_STEP = 1024
BF = jnp.bfloat16
F32 = jnp.float32


def rms_scale(values, scaling):
    return values * lax.rsqrt(jnp.mean(values * values, axis=-1, keepdims=True) + EPS) * scaling


def rotary_tables(position):
    half = HEAD_SIZE // 2
    index_float = jnp.arange(half, dtype=jnp.float32)
    freq = jnp.power(jnp.float32(THETA), -2.0 * index_float / HEAD_SIZE)
    angle = position.astype(jnp.float32)[:, None] * freq[None, :]
    cosine, sine = jnp.cos(angle), jnp.sin(angle)
    return (
        jnp.concatenate([cosine, cosine], axis=-1),
        jnp.concatenate([-sine, sine], axis=-1),
    )


def stack_kernel(rows, *refs):
    *block_refs, out_ref = refs
    blocks = [ref[...].astype(F32) for ref in block_refs]
    stack = [block[:rows] for block in blocks] + [block[rows:] for block in blocks]
    out_ref[...] = jnp.concatenate(stack, axis=0).astype(BF)


def stack_rows(blocks, rows):
    height, width = blocks[0].shape
    return pl.pallas_call(
        lambda *refs: stack_kernel(rows, *refs),
        out_shape=jax.ShapeDtypeStruct((height * len(blocks), width), BF),
    )(*blocks)


def project_kernel(starts_ref, x_ref, cos_ref, sin_ref, gains_ref, *refs):
    pieces, (w_ref, proj_ref, turned_ref) = refs[:-3], refs[-3:]
    last = pl.program_id(0) == pl.num_programs(0) - 1
    rows = pieces[0].shape[0] // 4
    for number, piece in enumerate(pieces):
        for k in range(4):
            at = pl.multiple_of(starts_ref[number * 4 + k], rows)
            w_ref[pl.ds(at, rows), :] = piece[k * rows : (k + 1) * rows, :]
    projected = jnp.dot(x_ref[...], w_ref[...], preferred_element_type=F32)
    proj_ref[...] = projected

    def turn(values, gain):
        scaled = (
            values * lax.rsqrt(jnp.mean(values * values, axis=-1, keepdims=True) + EPS) * gain
        )
        swapped = pltpu.roll(scaled, HEAD_SIZE // 2, 1)
        return scaled * cos_ref[...] + swapped * sin_ref[...]

    gain_q, gain_k = gains_ref[0:1], gains_ref[1:2]
    first, second = projected[:, :HEAD_SIZE], projected[:, HEAD_SIZE:]
    turned_ref[:, :HEAD_SIZE] = turn(first, jnp.where(last, gain_k, gain_q)).astype(BF)
    turned_ref[:, HEAD_SIZE:] = jnp.where(last, second, turn(second, gain_q)).astype(BF)


def project(rows, starts, rows_in, cosine, sine, gains, *pieces):
    count, width = rows_in.shape
    height, columns = 4 * rows, pieces[0].shape[1]
    step = 2 * HEAD_SIZE
    whole = lambda array: pl.BlockSpec(array.shape, lambda i: (0, 0))
    strip = lambda height: pl.BlockSpec((height, step), lambda i: (0, i))
    return pl.pallas_call(
        project_kernel,
        grid=(columns // step,),
        in_specs=[pl.BlockSpec(memory_space=pltpu.SMEM)]
        + [whole(rows_in), whole(cosine), whole(sine), whole(gains)]
        + [strip(height)] * len(pieces),
        out_specs=[strip(width), strip(count), strip(count)],
        out_shape=[
            jax.ShapeDtypeStruct((width, columns), BF),
            jax.ShapeDtypeStruct((count, columns), F32),
            jax.ShapeDtypeStruct((count, columns), BF),
        ],
        cost_estimate=pl.CostEstimate(
            flops=2 * count * width * columns,
            bytes_accessed=2 * (count + columns) * width,
            transcendentals=0,
        ),
        compiler_params=pltpu.CompilerParams(vmem_limit_bytes=60 * 2**20),
    )(starts, rows_in, cosine, sine, gains, *pieces)


def unturned(grad, values, cosine, sine, gain):
    grad = grad * cosine + pltpu.roll(grad * sine, HEAD_SIZE // 2, 1)
    scale = lax.rsqrt(jnp.mean(values * values, axis=-1, keepdims=True) + EPS)
    gain_grad = jnp.sum(grad * values * scale, axis=0, keepdims=True)
    grad = grad * gain
    inner = jnp.mean(grad * values, axis=-1, keepdims=True)
    return (scale * grad - values * (scale * scale * scale * inner)).astype(BF), gain_grad


def unturn_kernel(grad_ref, proj_ref, cos_ref, sin_ref, gain_ref, out_ref, gain_grad_ref):
    out_ref[...], gain_grad_ref[...] = unturned(
        grad_ref[...], proj_ref[...], cos_ref[...], sin_ref[...], gain_ref[...]
    )


def unturn(grad, projected, cosine, sine, gain):
    return pl.pallas_call(
        unturn_kernel,
        out_shape=[
            jax.ShapeDtypeStruct(grad.shape, BF),
            jax.ShapeDtypeStruct(gain.shape, F32),
        ],
    )(grad, projected, cosine, sine, gain)


def input_kernel(grad_ref, w_ref, out_ref):
    dims = (((1,), (1,)), ((), ()))
    out_ref[...] = lax.dot_general(grad_ref[...], w_ref[...], dims, preferred_element_type=F32)


def input_gradient(proj_grad, weights):
    count, columns = proj_grad.shape
    width = weights.shape[0]
    step = 256
    return pl.pallas_call(
        input_kernel,
        grid=(width // step,),
        in_specs=[
            pl.BlockSpec((count, columns), lambda i: (0, 0)),
            pl.BlockSpec((step, columns), lambda i: (i, 0)),
        ],
        out_specs=pl.BlockSpec((count, step), lambda i: (0, i)),
        out_shape=jax.ShapeDtypeStruct((count, width), F32),
        cost_estimate=pl.CostEstimate(
            flops=2 * count * width * columns,
            bytes_accessed=6 * (count + columns) * width,
            transcendentals=0,
        ),
        compiler_params=pltpu.CompilerParams(vmem_limit_bytes=24 * 2**20),
    )(proj_grad, weights)


def output_kernel(order_ref, *refs):
    *part_refs, own_ref, other_ref, out_ref, rows_ref, natural_ref = refs
    half = own_ref.shape[0]

    @pl.when(pl.program_id(0) == 0)
    def _():
        at = 0
        for part_ref in part_refs:
            width = part_ref.shape[1]
            natural_ref[:, at : at + width] = part_ref[...]
            at += width
        for head in range(at // HEAD_SIZE):
            start = pl.multiple_of(order_ref[head] * HEAD_SIZE, HEAD_SIZE)
            here = slice(head * HEAD_SIZE, (head + 1) * HEAD_SIZE)
            rows_ref[:, here] = natural_ref[:, pl.ds(start, HEAD_SIZE)]

    out_ref[...] = jnp.dot(
        rows_ref[:, :half], own_ref[...], preferred_element_type=F32
    ) + jnp.dot(rows_ref[:, half:], other_ref[...], preferred_element_type=F32)


def output_projection(order, parts, own, other):
    count = parts[0].shape[0]
    half, width = own.shape
    columns = 2 * half
    step = 256
    strip = lambda height: pl.BlockSpec((height, step), lambda i: (0, i))
    whole = lambda shape: pl.BlockSpec(shape, lambda i: (0, 0))
    return pl.pallas_call(
        output_kernel,
        grid=(width // step,),
        in_specs=[pl.BlockSpec(memory_space=pltpu.SMEM)]
        + [whole(part.shape) for part in parts]
        + [strip(half), strip(half)],
        out_specs=[strip(count), whole((count, columns))],
        out_shape=[
            jax.ShapeDtypeStruct((count, width), F32),
            jax.ShapeDtypeStruct((count, columns), BF),
        ],
        scratch_shapes=[pltpu.VMEM((count, columns), BF)],
        cost_estimate=pl.CostEstimate(
            flops=2 * count * width * columns,
            bytes_accessed=4 * (count + columns) * width,
            transcendentals=0,
        ),
        compiler_params=pltpu.CompilerParams(vmem_limit_bytes=24 * 2**20),
    )(order, *parts, own, other)


def forward_kernel(q_ref, kv_ref, vt_ref, place_ref, low_ref, high_ref, out_ref, p_ref, sum_ref):
    count, queries = p_ref.shape
    step = min(KEY_STEP, count)
    part = lambda i: pl.ds(pl.multiple_of(i * step, step), step)
    q, low, high = q_ref[...], low_ref[...], high_ref[...]

    def score(i, top):
        place = place_ref[part(i), :]
        seen = (place >= low) & (place <= high)
        scores = lax.dot_general(
            kv_ref[part(i), :HEAD_SIZE], q, (((1,), (1,)), ((), ())), preferred_element_type=F32
        )
        scores = jnp.where(seen, scores * HEAD_SIZE**-0.5, MASKED)
        p_ref[part(i), :] = scores
        return jnp.maximum(top, jnp.max(scores, axis=0, keepdims=True))

    top = lax.fori_loop(0, count // step, score, jnp.full((1, queries), MASKED, F32))

    def lift(i, total):
        exponent = jnp.exp(p_ref[part(i), :] - top)
        p_ref[part(i), :] = exponent
        return total + jnp.sum(exponent, axis=0, keepdims=True)

    total = lax.fori_loop(0, count // step, lift, jnp.zeros((1, queries), F32))
    share = 1.0 / total
    sum_ref[...] = jnp.zeros_like(sum_ref)

    def mix(i, carry):
        probs = (p_ref[part(i), :] * share).astype(BF)
        sum_ref[...] += jnp.dot(vt_ref[:, part(i)], probs, preferred_element_type=F32)
        return carry

    lax.fori_loop(0, count // step, mix, 0)
    out_ref[...] = sum_ref[...].T.astype(BF)


def attention_blocks(rows, count):
    step = min(rows, 512 * 2048 // count)
    whole = lambda array: pl.BlockSpec(array.shape, lambda i, j: (0, 0))
    head = pl.BlockSpec((step, HEAD_SIZE), lambda i, j: (j, i))
    along = pl.BlockSpec((1, step), lambda i, j: (0, j))
    down = pl.BlockSpec((step, HEAD_SIZE), lambda i, j: (j, 0))
    limit = (32 if count <= 2048 else 60) * 2**20
    return step, whole, head, along, down, limit


def attention_forward(q, keys_values, values_turned, place, low, high):
    rows, columns = q.shape
    count = keys_values.shape[0]
    step, whole, head, along, _, limit = attention_blocks(rows, count)
    return pl.pallas_call(
        forward_kernel,
        grid=(columns // HEAD_SIZE, rows // step),
        in_specs=[head, whole(keys_values), whole(values_turned), whole(place), along, along],
        out_specs=head,
        out_shape=jax.ShapeDtypeStruct(q.shape, BF),
        scratch_shapes=[pltpu.VMEM((count, step), F32), pltpu.VMEM((HEAD_SIZE, step), F32)],
        cost_estimate=pl.CostEstimate(
            flops=8 * rows * columns * count, bytes_accessed=4 * rows * columns, transcendentals=0
        ),
        compiler_params=pltpu.CompilerParams(vmem_limit_bytes=limit),
    )(q, keys_values, values_turned, place, low, high)


def backward_kernel(
    q_ref, grad_ref, proj_ref, kv_ref, kt_ref, place_ref, low_ref, high_ref, cos_ref, sin_ref,
    gain_ref, out_ref, dkv_ref, gain_grad_ref, p_ref, dp_ref, dq_ref,
):
    @pl.when((pl.program_id(0) == 0) & (pl.program_id(1) == 0))
    def _():
        dkv_ref[...] = jnp.zeros_like(dkv_ref)
        gain_grad_ref[...] = jnp.zeros_like(gain_grad_ref)

    count, queries = p_ref.shape
    step = min(KEY_STEP, count)
    part = lambda i: pl.ds(pl.multiple_of(i * step, step), step)
    scale = HEAD_SIZE**-0.5
    q, grad = q_ref[...], grad_ref[...]
    low, high = low_ref[...], high_ref[...]

    def across(left, right):
        dims = (((1,), (1,)), ((), ()))
        return lax.dot_general(left, right, dims, preferred_element_type=F32)

    def score(i, top):
        place = place_ref[part(i), :]
        seen = (place >= low) & (place <= high)
        scores = jnp.where(seen, across(kv_ref[part(i), :HEAD_SIZE], q) * scale, MASKED)
        p_ref[part(i), :] = scores
        return jnp.maximum(top, jnp.max(scores, axis=0, keepdims=True))

    top = lax.fori_loop(0, count // step, score, jnp.full((1, queries), MASKED, F32))

    def lift(i, sums):
        total, inner = sums
        exponent = jnp.exp(p_ref[part(i), :] - top)
        p_ref[part(i), :] = exponent
        total = total + jnp.sum(exponent, axis=0, keepdims=True)
        prob_grad = across(kv_ref[part(i), HEAD_SIZE:], grad)
        dp_ref[part(i), :] = prob_grad
        return total, inner + jnp.sum(exponent * prob_grad, axis=0, keepdims=True)

    nothing = jnp.zeros((1, queries), F32)
    total, inner = lax.fori_loop(0, count // step, lift, (nothing, nothing))
    share = 1.0 / total
    inner = inner * share
    dq_ref[...] = jnp.zeros_like(dq_ref)

    def back(i, carry):
        probs = p_ref[part(i), :] * share
        score_grad = (probs * (dp_ref[part(i), :] - inner)).astype(BF)
        dkv_ref[part(i), HEAD_SIZE:] += jnp.dot(
            probs.astype(BF), grad, preferred_element_type=F32
        )
        dkv_ref[part(i), :HEAD_SIZE] += (
            jnp.dot(score_grad, q, preferred_element_type=F32) * scale
        )
        dq_ref[...] += jnp.dot(kt_ref[:, part(i)], score_grad, preferred_element_type=F32)
        return carry

    lax.fori_loop(0, count // step, back, 0)
    out_ref[...], gain_grad = unturned(
        dq_ref[...].T * scale, proj_ref[...], cos_ref[...], sin_ref[...], gain_ref[...]
    )
    gain_grad_ref[...] += gain_grad


def attention_backward(
    q, grad, projected, keys_values, keys_turned, place, low, high, cosine, sine, gain
):
    rows, columns = q.shape
    count = keys_values.shape[0]
    step, whole, head, along, down, limit = attention_blocks(rows, count)
    return pl.pallas_call(
        backward_kernel,
        grid=(columns // HEAD_SIZE, rows // step),
        in_specs=[head, head, head, whole(keys_values), whole(keys_turned), whole(place)]
        + [along, along, down, down, whole(gain)],
        out_specs=[head, whole(keys_values), whole(gain)],
        out_shape=[
            jax.ShapeDtypeStruct(q.shape, BF),
            jax.ShapeDtypeStruct(keys_values.shape, F32),
            jax.ShapeDtypeStruct(gain.shape, F32),
        ],
        scratch_shapes=[pltpu.VMEM((count, step), F32)] * 2
        + [pltpu.VMEM((HEAD_SIZE, step), F32)],
        cost_estimate=pl.CostEstimate(
            flops=10 * rows * columns * count, bytes_accessed=8 * rows * columns, transcendentals=0
        ),
        compiler_params=pltpu.CompilerParams(vmem_limit_bytes=60 * 2**20),
    )(q, grad, projected, keys_values, keys_turned, place, low, high, cosine, sine, gain)


def pack_kernel(*refs):
    *array_refs, out_0, out_1, out_2, out_3 = refs
    rows = out_0.shape[0]
    for k, out_ref in enumerate((out_0, out_1, out_2, out_3)):
        at = 0
        for array_ref in array_refs:
            width = array_ref.shape[1]
            out_ref[:, at : at + width] = array_ref[k * rows : (k + 1) * rows, :]
            at += width


def pack_rows(*arrays):
    rows = arrays[0].shape[0] // 4
    width = sum(array.shape[1] for array in arrays)
    return pl.pallas_call(
        pack_kernel,
        out_shape=[jax.ShapeDtypeStruct((rows, width), BF)] * 4,
    )(*arrays)


def finish_kernel(ids_ref, b0, b1, b2, b3, wq_ref, wk_ref, wv_ref, *refs):
    gq_ref, gk_ref, gv_ref, first_ref, last_ref, inner_ref = refs
    half = QW // 2
    lanes = first_ref.shape[1]
    at = QW + lanes
    first = last = 0.0
    for k, ref in enumerate((b0, b1, b2, b3)):
        head = ids_ref[0] ^ k
        block = ref[...].astype(F32)
        wide = pl.multiple_of(head * QW, QW)
        thin = pl.multiple_of(head * HEAD_SIZE, HEAD_SIZE)
        gq_ref[:, pl.ds(wide, half)] = block[:, :half]
        gq_ref[:, pl.ds(wide + half, half)] = block[:, half + lanes : at]
        gk_ref[:, pl.ds(thin, HEAD_SIZE)] = block[:, at : at + HEAD_SIZE]
        gv_ref[:, pl.ds(thin, HEAD_SIZE)] = block[:, at + HEAD_SIZE : at + 2 * HEAD_SIZE]
        first = first + block[:, half : half + lanes]
        last = last + block[:, at + 2 * HEAD_SIZE :]
    first_ref[...] = first
    last_ref[...] = last
    inner = 0.0
    for w_ref, g_ref in ((wq_ref, gq_ref), (wk_ref, gk_ref), (wv_ref, gv_ref)):
        inner = inner + jnp.sum(w_ref[...].astype(F32) * g_ref[...], axis=1, keepdims=True)
    inner_ref[...] = jnp.broadcast_to(inner, inner_ref.shape)


def finish(b, blocks, *weights):
    rows = blocks[0].shape[0]
    sums = jax.ShapeDtypeStruct((rows, 128), F32)
    return pl.pallas_call(
        finish_kernel,
        in_specs=[pl.BlockSpec(memory_space=pltpu.SMEM)]
        + [pl.BlockSpec(memory_space=pltpu.VMEM)] * 7,
        out_shape=[jax.ShapeDtypeStruct(weight.shape, F32) for weight in weights] + [sums] * 3,
    )(b.astype(jnp.int32)[None], *blocks, *weights)


def choose_kernel(blocks, table_ref, piece_ref, *refs):
    chosen = jnp.dot(table_ref[...], piece_ref[...], preferred_element_type=F32)
    back_refs, out_refs = refs[:-blocks], refs[-blocks:]
    count = out_refs[0].shape[0]
    width = piece_ref.shape[1]
    for k, out_ref in enumerate(out_refs):
        part = chosen[k * count : (k + 1) * count].astype(BF)
        if back_refs:
            out_ref[:, :width] = part
            out_ref[:, width:] = back_refs[k][...]
        else:
            out_ref[...] = part


def choose_rows(table, piece, blocks, backs=()):
    width = piece.shape[1] + (backs[0].shape[1] if backs else 0)
    shape = (table.shape[0] // blocks, width)
    return pl.pallas_call(
        lambda *refs: choose_kernel(blocks, *refs),
        out_shape=[jax.ShapeDtypeStruct(shape, BF)] * blocks,
        compiler_params=pltpu.CompilerParams(vmem_limit_bytes=16 * 2**20),
    )(table, piece, *backs)


def collect_kernel(blocks, table_ref, *refs):
    width = refs[-1].shape[1]
    rows_in = [ref[:, ref.shape[1] - width :].astype(F32) for ref in refs[:blocks]]
    stack = jnp.concatenate(rows_in, axis=0).astype(BF)
    total = jnp.dot(table_ref[...], stack, preferred_element_type=F32)
    if len(refs) > blocks + 1:
        total = total + refs[blocks][...].astype(F32)
    refs[-1][...] = total.astype(refs[-1].dtype)


def collect_rows(table, blocks, width, more=None, kind=BF):
    extra = [] if more is None else [more]
    return pl.pallas_call(
        lambda *refs: collect_kernel(len(blocks), *refs),
        out_shape=jax.ShapeDtypeStruct((table.shape[0], width), kind),
        compiler_params=pltpu.CompilerParams(vmem_limit_bytes=24 * 2**20),
    )(table, *blocks, *extra)


def expert_kernel(blocks, me_ref, *refs):
    rows_refs, refs = refs[:blocks], refs[blocks:]
    upstream_ref, chooser_ref, router_ref, gate_ref, up_ref, down_ref = refs[:6]
    back_refs, mixed_refs = refs[6 : 6 + blocks], refs[6 + blocks : 6 + 2 * blocks]
    refs = refs[6 + 2 * blocks :]
    rows_ref, act_ref, out_grad_ref, gate_low_ref, up_low_ref = refs[:5]
    share_ref, returned_ref, pair_ref = refs[5:]
    step = pl.program_id(0)
    across = (((1,), (1,)), ((), ()))

    @pl.when(step == 0)
    def _():
        rows_in = jnp.concatenate([ref[...].astype(F32) for ref in rows_refs], axis=0).astype(BF)
        upstream = upstream_ref[...].astype(F32)
        logits = jnp.dot(rows_in, router_ref[...], preferred_element_type=F32)
        chosen = chooser_ref[...] > 0.0
        top = jnp.max(jnp.where(chosen, logits, MASKED), axis=1, keepdims=True)
        exponent = jnp.where(chosen, jnp.exp(jnp.where(chosen, logits - top, 0.0)), 0.0)
        total = jnp.sum(exponent, axis=1, keepdims=True)
        number = lax.broadcasted_iota(jnp.int32, exponent.shape, 1)
        mine = jnp.sum(jnp.where(number == me_ref[0], exponent, 0.0), axis=1, keepdims=True)
        share = mine / jnp.where(total > 0.0, total, 1.0)
        rows_ref[...] = rows_in
        out_grad_ref[...] = (share * upstream).astype(BF)
        share_ref[...] = jnp.broadcast_to(share, share_ref.shape)
        returned_ref[...] = jnp.zeros_like(returned_ref)
        pair_ref[...] = jnp.zeros_like(pair_ref)

    rows_in, out_grad = rows_ref[...], out_grad_ref[...]
    gate, up, down = gate_ref[...], up_ref[...], down_ref[...]
    gate_pre = jnp.dot(rows_in, gate, preferred_element_type=F32)
    up_pre = jnp.dot(rows_in, up, preferred_element_type=F32)
    act_grad = lax.dot_general(out_grad, down, across, preferred_element_type=F32)
    logistic = jax.nn.sigmoid(gate_pre)
    silu = gate_pre * logistic
    act = (silu * up_pre).astype(BF)
    gate_low = (act_grad * up_pre * logistic * (1.0 + gate_pre * (1.0 - logistic))).astype(BF)
    up_low = (act_grad * silu).astype(BF)
    act_ref[...], gate_low_ref[...], up_low_ref[...] = act, gate_low, up_low
    returned_ref[...] += jnp.dot(act, down, preferred_element_type=F32)
    pair_ref[...] += lax.dot_general(
        gate_low, gate, across, preferred_element_type=F32
    ) + lax.dot_general(up_low, up, across, preferred_element_type=F32)

    @pl.when(step == pl.num_programs(0) - 1)
    def _():
        returned = returned_ref[...].astype(BF).astype(F32)
        upstream = upstream_ref[...].astype(F32)
        gate_grad = jnp.sum(upstream * returned, axis=1, keepdims=True)
        mixed = share_ref[:, :1] * returned
        pair = pair_ref[...]
        count = rows_refs[0].shape[0]
        width = pair.shape[1]
        number = lax.broadcasted_iota(jnp.int32, share_ref.shape, 1)
        gates = jnp.where(number == me_ref[0], gate_grad, 0.0)
        for k in range(blocks):
            part = slice(k * count, (k + 1) * count)
            back_refs[k][:, :width] = pair[part].astype(BF)
            back_refs[k][:, width:] = gates[part].astype(BF)
            mixed_refs[k][...] = mixed[part].astype(BF)


def expert_rows(me, rows_in, upstream, chooser, router, gate, up, down):
    blocks = len(rows_in)
    slots, width = upstream.shape
    block = (slots // blocks, width)
    ff = gate.shape[1]
    step = 256
    lanes = 128
    whole = lambda shape: pl.BlockSpec(shape, lambda i: (0, 0))
    columns = lambda height: pl.BlockSpec((height, step), lambda i: (0, i))
    shape = jax.ShapeDtypeStruct
    out = [((block[0], width + lanes), BF)] * blocks + [(block, BF)] * blocks
    out_specs = [whole(dims) for dims, _ in out]
    out_specs += [whole((slots, width)), columns(slots), whole((slots, width))]
    out_specs += [columns(slots)] * 2
    out += [((slots, width), BF), ((slots, ff), BF), ((slots, width), BF)]
    out += [((slots, ff), BF)] * 2
    return pl.pallas_call(
        lambda *refs: expert_kernel(blocks, *refs),
        grid=(ff // step,),
        in_specs=[pl.BlockSpec(memory_space=pltpu.SMEM)]
        + [whole(block)] * blocks
        + [whole(upstream.shape), whole(chooser.shape), whole(router.shape)]
        + [columns(width), columns(width), pl.BlockSpec((step, width), lambda i: (i, 0))],
        out_specs=out_specs,
        out_shape=[shape(dims, kind) for dims, kind in out],
        scratch_shapes=[
            pltpu.VMEM((slots, lanes), F32),
            pltpu.VMEM((slots, width), F32),
            pltpu.VMEM((slots, width), F32),
        ],
        cost_estimate=pl.CostEstimate(
            flops=12 * slots * width * ff, bytes_accessed=6 * width * ff, transcendentals=0
        ),
        compiler_params=pltpu.CompilerParams(vmem_limit_bytes=44 * 2**20),
    )(me, *rows_in, upstream, chooser, router, gate, up, down)


def table_kernel(capacity, ids_ref, pairs_ref, send_ref, back_ref, chosen_ref):
    mine_a, mine_b = ids_ref[0], ids_ref[1]
    slots, tokens = send_ref.shape[1:]
    experts = chosen_ref.shape[2]
    numbers = lax.broadcasted_iota(jnp.int32, (slots, tokens), 0).astype(F32)
    nowhere = 1e6

    def table(source, expert, k):
        hit = pairs_ref[0, source, 0] == expert.astype(F32)
        order = pairs_ref[0, source, 1] * 32.0 + pairs_ref[0, source, 2]
        place = jnp.min(jnp.where(hit, order, nowhere), axis=0, keepdims=True)
        across = jnp.broadcast_to(place, (tokens, tokens))
        before = jnp.where(across.T < across, 1.0, 0.0)
        rank = jnp.sum(before, axis=0, keepdims=True)
        inside = (place < nowhere) & (rank < capacity)
        rank = jnp.where(inside, rank + k * capacity, -1.0)
        return jnp.where(numbers == rank, 1.0, 0.0)

    send = chosen = 0.0
    for k in range(4):
        send = send + table(0, mine_a * 4 + (mine_b ^ k), k)
        kept = table(k, mine_a * 4 + mine_b, k)
        routes = pairs_ref[0, k, 0]
        expert_rows = lax.broadcasted_iota(jnp.int32, (experts, tokens), 0).astype(F32)
        chooser = sum(
            jnp.where(routes[j : j + 1] == expert_rows, 1.0, 0.0) for j in range(TOP)
        )
        chosen = chosen + lax.dot_general(
            kept.astype(BF),
            chooser.astype(BF),
            (((1,), (1,)), ((), ())),
            preferred_element_type=F32,
        )
    send_ref[0] = send.astype(BF)
    back_ref[0] = send.T.astype(BF)
    chosen_ref[0] = chosen


def slot_tables(ids, pairs, capacity, experts):
    planes, _, _, _, tokens = pairs.shape
    slots = 4 * capacity
    block = lambda *shape: pl.BlockSpec((1,) + shape, lambda i: (i,) + (0,) * len(shape))
    return pl.pallas_call(
        lambda *refs: table_kernel(capacity, *refs),
        grid=(planes,),
        in_specs=[pl.BlockSpec(memory_space=pltpu.SMEM), block(4, 3, TOP, tokens)],
        out_specs=[block(slots, tokens), block(tokens, slots), block(slots, experts)],
        out_shape=[
            jax.ShapeDtypeStruct((planes, slots, tokens), BF),
            jax.ShapeDtypeStruct((planes, tokens, slots), BF),
            jax.ShapeDtypeStruct((planes, slots, experts), F32),
        ],
    )(ids, pairs)


def places(slot_rows, lengths_row):
    seq_ends = jnp.cumsum(lengths_row)
    starts = seq_ends - lengths_row
    segment = jnp.sum((slot_rows[:, None] >= seq_ends[None, :]).astype(jnp.int32), axis=1)
    chosen = segment[:, None] == jnp.arange(lengths_row.shape[0], dtype=jnp.int32)[None, :]
    start_of = jnp.sum(jnp.where(chosen, starts[None, :], 0), axis=1)
    return (segment, slot_rows - start_of)


def pick(blocks, index):
    return lax.dynamic_index_in_dim(blocks, index, 0, keepdims=False)


class Rounds:
    def __init__(self):
        self.active = {}
        self.asked = {}
        self.values = {}
        self.count = 0
        self.strict = True
        self.alone = None

    def start(self, task):
        self.count += 1
        self.active[self.count] = (task, None)
        return self.count

    def until(self, *wanted):
        def waiting_now():
            ready = [n for n in self.active if n in self.alone] if self.alone else self.active
            return [number for number in ready if number not in self.asked]

        while True:
            while waiting := waiting_now():
                for number in waiting:
                    task, came = self.active[number]
                    try:
                        self.asked[number] = task.send(came)
                    except StopIteration as end:
                        self.values[number] = end.value
                        del self.active[number]
            if all(number in self.values for number in wanted):
                break
            asked = {n: c for n, c in self.asked.items() if not self.alone or n in self.alone}
            given = {number: [args for _, args in calls] for number, calls in asked.items()}
            if self.strict:
                given = lax.optimization_barrier(given)
            came = {
                number: [call(*args) for (call, _), args in zip(calls, given[number])]
                for number, calls in asked.items()
            }
            if self.strict:
                came = lax.optimization_barrier(came)
            for number, results in came.items():
                self.active[number] = (self.active[number][0], results)
            self.asked = {n: calls for n, calls in self.asked.items() if n not in asked}
        values = [self.values[number] for number in wanted]
        return values[0] if len(values) == 1 else values

    def run(self, task):
        return self.until(self.start(task))

    def loosely(self, *wanted, also=None):
        self.strict, self.alone = False, None if also is None else wanted + also
        values = self.until(*wanted)
        self.strict, self.alone = True, None
        return values


def hold(count, *values):
    for _ in range(count):
        (values,) = yield [(lambda *v: v, values)]
    return values


def later(count, task):
    yield from hold(count)
    return (yield from task)


def work(function, *args):
    (result,) = yield [(function, args)]
    return result


class Links:
    def __init__(self, n):
        self.n = n
        self.planes = n // 4
        index = lax.axis_index("expert")
        self.g = lax.axis_index("dp")
        self.index = index
        self.p = index % 4
        self.l = index // 4
        self.square = n == 16
        if self.square:
            self.a = index % 2 + index // 8 * 2
            self.b = index // 2 % 2 * 2 + index // 4 % 2
        else:
            self.a, self.b = self.l, self.p
        masks = (0, 4, 2, 6) if self.square else (0, 1, 2, 3)
        self.places = [lambda v, k=k: self.flip(v, k) for k in range(4)]
        self.heads = [lambda v, m=m: self.flip(v, m) for m in masks]
        self.shifts = [lambda v, s=s: self.shift(v, s) for s in range(self.planes)]
        self.backs = [lambda v, s=s: self.shift(v, -s) for s in range(self.planes)]

    def device(self, a, b):
        if not self.square:
            return a * 4 + b
        return a % 2 + b // 2 * 2 + b % 2 * 4 + a // 2 * 8

    def row_block(self, g, a):
        return a % 2 + g * 2 + a // 2 * 4 if self.square else g * self.planes + a

    def block(self, r):
        return self.a ^ r if self.square else (self.a - r) % self.planes

    def flip(self, value, mask):
        return lax.ppermute(value, "expert", [(i, i ^ mask) for i in range(self.n)])

    def shift(self, value, step):
        return lax.ppermute(
            value, "expert", [(i, (i + step * 4) % self.n) for i in range(self.n)]
        )

    def onward(self, value):
        return self.shift(value, 1)

    def twin(self, value):
        return lax.ppermute(value, "dp", [(0, 1), (1, 0)])

    def natural(self, blocks, mine):
        odd, high = mine % 2 == 1, mine >= 2
        pair = [jnp.where(odd, blocks[q ^ 1], blocks[q]) for q in range(4)]
        return [jnp.where(high, pair[q ^ 2], pair[q]) for q in range(4)]

    def turned_line(self, blocks):
        twice = jnp.concatenate([blocks[::-1], blocks[::-1]], axis=0)
        return lax.dynamic_slice_in_dim(twice, self.planes - 1 - self.l, self.planes, 0)

    def head_gather(self, own):
        half = own.shape[0] // 2
        near_x, near_y = yield [(self.heads[1], (own,)), (self.heads[2], (own,))]
        low, high = yield [(self.heads[2], (near_x[:half],)), (self.heads[1], (near_y[half:],))]
        return jnp.concatenate([own, near_x, near_y, low, high], axis=0)

    def exchange(self, flips, blocks):
        came = yield [(flips[k], (blocks[k],)) for k in (3, 1, 2)]
        return [blocks[0], came[1], came[2], came[0]]

    def head_scatter(self, total):
        count = total.shape[0] // 4
        half = count // 2
        cut = lambda k, low, high: total[k * count + low : k * count + high]
        low, high = yield [
            (self.heads[2], (cut(3, 0, half).astype(BF),)),
            (self.heads[1], (cut(3, half, count).astype(BF),)),
        ]
        to_x = jnp.concatenate([cut(1, 0, half) + low.astype(F32), cut(1, half, count)], axis=0)
        to_y = jnp.concatenate([cut(2, 0, half), cut(2, half, count) + high.astype(F32)], axis=0)
        got_x, got_y = yield [
            (self.heads[1], (to_x.astype(BF),)),
            (self.heads[2], (to_y.astype(BF),)),
        ]
        return cut(0, 0, count) + got_x.astype(F32) + got_y.astype(F32)

    def block_gather(self, own, idle=(0, 0), count=None, give=None):
        if not self.square:
            came = yield [(shift, (own,)) for shift in self.shifts[1:]]
            return [own] + came
        x, z = (lambda v: self.flip(v, 1)), (lambda v: self.flip(v, 8))
        count = count or own.shape[0]
        half = count // 2 + own.shape[0] - count
        near, low = yield [(x, (own,)), (z, (own[:half],))]
        near, low = yield from hold(idle[0], near, low)
        rest = count - half
        more = [own[half:]] if give is None else [own[half:], near[count:]]
        high, far_low = yield [(z, (jnp.concatenate(more),)), (x, (low,))]
        high, far_low = yield from hold(idle[1], high, far_low)
        if give is not None:
            give(jnp.concatenate([own[count:], near[count:], high[rest:]]))
        (far_high,) = yield [(x, (high[:rest],))]
        return [
            own,
            near,
            jnp.concatenate([low, high[:rest]], axis=0),
            jnp.concatenate([far_low, far_high], axis=0),
        ]

    def block_gather_short(self, own):
        if not self.square:
            came = yield [(shift, (own,)) for shift in self.shifts[1:]]
            return [own] + came
        x, z = (lambda v: self.flip(v, 1)), (lambda v: self.flip(v, 8))
        near, across = yield [(x, (own,)), (z, (own,))]
        (far,) = yield [(x, (across,))]
        return [own, near, across, far]

    def block_scatter(self, blocks, split=False, idle=0):
        if not self.square:
            came = yield [
                (back, (block.astype(BF),)) for back, block in zip(self.backs[1:], blocks[1:])
            ]
            return sum((block.astype(F32) for block in came), blocks[0].astype(F32))
        x, z = (lambda v: self.flip(v, 1)), (lambda v: self.flip(v, 8))
        (came,) = yield [(x, (blocks[3].astype(BF),))]
        (came,) = yield from hold(idle, came)
        across = (blocks[2].astype(F32) + came.astype(F32)).astype(BF)
        if split:
            half = across.shape[0] // 2
            (got,) = yield [(z, (across[:half],))]
            near, more = yield [(x, (blocks[1].astype(BF),)), (z, (across[half:],))]
            got = jnp.concatenate([got, more], axis=0)
        else:
            near, got = yield [(x, (blocks[1].astype(BF),)), (z, (across,))]
        return blocks[0].astype(F32) + near.astype(F32) + got.astype(F32)

    def twin_scatter(self, make, own, other, idle=None, now=False):
        low = lambda *args: make(*args).astype(BF)
        if now:
            block = low(*other)
        else:
            (block,) = yield [(low, other)]
        if idle is None:
            came, total = yield [(self.twin, (block,)), (make, own)]
            return total + came.astype(F32)
        (came,) = yield [(self.twin, (block,))]
        (came,) = yield from hold(idle, came)
        (total,) = yield [(lambda came, *args: make(*args) + came.astype(F32), (came, *own))]
        return total


def body(
    hidden,
    lengths,
    slots,
    routes,
    order,
    gain_in,
    w_query,
    key_projection_weight,
    value_projection_weight,
    gain_q,
    gain_k,
    w_out,
    gain_mid,
    w_router,
    w_gate,
    w_up,
    w_down,
    cotangent,
):
    tokens = hidden.shape[0]
    experts = w_router.shape[1]
    links = Links(experts)
    planes = links.planes
    capacity = max(2, (tokens * TOP * 9 + 8 * experts - 1) // (8 * experts))
    block_tokens = 4 * tokens
    rows = gain_in.shape[0]
    head_part = gain_q.shape[0]
    devices = 2 * experts

    rounds = Rounds()
    spread = rounds.start
    slot_count = 4 * capacity

    gate_full = lax.all_gather(w_gate, "dp", axis=1, tiled=True)[0]
    up_full = lax.all_gather(w_up, "dp", axis=1, tiled=True)[0]
    down_full = lax.all_gather(w_down, "dp", axis=2, tiled=True)[0]

    lanes = 128
    gains = jnp.concatenate([gain_in, gain_mid, gain_q, gain_k], axis=0)
    gain_count = gains.shape[0]
    gains = jnp.pad(gains, (0, -gain_count % lanes)).reshape(-1, lanes)
    router_rows = rows * experts // lanes
    small = jnp.concatenate([w_router.reshape(-1, lanes), gains], axis=0)
    small = jnp.pad(small, ((0, -small.shape[0] % 8), (0, 0)))
    small_rows = small.shape[0]
    pairs = jnp.concatenate([part.T.astype(BF) for part in (routes, order // 32, order % 32)])
    expert_numbers = jnp.arange(experts, dtype=jnp.int32)
    ids = jnp.stack([links.l, links.p]).astype(jnp.int32)
    tables = {}

    qkv_width = QW + 2 * HEAD_SIZE
    rider = jnp.concatenate([small, pairs], axis=0)
    rider_rows = rider.shape[0]

    def own_columns(b):
        cut = lambda array, width: lax.dynamic_slice_in_dim(array, b * width, width, 1)
        return jnp.concatenate(
            [
                cut(w_query, QW),
                cut(key_projection_weight, HEAD_SIZE),
                cut(value_projection_weight, HEAD_SIZE),
            ],
            axis=1,
        )

    def gather_qkv():
        blocks = [own_columns(links.b ^ k) for k in range(4)]
        if not links.square:
            blocks = yield from links.exchange(links.heads, blocks)
            pieces = yield from links.block_gather(jnp.concatenate(blocks, axis=0))
            others = yield [(links.twin, (piece,)) for piece in pieces]
            return pieces + others
        more = rider.reshape(-1, qkv_width)
        held = more.shape[0]
        more = jnp.pad(more, ((0, -held % 8), (0, 0)))
        blocks = [jnp.concatenate([block, more], axis=0) for block in blocks]
        blocks = yield from links.exchange(links.heads, blocks)
        wide = stack_rows(blocks, rows)

        def give(found):
            found = found.reshape(4, 4, -1, qkv_width)[:, :, :held]
            tables["riders"] = found.reshape(4, 4, rider_rows, lanes)

        pieces = yield from links.block_gather(wide, count=4 * rows, give=give)
        others = yield [(links.twin, (piece,)) for piece in pieces]
        return pieces + others

    def gather_small():
        if links.square:
            yield from hold(3)
            parts = tables["riders"]
            parts = jnp.stack(links.natural([parts[r] for r in range(4)], links.a))
            parts = jnp.stack(links.natural([parts[:, k] for k in range(4)], links.b), axis=1)
            parts = parts.reshape(2, 2, 2, 2, rider_rows, lanes).transpose(0, 3, 2, 1, 4, 5)
            parts = parts.reshape(experts, rider_rows, lanes)
        else:
            blocks = yield from links.exchange(links.places, [rider] * 4)
            line = jnp.stack(links.natural(blocks, links.p))
            came = yield [(shift, (line,)) for shift in links.shifts[1:]]
            parts = links.turned_line(jnp.stack([line] + came))
            parts = parts.reshape(experts, rider_rows, lanes)
            yield from hold(1)
        own_small = parts[:, :small_rows]
        (other_small,) = yield [(links.twin, (own_small,))]
        tables["pairs"] = parts[:, small_rows:]
        return (yield from work(sort_small, own_small, other_small, rounds.values[hidden_task]))

    def sort_small(own_small, other_small, block_hidden):
        swap = links.g == 1
        small_all = jnp.concatenate(
            [jnp.where(swap, other_small, own_small), jnp.where(swap, own_small, other_small)]
        )
        gains = small_all[:, router_rows:].reshape(devices, -1)
        head_gains = gains[:, 2 * rows : gain_count].reshape(devices, 2, head_part)
        values = block_hidden.astype(F32)
        scale = lax.rsqrt(jnp.mean(values * values, axis=-1, keepdims=True) + EPS)
        full_in = gains[:, :rows].reshape(MODEL_WIDTH).astype(F32)
        return (
            (values * scale * full_in).astype(BF),
            small_all[:, :router_rows].reshape(MODEL_WIDTH, experts),
            full_in,
            gains[:, rows : 2 * rows].reshape(MODEL_WIDTH).astype(F32),
            head_gains.swapaxes(0, 1).reshape(2, HEAD_SIZE).astype(F32),
        )

    def make_tables(pairs):
        pairs = pairs.astype(F32).reshape(planes, 4, 3, TOP, tokens)
        pairs = links.turned_line(pairs)
        near = [lax.dynamic_index_in_dim(pairs, links.p ^ k, 1, keepdims=False) for k in range(4)]
        return slot_tables(ids, jnp.stack(near, axis=1), capacity, experts)

    exchange_task = spread(hold(1))
    qkv_task = spread(gather_qkv())

    def gather_hidden():
        (value,) = yield from hold(1, hidden)
        return (yield from links.head_gather(value))

    hidden_task = spread(gather_hidden())
    small_task = spread(gather_small())

    aligned = capacity % 8 == 0

    def choose(piece, step, backs=()):
        found = choose_rows(tables["send"][step], piece, 4 if aligned else 1, as_blocks(backs))
        return found if aligned else by_place(found[0])

    def by_place(slot_rows):
        return [slot_rows[k * capacity : (k + 1) * capacity] for k in range(4)]

    def as_blocks(blocks):
        return blocks if aligned or not blocks else [jnp.concatenate(blocks, axis=0)]

    def collect(blocks, step, width, more=None, kind=BF):
        return collect_rows(tables["back"][step], as_blocks(blocks), width, more, kind)

    def in_places(own, came):
        return [own, came[0], came[1], came[2]]

    def to_places(blocks):
        return [(links.places[k], (blocks[k],)) for k in (1, 2, 3)]

    def gather_upstream():
        pieces, out = [cotangent], []
        yield from hold(2)
        found = yield from work(make_tables, tables["pairs"])
        tables["send"], tables["back"], tables["chooser"] = found
        plan = [(1, True, 0)] + [(0, s < planes - 1, s) for s in range(1, planes)]
        for idle, hop, step in plan:
            yield from hold(idle)
            asks = [(links.onward, (pieces[-1],))] if hop else []
            if step is not None:
                blocks = choose(pieces[step], step)
                asks += to_places(blocks)
            came = yield asks
            if hop:
                pieces.append(came[0])
            if step is not None:
                out.append(jnp.concatenate([blocks[0]] + came[-3:], axis=0))
        return out

    upstream_task = spread(gather_upstream())

    head_rows = w_out.shape[0]
    if links.square:
        pairs_of = [(g, i) for g in range(2) for i in range(experts)]
        line = lambda i: i & 3 | (i >> 3 & 1) << 2 | (i >> 2 & 1) << 3
        swap_line = [(g * experts + i, g * experts + line(i)) for g, i in pairs_of]
        swap_core = [
            (g * experts + i, (i >> 1 & 1) * experts + (i & 13 | g << 1)) for g, i in pairs_of
        ]
        there = back = (swap_line, swap_core)
    else:
        to_block = [
            (b * 2 * planes + links.row_block(g, a), g * experts + links.device(a, b))
            for g in range(2)
            for a in range(planes)
            for b in range(4)
        ]
        there = (to_block, None)
        back = ([(to, of) for of, to in to_block], None)

    def moved(value, pairs_of):
        return value if pairs_of is None else lax.ppermute(value, ("dp", "expert"), pairs_of)

    def gather_out():
        pieces = yield from links.block_gather(rounds.values[move_task], (1, 0))
        pieces = jnp.concatenate(pieces, axis=0)
        (others,) = yield [(links.twin, (pieces,))]
        return pieces, others

    def move_out():
        value = yield from work(lambda value: moved(value, there[0]), w_out)
        return (yield from work(lambda value: moved(value, there[1]), value))

    move_task = spread(move_out())

    device_of = jnp.stack(
        [links.device(links.block(r), links.b ^ k) for r in range(planes) for k in range(4)]
    )
    starts = jnp.concatenate([(links.g ^ t) * experts + device_of for t in range(2)]) * rows
    all_slots = slots.reshape(experts, tokens)[device_of].reshape(experts * tokens)
    _, position = places(all_slots[:block_tokens], lengths[0])
    cosine, sine = rotary_tables(position)
    high = all_slots[:block_tokens]
    low = high - position

    rounds.until(exchange_task)
    found, block_hidden, qkv_pieces, _ = rounds.loosely(
        small_task, hidden_task, qkv_task, move_task, also=()
    )
    out_task = spread(gather_out())
    normalized, full_router, full_in, full_mid, head_gains = found
    w_qkv, projected, turned = rounds.run(
        work(
            lambda *args: project(rows, *args),
            starts,
            normalized,
            cosine,
            sine,
            head_gains,
            *qkv_pieces,
        )
    )
    keys_values = jnp.concatenate(
        rounds.run(links.block_gather_short(turned[:, QW:])), axis=0
    )
    keys_turned = keys_values[:, :HEAD_SIZE].T
    values_turned = keys_values[:, HEAD_SIZE:].T
    place_column = all_slots[:, None]
    low, high = low[None, :], high[None, :]

    def part_of(array, part, parts):
        width = array.shape[1] // parts
        return array[:, part * width : (part + 1) * width]

    def forward_part(query_rows):
        return attention_forward(query_rows, keys_values, values_turned, place_column, low, high)

    bounds = [0, PER_KV // 2, PER_KV]
    attended = [
        rounds.run(work(forward_part, turned[:, low_head * HEAD_SIZE : high_head * HEAD_SIZE]))
        for low_head, high_head in zip(bounds, bounds[1:])
    ]
    block_out = rounds.until(out_task)
    if head_rows == HEAD_SIZE:
        order_of = [
            links.row_block(links.g ^ t, links.block(r)) for t in range(2) for r in range(planes)
        ]
        order_of = jnp.stack(order_of).astype(jnp.int32)
    else:
        attended = jnp.concatenate(attended, axis=1)
        attended = [
            lax.dynamic_slice_in_dim(
                attended, links.row_block(links.g ^ t, links.block(r)) * head_rows, head_rows, 1
            )
            for t in range(2)
            for r in range(planes)
        ]
        attended = [jnp.concatenate(attended, axis=1)]
        order_of = jnp.arange(PER_KV, dtype=jnp.int32)
    branch, attended = rounds.run(
        work(lambda *parts: output_projection(order_of, parts, *block_out), *attended)
    )
    branch = rounds.loosely(spread(links.head_scatter(branch)))
    x_float = hidden.astype(F32)
    x_one = x_float + branch
    norm_two, norm_two_back = jax.vjp(rms_scale, x_one, full_mid)
    xn_two = norm_two.astype(BF)

    own_chooser = jnp.any(routes[:, :, None] == expert_numbers, axis=1)

    def masked_softmax(logits, chooser):
        top = jnp.max(jnp.where(chooser, logits, MASKED), axis=-1, keepdims=True)
        exponent = jnp.where(chooser, jnp.exp(jnp.where(chooser, logits - top, 0.0)), 0.0)
        total = jnp.sum(exponent, axis=-1, keepdims=True)
        return exponent / jnp.where(total > 0.0, total, 1.0)

    upstream_slots = rounds.until(upstream_task)
    me = links.index.astype(jnp.int32)[None]
    made = []

    def expert_step(step, *rows_in):
        found = expert_rows(
            me,
            as_blocks(list(rows_in)),
            upstream_slots[step],
            tables["chooser"][step],
            full_router,
            gate_full,
            up_full,
            down_full,
        )
        if aligned:
            return (found[:4], found[4:8], found[8:])
        return (by_place(found[0]), by_place(found[1]), found[2:])

    def return_mixture():
        def add(step, came, back, kind=BF):
            blocks = in_places(made[step][1][0], back)
            return collect(blocks, step, MODEL_WIDTH, came, kind)

        back = yield to_places(made[1][1])
        total = add(1, None, back)
        yield from hold(2)
        came, *back = yield [(links.onward, (total,))] + to_places(made[2][1])
        total = add(2, came, back)
        for step in range(3, planes):
            came, *back = yield [(links.onward, (total,))] + to_places(made[step][1])
            total = add(step, came, back)
        came, *back = yield [(links.onward, (total,))] + to_places(made[0][1])
        return add(0, came, back, F32)

    def experts_there_and_back():
        piece, ready, own_plane, total = xn_two, None, None, None
        wide = MODEL_WIDTH + lanes
        for step in range(planes + 3):
            asks = []
            back = made[step - 2][0] if 2 <= step < planes + 2 else []
            blocks = back
            if step < planes:
                blocks = choose(piece, step, back)
            if blocks:
                asks += to_places(blocks)
            if step < planes - 1:
                asks += [(links.onward, (piece,))]
            if step >= 4:
                asks += [(links.onward, (total,))]
            if 1 <= step <= planes:
                asks += [(lambda *v, s=step - 1: expert_step(s, *v), tuple(ready))]
            if step == planes + 2:
                tables["mixture"] = spread(return_mixture())
            came = yield asks
            if blocks:
                ready, came = in_places(blocks[0], came[:3]), came[3:]
            if step < planes - 1:
                piece, came = came[0], came[1:]
            if step >= 4:
                hop, came = came[0], came[1:]
            if 1 <= step <= planes:
                made.append(came[0])
            if step == 2:
                own_plane = collect(ready, 0, wide, None, F32)
            elif step == 3:
                total = collect(ready, 1, wide)
            elif step >= 4 and step < planes + 2:
                total = collect(ready, step - 2, wide, hop)
        return own_plane + hop.astype(F32)

    moe_grad = rounds.run(experts_there_and_back())
    gate_grads = moe_grad[:, MODEL_WIDTH : MODEL_WIDTH + experts]
    moe_grad = moe_grad[:, :MODEL_WIDTH]
    stacked = lambda place: jnp.concatenate([piece[2][place] for piece in made], axis=0)

    def by_rows(rows_in, grads_in):
        return jnp.einsum("rd,rf->df", rows_in, grads_in, preferred_element_type=F32)

    half_width = MODEL_WIDTH // 2

    def half_of(array, which):
        return lax.dynamic_slice_in_dim(array, which * half_width, half_width, 1)

    def gate_up_gradient(place):
        rows_in, grads_in = stacked(0), stacked(place)
        return links.twin_scatter(
            by_rows,
            (half_of(rows_in, links.g), grads_in),
            (half_of(rows_in, 1 - links.g), grads_in),
            idle=5,
        )

    def down_gradient():
        rows_in, grads_in = stacked(1), stacked(2)
        return links.twin_scatter(
            by_rows,
            (rows_in, half_of(grads_in, links.g)),
            (rows_in, half_of(grads_in, 1 - links.g)),
            idle=2,
        )

    gate_task = spread(gate_up_gradient(3))
    up_task = spread(later(1, gate_up_gradient(4)))
    down_task = spread(later(5, down_gradient()))

    def route(rows_in):
        logits = jnp.dot(rows_in, full_router, preferred_element_type=F32)
        return masked_softmax(logits, own_chooser)

    own_probs = route(lax.optimization_barrier((xn_two, moe_grad))[0])

    upstream = cotangent.astype(F32)
    chosen_grad = own_probs * (
        gate_grads - jnp.sum(own_probs * gate_grads, axis=-1, keepdims=True)
    )
    logit_grad = chosen_grad.astype(BF)
    xn_two_grad = moe_grad + jnp.dot(logit_grad, full_router.T, preferred_element_type=F32)
    x_one_norm_grad, grad_mid = norm_two_back(xn_two_grad)
    x_one_grad = upstream + x_one_norm_grad
    branch_grad = x_one_grad.astype(BF)

    block_grad = rounds.loosely(spread(links.head_gather(branch_grad)))

    def head_gradients(block_grad):
        grad = [
            jnp.einsum("td,hd->th", block_grad, part, preferred_element_type=F32).astype(BF)
            for part in block_out
        ]
        grad = jnp.concatenate(grad, axis=1)
        parts = []
        where = {links.row_block(g, a): (g, a) for g in range(2) for a in range(planes)}
        for head in range(2 * planes):
            g, a = where[head]
            at = ((links.g ^ g) * planes + links.block(a)) * head_rows
            parts.append(lax.dynamic_slice_in_dim(grad, at, head_rows, 1))
        return jnp.concatenate(parts, axis=1)

    heads_task = spread(work(head_gradients, block_grad))

    def scatter_out():
        half = QW // 2
        grad = yield from links.twin_scatter(
            lambda rows_in, grads_in: jnp.einsum(
                "th,td->hd", rows_in, grads_in, preferred_element_type=F32
            ),
            (attended[:, :half], block_grad),
            (attended[:, half:], block_grad),
            now=True,
        )
        grad = grad.astype(BF)
        blocks = [grad[r * head_rows : (r + 1) * head_rows] for r in range(planes)]
        grad = yield from links.block_scatter(blocks, split=True)
        (grad,) = yield from hold(2, grad.astype(BF))
        grad = yield from work(lambda value: moved(value, back[1]), grad)
        (grad,) = yield from hold(1, grad)
        grad = yield from work(lambda value: moved(value, back[0]), grad)
        return grad.astype(F32)

    grad_out_task = spread(scatter_out())

    def owners_blocks(grad):
        blocks = []
        for r in range(planes):
            owners = [links.device(links.block(r), links.b ^ k) for k in range(4)]
            parts = [lax.dynamic_slice_in_dim(grad, owner * rows, rows, 0) for owner in owners]
            blocks.append(jnp.concatenate(parts, axis=0))
        return blocks

    def half_rows(array, which):
        return lax.dynamic_slice_in_dim(array, which * (MODEL_WIDTH // 2), MODEL_WIDTH // 2, 0)

    def query_gradient(grads_in, extra):
        def make(which):
            grad = by_rows(half_of(normalized, which), grads_in)
            if extra is not None:
                grad = jnp.concatenate([grad, half_rows(extra, which)], axis=1)
            return grad

        grad = yield from links.twin_scatter(make, (links.g,), (1 - links.g,))
        grad = yield from links.block_scatter(owners_blocks(grad.astype(BF)))
        return grad.astype(BF)

    def key_value_gradient(key_value_grad, proj_grad):
        sums = jnp.concatenate([grad_qgain, grad_kgain]).reshape(2, devices, head_part)
        sums = jnp.pad(sums, ((0, 0), (0, 0), (0, rows - head_part))).reshape(2, MODEL_WIDTH).T
        sums = jnp.pad(sums, ((0, 0), (0, lanes - sums.shape[1])))

        def half(which):
            grad = by_rows(half_of(normalized, which), key_value_grad)
            return jnp.concatenate([grad, half_rows(sums, which)], axis=1)

        came, xn_one_grad = yield [
            (links.twin, (half(1 - links.g).astype(BF),)),
            (lambda proj_grad: input_gradient(proj_grad, w_qkv), (proj_grad,)),
        ]
        tables["scatter"] = spread(links.head_scatter(xn_one_grad))
        grad = (half(links.g) + came.astype(F32)).astype(BF)
        grad = yield from links.block_scatter(owners_blocks(grad))
        return grad.astype(BF)

    attended_grad = rounds.until(heads_task)
    grad_router = jnp.dot(xn_two.T, logit_grad, preferred_element_type=F32)
    first = jnp.concatenate([grad_router, grad_mid[:, None]], axis=1)
    first = jnp.pad(first, ((0, 0), (0, lanes - first.shape[1])))
    query_low_grads, query_tasks, key_terms, grad_qgain = [], [], None, None

    parts = 2
    for part in range(parts):
        got = rounds.run(
            work(
                lambda *args: attention_backward(
                    *args,
                    keys_values,
                    keys_turned,
                    place_column,
                    low,
                    high,
                    cosine,
                    sine,
                    head_gains[0:1],
                ),
                part_of(turned[:, :QW], part, parts),
                part_of(attended_grad, part, parts),
                part_of(projected[:, :QW], part, parts),
            )
        )
        query_low_grads.append(got[0])
        key_terms = got[1] if part == 0 else key_terms + got[1]
        grad_qgain = got[2] if part == 0 else grad_qgain + got[2]
        query_tasks.append(spread(query_gradient(got[0], None if part else first)))
    key_terms = rounds.run(
        links.block_scatter(
            [key_terms[r * block_tokens : (r + 1) * block_tokens] for r in range(planes)]
        )
    )

    key_proj_grad, grad_kgain = unturn(
        key_terms[:, :HEAD_SIZE],
        projected[:, QW : QW + HEAD_SIZE],
        cosine,
        sine,
        head_gains[1:2],
    )
    key_value_grad = jnp.concatenate([key_proj_grad, key_terms[:, HEAD_SIZE:].astype(BF)], axis=1)
    proj_grad = jnp.concatenate(query_low_grads + [key_value_grad], axis=1)
    key_value_task = spread(key_value_gradient(key_value_grad, proj_grad))
    one, two, three = rounds.until(*query_tasks, key_value_task)
    xn_one_grad = rounds.until(tables["scatter"])
    query_task = spread(links.exchange(links.heads, pack_rows(one, two, three)))
    _, norm_one_back = jax.vjp(lambda values: rms_scale(values, full_in), x_float)
    (x_norm_grad,) = norm_one_back(xn_one_grad)
    input_grad = (x_one_grad + x_norm_grad).astype(BF)

    grad_gate, grad_up, grad_down, mixture, grad_out, owned = rounds.until(
        gate_task, up_task, down_task, tables["mixture"], grad_out_task, query_task
    )
    result = (x_one + mixture).astype(BF)
    weights = (w_query, key_projection_weight, value_projection_weight)
    grad_query, grad_key, grad_value, first, last, inner = finish(links.b, owned, *weights)
    grad_router, grad_mid = first[:, :experts], first[:, experts]
    grad_qgain, grad_kgain = last[:head_part, 0], last[:head_part, 1]
    grad_in = inner[:, 0] / gain_in.astype(F32)

    return (
        result,
        input_grad,
        grad_in,
        grad_query,
        grad_key,
        grad_value,
        grad_qgain,
        grad_kgain,
        grad_out,
        grad_mid,
        grad_router,
        grad_gate[None],
        grad_up[None],
        grad_down[None],
    )


def solution(mesh):
    every = ("dp", "expert")
    in_specs = (
        P(every, None),
        P("dp", None),
        P("dp"),
        P(every, None),
        P(every, None),
        P(every),
        P(every, None),
        P(every, None),
        P(every, None),
        P(every),
        P(every),
        P(every, None),
        P(every),
        P(every, None),
        P("expert", "dp", None),
        P("expert", "dp", None),
        P("expert", None, "dp"),
        P(every, None),
    )
    out_specs = (
        P(every, None),
        P(every, None),
        P(every),
        P(every, None),
        P(every, None),
        P(every, None),
        P(every),
        P(every),
        P(every, None),
        P(every),
        P(every, None),
        P("expert", "dp", None),
        P("expert", "dp", None),
        P("expert", None, "dp"),
    )
    return jax.shard_map(body, mesh=mesh, in_specs=in_specs, out_specs=out_specs, check_vma=False)
```

```python
import math

import jax
import jax.numpy as jnp
from jax import lax
from jax.experimental import pallas as pl
from jax.experimental.pallas import tpu as pltpu
from jax.sharding import PartitionSpec as P

MODEL_WIDTH = 2048
QUERY_HEADS = 32
KEY_VALUE_HEADS = 4
HEAD_SIZE = 128
TOP = 8
PER_KV = QUERY_HEADS // KEY_VALUE_HEADS
QW = PER_KV * HEAD_SIZE

EPS = 1e-06
THETA = 1000000.0
MASKED = -1e30
KEY_STEP = 1024
EXPONENT = HEAD_SIZE**-0.5 / math.log(2.0)
BF = jnp.bfloat16
F32 = jnp.float32


def rms_scale(values, scaling):
    return values * lax.rsqrt(jnp.mean(values * values, axis=-1, keepdims=True) + EPS) * scaling


def rotary_tables(position):
    half = HEAD_SIZE // 2
    index_float = jnp.arange(half, dtype=jnp.float32)
    freq = jnp.power(jnp.float32(THETA), -2.0 * index_float / HEAD_SIZE)
    angle = position.astype(jnp.float32)[:, None] * freq[None, :]
    cosine, sine = jnp.cos(angle), jnp.sin(angle)
    return (
        jnp.concatenate([cosine, cosine], axis=-1),
        jnp.concatenate([-sine, sine], axis=-1),
    )


def stack_kernel(rows, *refs):
    *block_refs, out_ref = refs
    blocks = [ref[...].astype(F32) for ref in block_refs]
    stack = [block[:rows] for block in blocks] + [block[rows:] for block in blocks]
    out_ref[...] = jnp.concatenate(stack, axis=0).astype(BF)


def stack_rows(blocks, rows):
    height, width = blocks[0].shape
    return pl.pallas_call(
        lambda *refs: stack_kernel(rows, *refs),
        out_shape=jax.ShapeDtypeStruct((height * len(blocks), width), BF),
    )(*blocks)


def project_kernel(starts_ref, x_ref, cos_ref, sin_ref, gains_ref, *refs):
    pieces, (w_ref, proj_ref, turned_ref) = refs[:-3], refs[-3:]
    last = pl.program_id(0) == pl.num_programs(0) - 1
    rows = pieces[0].shape[0] // 4
    for number, piece in enumerate(pieces):
        for k in range(4):
            at = pl.multiple_of(starts_ref[number * 4 + k], rows)
            w_ref[pl.ds(at, rows), :] = piece[k * rows : (k + 1) * rows, :]
    projected = jnp.dot(x_ref[...], w_ref[...], preferred_element_type=F32)
    proj_ref[...] = projected

    def turn(values, gain):
        scaled = (
            values * lax.rsqrt(jnp.mean(values * values, axis=-1, keepdims=True) + EPS) * gain
        )
        swapped = pltpu.roll(scaled, HEAD_SIZE // 2, 1)
        return scaled * cos_ref[...] + swapped * sin_ref[...]

    gain_q, gain_k = gains_ref[0:1], gains_ref[1:2]
    first, second = projected[:, :HEAD_SIZE], projected[:, HEAD_SIZE:]
    turned_ref[:, :HEAD_SIZE] = turn(first, jnp.where(last, gain_k, gain_q)).astype(BF)
    turned_ref[:, HEAD_SIZE:] = jnp.where(last, second, turn(second, gain_q)).astype(BF)


def project(rows, starts, rows_in, cosine, sine, gains, *pieces):
    count, width = rows_in.shape
    height, columns = 4 * rows, pieces[0].shape[1]
    step = 2 * HEAD_SIZE
    whole = lambda array: pl.BlockSpec(array.shape, lambda i: (0, 0))
    strip = lambda height: pl.BlockSpec((height, step), lambda i: (0, i))
    return pl.pallas_call(
        project_kernel,
        grid=(columns // step,),
        in_specs=[pl.BlockSpec(memory_space=pltpu.SMEM)]
        + [whole(rows_in), whole(cosine), whole(sine), whole(gains)]
        + [strip(height)] * len(pieces),
        out_specs=[strip(width), strip(count), strip(count)],
        out_shape=[
            jax.ShapeDtypeStruct((width, columns), BF),
            jax.ShapeDtypeStruct((count, columns), F32),
            jax.ShapeDtypeStruct((count, columns), BF),
        ],
        cost_estimate=pl.CostEstimate(
            flops=2 * count * width * columns,
            bytes_accessed=2 * (count + columns) * width,
            transcendentals=0,
        ),
        compiler_params=pltpu.CompilerParams(vmem_limit_bytes=60 * 2**20),
    )(starts, rows_in, cosine, sine, gains, *pieces)


def unturned(grad, values, cosine, sine, gain):
    grad = grad * cosine + pltpu.roll(grad * sine, HEAD_SIZE // 2, 1)
    scale = lax.rsqrt(jnp.mean(values * values, axis=-1, keepdims=True) + EPS)
    gain_grad = jnp.sum(grad * values * scale, axis=0, keepdims=True)
    grad = grad * gain
    inner = jnp.mean(grad * values, axis=-1, keepdims=True)
    return (scale * grad - values * (scale * scale * scale * inner)).astype(BF), gain_grad


def unturn_kernel(grad_ref, proj_ref, cos_ref, sin_ref, gain_ref, out_ref, gain_grad_ref):
    out_ref[...], gain_grad_ref[...] = unturned(
        grad_ref[...], proj_ref[...], cos_ref[...], sin_ref[...], gain_ref[...]
    )


def unturn(grad, projected, cosine, sine, gain):
    return pl.pallas_call(
        unturn_kernel,
        out_shape=[
            jax.ShapeDtypeStruct(grad.shape, BF),
            jax.ShapeDtypeStruct(gain.shape, F32),
        ],
    )(grad, projected, cosine, sine, gain)


def input_kernel(grad_ref, w_ref, out_ref):
    dims = (((1,), (1,)), ((), ()))
    out_ref[...] = lax.dot_general(grad_ref[...], w_ref[...], dims, preferred_element_type=F32)


def input_gradient(proj_grad, weights):
    count, columns = proj_grad.shape
    width = weights.shape[0]
    step = 256
    return pl.pallas_call(
        input_kernel,
        grid=(width // step,),
        in_specs=[
            pl.BlockSpec((count, columns), lambda i: (0, 0)),
            pl.BlockSpec((step, columns), lambda i: (i, 0)),
        ],
        out_specs=pl.BlockSpec((count, step), lambda i: (0, i)),
        out_shape=jax.ShapeDtypeStruct((count, width), F32),
        cost_estimate=pl.CostEstimate(
            flops=2 * count * width * columns,
            bytes_accessed=6 * (count + columns) * width,
            transcendentals=0,
        ),
        compiler_params=pltpu.CompilerParams(vmem_limit_bytes=24 * 2**20),
    )(proj_grad, weights)


def output_kernel(order_ref, *refs):
    *part_refs, own_ref, other_ref, out_ref, rows_ref, natural_ref = refs
    half = own_ref.shape[0]

    @pl.when(pl.program_id(0) == 0)
    def _():
        at = 0
        for part_ref in part_refs:
            width = part_ref.shape[1]
            natural_ref[:, at : at + width] = part_ref[...]
            at += width
        for head in range(at // HEAD_SIZE):
            start = pl.multiple_of(order_ref[head] * HEAD_SIZE, HEAD_SIZE)
            here = slice(head * HEAD_SIZE, (head + 1) * HEAD_SIZE)
            rows_ref[:, here] = natural_ref[:, pl.ds(start, HEAD_SIZE)]

    out_ref[...] = jnp.dot(
        rows_ref[:, :half], own_ref[...], preferred_element_type=F32
    ) + jnp.dot(rows_ref[:, half:], other_ref[...], preferred_element_type=F32)


def output_projection(order, parts, own, other):
    count = parts[0].shape[0]
    half, width = own.shape
    columns = 2 * half
    step = 256
    strip = lambda height: pl.BlockSpec((height, step), lambda i: (0, i))
    whole = lambda shape: pl.BlockSpec(shape, lambda i: (0, 0))
    return pl.pallas_call(
        output_kernel,
        grid=(width // step,),
        in_specs=[pl.BlockSpec(memory_space=pltpu.SMEM)]
        + [whole(part.shape) for part in parts]
        + [strip(half), strip(half)],
        out_specs=[strip(count), whole((count, columns))],
        out_shape=[
            jax.ShapeDtypeStruct((count, width), F32),
            jax.ShapeDtypeStruct((count, columns), BF),
        ],
        scratch_shapes=[pltpu.VMEM((count, columns), BF)],
        cost_estimate=pl.CostEstimate(
            flops=2 * count * width * columns,
            bytes_accessed=4 * (count + columns) * width,
            transcendentals=0,
        ),
        compiler_params=pltpu.CompilerParams(vmem_limit_bytes=24 * 2**20),
    )(order, *parts, own, other)


def fill_bias(place_ref, low_ref, high_ref, bias_ref):
    step = min(KEY_STEP, bias_ref.shape[0])

    def fill(i, carry):
        at = pl.ds(pl.multiple_of(i * step, step), step)
        place = place_ref[at, :]
        seen = (place >= low_ref[...]) & (place <= high_ref[...])
        bias_ref[at, :] = jnp.where(seen, 0.0, MASKED)
        return carry

    lax.fori_loop(0, bias_ref.shape[0] // step, fill, 0)


def forward_kernel(
    q_ref, kv_ref, vt_ref, place_ref, low_ref, high_ref, out_ref, p_ref, bias_ref, sum_ref
):
    count, queries = p_ref.shape
    step = min(KEY_STEP, count)
    part = lambda i: pl.ds(pl.multiple_of(i * step, step), step)
    q = q_ref[...]

    @pl.when((pl.program_id(0) == 0) | (pl.num_programs(1) > 1))
    def _():
        fill_bias(place_ref, low_ref, high_ref, bias_ref)

    def score(i, top):
        scores = lax.dot_general(
            kv_ref[part(i), :HEAD_SIZE], q, (((1,), (1,)), ((), ())), preferred_element_type=F32
        )
        scores = scores + bias_ref[part(i), :]
        p_ref[part(i), :] = scores
        return jnp.maximum(top, jnp.max(scores, axis=0, keepdims=True))

    top = lax.fori_loop(0, count // step, score, jnp.full((1, queries), MASKED, F32))

    def lift(i, total):
        exponent = jnp.exp2((p_ref[part(i), :] - top) * EXPONENT)
        p_ref[part(i), :] = exponent
        return total + jnp.sum(exponent, axis=0, keepdims=True)

    total = lax.fori_loop(0, count // step, lift, jnp.zeros((1, queries), F32))
    share = 1.0 / total
    sum_ref[...] = jnp.zeros_like(sum_ref)

    def mix(i, carry):
        probs = (p_ref[part(i), :] * share).astype(BF)
        sum_ref[...] += jnp.dot(vt_ref[:, part(i)], probs, preferred_element_type=F32)
        return carry

    lax.fori_loop(0, count // step, mix, 0)
    out_ref[...] = sum_ref[...].T.astype(BF)


def attention_blocks(rows, count):
    step = min(rows, 512 * 2048 // count)
    whole = lambda array: pl.BlockSpec(array.shape, lambda i, j: (0, 0))
    head = pl.BlockSpec((step, HEAD_SIZE), lambda i, j: (j, i))
    along = pl.BlockSpec((1, step), lambda i, j: (0, j))
    down = pl.BlockSpec((step, HEAD_SIZE), lambda i, j: (j, 0))
    limit = (32 if count <= 2048 else 60) * 2**20
    return step, whole, head, along, down, limit


def attention_forward(q, keys_values, values_turned, place, low, high):
    rows, columns = q.shape
    count = keys_values.shape[0]
    step, whole, head, along, _, limit = attention_blocks(rows, count)
    return pl.pallas_call(
        forward_kernel,
        grid=(columns // HEAD_SIZE, rows // step),
        in_specs=[head, whole(keys_values), whole(values_turned), whole(place), along, along],
        out_specs=head,
        out_shape=jax.ShapeDtypeStruct(q.shape, BF),
        scratch_shapes=[pltpu.VMEM((count, step), F32)] * 2
        + [pltpu.VMEM((HEAD_SIZE, step), F32)],
        cost_estimate=pl.CostEstimate(
            flops=8 * rows * columns * count, bytes_accessed=4 * rows * columns, transcendentals=0
        ),
        compiler_params=pltpu.CompilerParams(vmem_limit_bytes=limit),
    )(q, keys_values, values_turned, place, low, high)


def backward_kernel(
    q_ref, grad_ref, proj_ref, kv_ref, kt_ref, place_ref, low_ref, high_ref, cos_ref, sin_ref,
    gain_ref, out_ref, dkv_ref, gain_grad_ref, p_ref, dp_ref, bias_ref, dq_ref,
):
    @pl.when((pl.program_id(0) == 0) & (pl.program_id(1) == 0))
    def _():
        dkv_ref[...] = jnp.zeros_like(dkv_ref)
        gain_grad_ref[...] = jnp.zeros_like(gain_grad_ref)

    @pl.when((pl.program_id(0) == 0) | (pl.num_programs(1) > 1))
    def _():
        fill_bias(place_ref, low_ref, high_ref, bias_ref)

    count, queries = p_ref.shape
    step = min(KEY_STEP, count)
    part = lambda i: pl.ds(pl.multiple_of(i * step, step), step)
    scale = HEAD_SIZE**-0.5
    q, grad = q_ref[...], grad_ref[...]

    def across(left, right):
        dims = (((1,), (1,)), ((), ()))
        return lax.dot_general(left, right, dims, preferred_element_type=F32)

    def score(i, top):
        scores = across(kv_ref[part(i), :HEAD_SIZE], q) + bias_ref[part(i), :]
        p_ref[part(i), :] = scores
        return jnp.maximum(top, jnp.max(scores, axis=0, keepdims=True))

    top = lax.fori_loop(0, count // step, score, jnp.full((1, queries), MASKED, F32))

    def lift(i, sums):
        total, inner = sums
        exponent = jnp.exp2((p_ref[part(i), :] - top) * EXPONENT)
        p_ref[part(i), :] = exponent
        total = total + jnp.sum(exponent, axis=0, keepdims=True)
        prob_grad = across(kv_ref[part(i), HEAD_SIZE:], grad)
        dp_ref[part(i), :] = prob_grad
        return total, inner + jnp.sum(exponent * prob_grad, axis=0, keepdims=True)

    nothing = jnp.zeros((1, queries), F32)
    total, inner = lax.fori_loop(0, count // step, lift, (nothing, nothing))
    share = 1.0 / total
    inner = inner * share
    dq_ref[...] = jnp.zeros_like(dq_ref)

    def back(i, carry):
        probs = p_ref[part(i), :] * share
        score_grad = (probs * (dp_ref[part(i), :] - inner)).astype(BF)
        dkv_ref[part(i), HEAD_SIZE:] += jnp.dot(
            probs.astype(BF), grad, preferred_element_type=F32
        )
        dkv_ref[part(i), :HEAD_SIZE] += (
            jnp.dot(score_grad, q, preferred_element_type=F32) * scale
        )
        dq_ref[...] += jnp.dot(kt_ref[:, part(i)], score_grad, preferred_element_type=F32)
        return carry

    lax.fori_loop(0, count // step, back, 0)
    out_ref[...], gain_grad = unturned(
        dq_ref[...].T * scale, proj_ref[...], cos_ref[...], sin_ref[...], gain_ref[...]
    )
    gain_grad_ref[...] += gain_grad


def attention_backward(
    q, grad, projected, keys_values, keys_turned, place, low, high, cosine, sine, gain
):
    rows, columns = q.shape
    count = keys_values.shape[0]
    step, whole, head, along, down, limit = attention_blocks(rows, count)
    return pl.pallas_call(
        backward_kernel,
        grid=(columns // HEAD_SIZE, rows // step),
        in_specs=[head, head, head, whole(keys_values), whole(keys_turned), whole(place)]
        + [along, along, down, down, whole(gain)],
        out_specs=[head, whole(keys_values), whole(gain)],
        out_shape=[
            jax.ShapeDtypeStruct(q.shape, BF),
            jax.ShapeDtypeStruct(keys_values.shape, F32),
            jax.ShapeDtypeStruct(gain.shape, F32),
        ],
        scratch_shapes=[pltpu.VMEM((count, step), F32)] * 3
        + [pltpu.VMEM((HEAD_SIZE, step), F32)],
        cost_estimate=pl.CostEstimate(
            flops=10 * rows * columns * count, bytes_accessed=8 * rows * columns, transcendentals=0
        ),
        compiler_params=pltpu.CompilerParams(vmem_limit_bytes=60 * 2**20),
    )(q, grad, projected, keys_values, keys_turned, place, low, high, cosine, sine, gain)


def pack_kernel(*refs):
    *array_refs, out_0, out_1, out_2, out_3 = refs
    rows = out_0.shape[0]
    for k, out_ref in enumerate((out_0, out_1, out_2, out_3)):
        at = 0
        for array_ref in array_refs:
            width = array_ref.shape[1]
            out_ref[:, at : at + width] = array_ref[k * rows : (k + 1) * rows, :]
            at += width


def pack_rows(*arrays):
    rows = arrays[0].shape[0] // 4
    width = sum(array.shape[1] for array in arrays)
    return pl.pallas_call(
        pack_kernel,
        out_shape=[jax.ShapeDtypeStruct((rows, width), BF)] * 4,
    )(*arrays)


def finish_kernel(ids_ref, b0, b1, b2, b3, gain_ref, low_ref, wq_ref, wk_ref, wv_ref, *refs):
    gq_ref, gk_ref, gv_ref, router_ref, out_ref, mid_ref, in_ref, q_ref, k_ref = refs
    out_ref[...] = low_ref[...].astype(F32)
    half = QW // 2
    lanes = 128
    at = QW + lanes
    first = last = 0.0
    for k, ref in enumerate((b0, b1, b2, b3)):
        head = ids_ref[0] ^ k
        block = ref[...].astype(F32)
        wide = pl.multiple_of(head * QW, QW)
        thin = pl.multiple_of(head * HEAD_SIZE, HEAD_SIZE)
        gq_ref[:, pl.ds(wide, half)] = block[:, :half]
        gq_ref[:, pl.ds(wide + half, half)] = block[:, half + lanes : at]
        gk_ref[:, pl.ds(thin, HEAD_SIZE)] = block[:, at : at + HEAD_SIZE]
        gv_ref[:, pl.ds(thin, HEAD_SIZE)] = block[:, at + HEAD_SIZE : at + 2 * HEAD_SIZE]
        first = first + block[:, half : half + lanes]
        last = last + block[:, at + 2 * HEAD_SIZE :]
    inner = 0.0
    for w_ref, g_ref in ((wq_ref, gq_ref), (wk_ref, gk_ref), (wv_ref, gv_ref)):
        inner = inner + jnp.sum(w_ref[...].astype(F32) * g_ref[...], axis=1, keepdims=True)
    experts = router_ref.shape[1]
    router_ref[...] = first[:, :experts]
    first, last = first.T, last.T
    inner = jnp.broadcast_to(inner, (inner.shape[0], lanes)).T
    mid_ref[...] = first[experts : experts + 1]
    in_ref[...] = inner[0:1] / gain_ref[...]
    part = q_ref.shape[1]
    q_ref[...] = last[0:1, :part]
    k_ref[...] = last[1:2, :part]


def finish(b, blocks, gain, low, experts, head_part, *weights):
    rows = blocks[0].shape[0]
    shapes = [weight.shape for weight in weights] + [(rows, experts), low.shape]
    shapes += [(1, rows)] * 2 + [(1, head_part)] * 2
    return pl.pallas_call(
        finish_kernel,
        in_specs=[pl.BlockSpec(memory_space=pltpu.SMEM)]
        + [pl.BlockSpec(memory_space=pltpu.VMEM)] * 9,
        out_shape=[jax.ShapeDtypeStruct(shape, F32) for shape in shapes],
    )(b.astype(jnp.int32)[None], *blocks, gain, low, *weights)


def choose_kernel(blocks, table_ref, piece_ref, *refs):
    chosen = jnp.dot(table_ref[...], piece_ref[...], preferred_element_type=F32)
    back_refs, out_refs = refs[:-blocks], refs[-blocks:]
    count = out_refs[0].shape[0]
    width = piece_ref.shape[1]
    for k, out_ref in enumerate(out_refs):
        part = chosen[k * count : (k + 1) * count].astype(BF)
        if back_refs:
            out_ref[:, :width] = part
            out_ref[:, width:] = back_refs[k][...]
        else:
            out_ref[...] = part


def choose_rows(table, piece, blocks, backs=()):
    width = piece.shape[1] + (backs[0].shape[1] if backs else 0)
    shape = (table.shape[0] // blocks, width)
    return pl.pallas_call(
        lambda *refs: choose_kernel(blocks, *refs),
        out_shape=[jax.ShapeDtypeStruct(shape, BF)] * blocks,
        compiler_params=pltpu.CompilerParams(vmem_limit_bytes=16 * 2**20),
    )(table, piece, *backs)


def collect_kernel(blocks, table_ref, *refs):
    width = refs[-1].shape[1]
    rows_in = [ref[:, ref.shape[1] - width :].astype(F32) for ref in refs[:blocks]]
    stack = jnp.concatenate(rows_in, axis=0).astype(BF)
    total = jnp.dot(table_ref[...], stack, preferred_element_type=F32)
    if len(refs) > blocks + 1:
        total = total + refs[blocks][...].astype(F32)
    refs[-1][...] = total.astype(refs[-1].dtype)


def collect_rows(table, blocks, width, more=None, kind=BF):
    extra = [] if more is None else [more]
    return pl.pallas_call(
        lambda *refs: collect_kernel(len(blocks), *refs),
        out_shape=jax.ShapeDtypeStruct((table.shape[0], width), kind),
        compiler_params=pltpu.CompilerParams(vmem_limit_bytes=24 * 2**20),
    )(table, *blocks, *extra)


def expert_kernel(blocks, me_ref, *refs):
    rows_refs, refs = refs[:blocks], refs[blocks:]
    upstream_ref, chooser_ref, router_ref, gate_ref, up_ref, down_ref = refs[:6]
    back_refs, mixed_refs = refs[6 : 6 + blocks], refs[6 + blocks : 6 + 2 * blocks]
    refs = refs[6 + 2 * blocks :]
    rows_ref, act_ref, out_grad_ref, gate_low_ref, up_low_ref = refs[:5]
    share_ref, returned_ref, pair_ref = refs[5:]
    step = pl.program_id(0)
    across = (((1,), (1,)), ((), ()))

    @pl.when(step == 0)
    def _():
        rows_in = jnp.concatenate([ref[...].astype(F32) for ref in rows_refs], axis=0).astype(BF)
        upstream = upstream_ref[...].astype(F32)
        logits = jnp.dot(rows_in, router_ref[...], preferred_element_type=F32)
        chosen = chooser_ref[...] > 0.0
        top = jnp.max(jnp.where(chosen, logits, MASKED), axis=1, keepdims=True)
        exponent = jnp.where(chosen, jnp.exp(jnp.where(chosen, logits - top, 0.0)), 0.0)
        total = jnp.sum(exponent, axis=1, keepdims=True)
        number = lax.broadcasted_iota(jnp.int32, exponent.shape, 1)
        mine = jnp.sum(jnp.where(number == me_ref[0], exponent, 0.0), axis=1, keepdims=True)
        share = mine / jnp.where(total > 0.0, total, 1.0)
        rows_ref[...] = rows_in
        out_grad_ref[...] = (share * upstream).astype(BF)
        share_ref[...] = jnp.broadcast_to(share, share_ref.shape)
        returned_ref[...] = jnp.zeros_like(returned_ref)
        pair_ref[...] = jnp.zeros_like(pair_ref)

    rows_in, out_grad = rows_ref[...], out_grad_ref[...]
    gate, up, down = gate_ref[...], up_ref[...], down_ref[...]
    gate_pre = jnp.dot(rows_in, gate, preferred_element_type=F32)
    up_pre = jnp.dot(rows_in, up, preferred_element_type=F32)
    act_grad = lax.dot_general(out_grad, down, across, preferred_element_type=F32)
    logistic = jax.nn.sigmoid(gate_pre)
    silu = gate_pre * logistic
    act = (silu * up_pre).astype(BF)
    gate_low = (act_grad * up_pre * logistic * (1.0 + gate_pre * (1.0 - logistic))).astype(BF)
    up_low = (act_grad * silu).astype(BF)
    act_ref[...], gate_low_ref[...], up_low_ref[...] = act, gate_low, up_low
    returned_ref[...] += jnp.dot(act, down, preferred_element_type=F32)
    pair_ref[...] += lax.dot_general(
        gate_low, gate, across, preferred_element_type=F32
    ) + lax.dot_general(up_low, up, across, preferred_element_type=F32)

    @pl.when(step == pl.num_programs(0) - 1)
    def _():
        returned = returned_ref[...].astype(BF).astype(F32)
        upstream = upstream_ref[...].astype(F32)
        gate_grad = jnp.sum(upstream * returned, axis=1, keepdims=True)
        mixed = share_ref[:, :1] * returned
        pair = pair_ref[...]
        count = rows_refs[0].shape[0]
        width = pair.shape[1]
        number = lax.broadcasted_iota(jnp.int32, share_ref.shape, 1)
        gates = jnp.where(number == me_ref[0], gate_grad, 0.0)
        for k in range(blocks):
            part = slice(k * count, (k + 1) * count)
            back_refs[k][:, :width] = pair[part].astype(BF)
            back_refs[k][:, width:] = gates[part].astype(BF)
            mixed_refs[k][...] = mixed[part].astype(BF)


def expert_rows(me, rows_in, upstream, chooser, router, gate, up, down):
    blocks = len(rows_in)
    slots, width = upstream.shape
    block = (slots // blocks, width)
    ff = gate.shape[1]
    step = 256
    lanes = 128
    whole = lambda shape: pl.BlockSpec(shape, lambda i: (0, 0))
    columns = lambda height: pl.BlockSpec((height, step), lambda i: (0, i))
    shape = jax.ShapeDtypeStruct
    out = [((block[0], width + lanes), BF)] * blocks + [(block, BF)] * blocks
    out_specs = [whole(dims) for dims, _ in out]
    out_specs += [whole((slots, width)), columns(slots), whole((slots, width))]
    out_specs += [columns(slots)] * 2
    out += [((slots, width), BF), ((slots, ff), BF), ((slots, width), BF)]
    out += [((slots, ff), BF)] * 2
    return pl.pallas_call(
        lambda *refs: expert_kernel(blocks, *refs),
        grid=(ff // step,),
        in_specs=[pl.BlockSpec(memory_space=pltpu.SMEM)]
        + [whole(block)] * blocks
        + [whole(upstream.shape), whole(chooser.shape), whole(router.shape)]
        + [columns(width), columns(width), pl.BlockSpec((step, width), lambda i: (i, 0))],
        out_specs=out_specs,
        out_shape=[shape(dims, kind) for dims, kind in out],
        scratch_shapes=[
            pltpu.VMEM((slots, lanes), F32),
            pltpu.VMEM((slots, width), F32),
            pltpu.VMEM((slots, width), F32),
        ],
        cost_estimate=pl.CostEstimate(
            flops=12 * slots * width * ff, bytes_accessed=6 * width * ff, transcendentals=0
        ),
        compiler_params=pltpu.CompilerParams(vmem_limit_bytes=44 * 2**20),
    )(me, *rows_in, upstream, chooser, router, gate, up, down)


def table_kernel(capacity, ids_ref, pairs_ref, send_ref, back_ref, chosen_ref):
    mine_a, mine_b = ids_ref[0], ids_ref[1]
    slots, tokens = send_ref.shape[1:]
    experts = chosen_ref.shape[2]
    numbers = lax.broadcasted_iota(jnp.int32, (slots, tokens), 0).astype(F32)
    nowhere = 1e6

    def table(source, expert, k):
        hit = pairs_ref[0, source, 0] == expert.astype(F32)
        order = pairs_ref[0, source, 1] * 32.0 + pairs_ref[0, source, 2]
        place = jnp.min(jnp.where(hit, order, nowhere), axis=0, keepdims=True)
        across = jnp.broadcast_to(place, (tokens, tokens))
        before = jnp.where(across.T < across, 1.0, 0.0)
        rank = jnp.sum(before, axis=0, keepdims=True)
        inside = (place < nowhere) & (rank < capacity)
        rank = jnp.where(inside, rank + k * capacity, -1.0)
        return jnp.where(numbers == rank, 1.0, 0.0)

    send = chosen = 0.0
    for k in range(4):
        send = send + table(0, mine_a * 4 + (mine_b ^ k), k)
        kept = table(k, mine_a * 4 + mine_b, k)
        routes = pairs_ref[0, k, 0]
        expert_rows = lax.broadcasted_iota(jnp.int32, (experts, tokens), 0).astype(F32)
        chooser = sum(
            jnp.where(routes[j : j + 1] == expert_rows, 1.0, 0.0) for j in range(TOP)
        )
        chosen = chosen + lax.dot_general(
            kept.astype(BF),
            chooser.astype(BF),
            (((1,), (1,)), ((), ())),
            preferred_element_type=F32,
        )
    send_ref[0] = send.astype(BF)
    back_ref[0] = send.T.astype(BF)
    chosen_ref[0] = chosen


def slot_tables(ids, pairs, capacity, experts):
    planes, _, _, _, tokens = pairs.shape
    slots = 4 * capacity
    block = lambda *shape: pl.BlockSpec((1,) + shape, lambda i: (i,) + (0,) * len(shape))
    return pl.pallas_call(
        lambda *refs: table_kernel(capacity, *refs),
        grid=(planes,),
        in_specs=[pl.BlockSpec(memory_space=pltpu.SMEM), block(4, 3, TOP, tokens)],
        out_specs=[block(slots, tokens), block(tokens, slots), block(slots, experts)],
        out_shape=[
            jax.ShapeDtypeStruct((planes, slots, tokens), BF),
            jax.ShapeDtypeStruct((planes, tokens, slots), BF),
            jax.ShapeDtypeStruct((planes, slots, experts), F32),
        ],
    )(ids, pairs)


def places(slot_rows, lengths_row):
    seq_ends = jnp.cumsum(lengths_row)
    starts = seq_ends - lengths_row
    segment = jnp.sum((slot_rows[:, None] >= seq_ends[None, :]).astype(jnp.int32), axis=1)
    chosen = segment[:, None] == jnp.arange(lengths_row.shape[0], dtype=jnp.int32)[None, :]
    start_of = jnp.sum(jnp.where(chosen, starts[None, :], 0), axis=1)
    return (segment, slot_rows - start_of)


def pick(blocks, index):
    return lax.dynamic_index_in_dim(blocks, index, 0, keepdims=False)


class Rounds:
    def __init__(self):
        self.active = {}
        self.asked = {}
        self.values = {}
        self.count = 0
        self.strict = True
        self.alone = None

    def start(self, task):
        self.count += 1
        self.active[self.count] = (task, None)
        return self.count

    def until(self, *wanted):
        def waiting_now():
            ready = [n for n in self.active if n in self.alone] if self.alone else self.active
            return [number for number in ready if number not in self.asked]

        while True:
            while waiting := waiting_now():
                for number in waiting:
                    task, came = self.active[number]
                    try:
                        self.asked[number] = task.send(came)
                    except StopIteration as end:
                        self.values[number] = end.value
                        del self.active[number]
            if all(number in self.values for number in wanted):
                break
            asked = {n: c for n, c in self.asked.items() if not self.alone or n in self.alone}
            given = {number: [args for _, args in calls] for number, calls in asked.items()}
            if self.strict:
                given = lax.optimization_barrier(given)
            came = {
                number: [call(*args) for (call, _), args in zip(calls, given[number])]
                for number, calls in asked.items()
            }
            if self.strict:
                came = lax.optimization_barrier(came)
            for number, results in came.items():
                self.active[number] = (self.active[number][0], results)
            self.asked = {n: calls for n, calls in self.asked.items() if n not in asked}
        values = [self.values[number] for number in wanted]
        return values[0] if len(values) == 1 else values

    def run(self, task):
        return self.until(self.start(task))

    def loosely(self, *wanted, also=None):
        self.strict, self.alone = False, None if also is None else wanted + also
        values = self.until(*wanted)
        self.strict, self.alone = True, None
        return values


def hold(count, *values):
    for _ in range(count):
        (values,) = yield [(lambda *v: v, values)]
    return values


def later(count, task):
    yield from hold(count)
    return (yield from task)


def work(function, *args):
    (result,) = yield [(function, args)]
    return result


class Links:
    def __init__(self, n):
        self.n = n
        self.planes = n // 4
        index = lax.axis_index("expert")
        self.g = lax.axis_index("dp")
        self.index = index
        self.p = index % 4
        self.l = index // 4
        self.square = n == 16
        if self.square:
            self.a = index % 2 + index // 8 * 2
            self.b = index // 2 % 2 * 2 + index // 4 % 2
        else:
            self.a, self.b = self.l, self.p
        masks = (0, 4, 2, 6) if self.square else (0, 1, 2, 3)
        self.places = [lambda v, k=k: self.flip(v, k) for k in range(4)]
        self.heads = [lambda v, m=m: self.flip(v, m) for m in masks]
        self.shifts = [lambda v, s=s: self.shift(v, s) for s in range(self.planes)]
        self.backs = [lambda v, s=s: self.shift(v, -s) for s in range(self.planes)]

    def device(self, a, b):
        if not self.square:
            return a * 4 + b
        return a % 2 + b // 2 * 2 + b % 2 * 4 + a // 2 * 8

    def row_block(self, g, a):
        return a % 2 + g * 2 + a // 2 * 4 if self.square else g * self.planes + a

    def block(self, r):
        return self.a ^ r if self.square else (self.a - r) % self.planes

    def flip(self, value, mask):
        return lax.ppermute(value, "expert", [(i, i ^ mask) for i in range(self.n)])

    def shift(self, value, step):
        return lax.ppermute(
            value, "expert", [(i, (i + step * 4) % self.n) for i in range(self.n)]
        )

    def onward(self, value):
        return self.shift(value, 1)

    def twin(self, value):
        return lax.ppermute(value, "dp", [(0, 1), (1, 0)])

    def natural(self, blocks, mine):
        odd, high = mine % 2 == 1, mine >= 2
        pair = [jnp.where(odd, blocks[q ^ 1], blocks[q]) for q in range(4)]
        return [jnp.where(high, pair[q ^ 2], pair[q]) for q in range(4)]

    def turned_line(self, blocks):
        twice = jnp.concatenate([blocks[::-1], blocks[::-1]], axis=0)
        return lax.dynamic_slice_in_dim(twice, self.planes - 1 - self.l, self.planes, 0)

    def head_gather(self, own):
        half = own.shape[0] // 2
        near_x, near_y = yield [(self.heads[1], (own,)), (self.heads[2], (own,))]
        low, high = yield [(self.heads[2], (near_x[:half],)), (self.heads[1], (near_y[half:],))]
        return jnp.concatenate([own, near_x, near_y, low, high], axis=0)

    def exchange(self, flips, blocks):
        came = yield [(flips[k], (blocks[k],)) for k in (3, 1, 2)]
        return [blocks[0], came[1], came[2], came[0]]

    def head_scatter(self, total):
        count = total.shape[0] // 4
        half = count // 2
        cut = lambda k, low, high: total[k * count + low : k * count + high]
        low, high = yield [
            (self.heads[2], (cut(3, 0, half).astype(BF),)),
            (self.heads[1], (cut(3, half, count).astype(BF),)),
        ]
        to_x = jnp.concatenate([cut(1, 0, half) + low.astype(F32), cut(1, half, count)], axis=0)
        to_y = jnp.concatenate([cut(2, 0, half), cut(2, half, count) + high.astype(F32)], axis=0)
        got_x, got_y = yield [
            (self.heads[1], (to_x.astype(BF),)),
            (self.heads[2], (to_y.astype(BF),)),
        ]
        return cut(0, 0, count) + got_x.astype(F32) + got_y.astype(F32)

    def block_gather(self, own, idle=(0, 0), count=None, give=None):
        if not self.square:
            came = yield [(shift, (own,)) for shift in self.shifts[1:]]
            return [own] + came
        x, z = (lambda v: self.flip(v, 1)), (lambda v: self.flip(v, 8))
        count = count or own.shape[0]
        half = count // 2 + own.shape[0] - count
        near, low = yield [(x, (own,)), (z, (own[:half],))]
        near, low = yield from hold(idle[0], near, low)
        rest = count - half
        more = [own[half:]] if give is None else [own[half:], near[count:]]
        high, far_low = yield [(z, (jnp.concatenate(more),)), (x, (low,))]
        high, far_low = yield from hold(idle[1], high, far_low)
        if give is not None:
            give(jnp.concatenate([own[count:], near[count:], high[rest:]]))
        (far_high,) = yield [(x, (high[:rest],))]
        return [
            own,
            near,
            jnp.concatenate([low, high[:rest]], axis=0),
            jnp.concatenate([far_low, far_high], axis=0),
        ]

    def block_gather_short(self, own):
        if not self.square:
            came = yield [(shift, (own,)) for shift in self.shifts[1:]]
            return [own] + came
        x, z = (lambda v: self.flip(v, 1)), (lambda v: self.flip(v, 8))
        near, across = yield [(x, (own,)), (z, (own,))]
        (far,) = yield [(x, (across,))]
        return [own, near, across, far]

    def block_scatter(self, blocks, split=False, idle=0):
        if not self.square:
            came = yield [
                (back, (block.astype(BF),)) for back, block in zip(self.backs[1:], blocks[1:])
            ]
            return sum((block.astype(F32) for block in came), blocks[0].astype(F32))
        x, z = (lambda v: self.flip(v, 1)), (lambda v: self.flip(v, 8))
        (came,) = yield [(x, (blocks[3].astype(BF),))]
        (came,) = yield from hold(idle, came)
        across = (blocks[2].astype(F32) + came.astype(F32)).astype(BF)
        if split:
            half = across.shape[0] // 2
            (got,) = yield [(z, (across[:half],))]
            near, more = yield [(x, (blocks[1].astype(BF),)), (z, (across[half:],))]
            got = jnp.concatenate([got, more], axis=0)
        else:
            near, got = yield [(x, (blocks[1].astype(BF),)), (z, (across,))]
        return blocks[0].astype(F32) + near.astype(F32) + got.astype(F32)

    def twin_scatter(self, make, own, other, idle=None, now=False, rest=0):
        low = lambda *args: make(*args).astype(BF)
        if now:
            block = low(*other)
        else:
            (block,) = yield [(low, other)]
            (block,) = yield from hold(rest, block)
        if idle is None:
            came, total = yield [(self.twin, (block,)), (make, own)]
            return total + came.astype(F32)
        (came,) = yield [(self.twin, (block,))]
        (came,) = yield from hold(idle, came)
        (total,) = yield [(lambda came, *args: make(*args) + came.astype(F32), (came, *own))]
        return total


def body(
    hidden,
    lengths,
    slots,
    routes,
    order,
    gain_in,
    w_query,
    key_projection_weight,
    value_projection_weight,
    gain_q,
    gain_k,
    w_out,
    gain_mid,
    w_router,
    w_gate,
    w_up,
    w_down,
    cotangent,
):
    tokens = hidden.shape[0]
    experts = w_router.shape[1]
    links = Links(experts)
    planes = links.planes
    capacity = max(2, (tokens * TOP * 9 + 8 * experts - 1) // (8 * experts))
    block_tokens = 4 * tokens
    rows = gain_in.shape[0]
    head_part = gain_q.shape[0]
    devices = 2 * experts

    rounds = Rounds()
    spread = rounds.start
    slot_count = 4 * capacity

    gate_full = lax.all_gather(w_gate, "dp", axis=1, tiled=True)[0]
    up_full = lax.all_gather(w_up, "dp", axis=1, tiled=True)[0]
    down_full = lax.all_gather(w_down, "dp", axis=2, tiled=True)[0]

    lanes = 128
    gains = jnp.concatenate([gain_in, gain_mid, gain_q, gain_k], axis=0)
    gain_count = gains.shape[0]
    gains = jnp.pad(gains, (0, -gain_count % lanes)).reshape(-1, lanes)
    router_rows = rows * experts // lanes
    small = jnp.concatenate([w_router.reshape(-1, lanes), gains], axis=0)
    small = jnp.pad(small, ((0, -small.shape[0] % 8), (0, 0)))
    small_rows = small.shape[0]
    pairs = jnp.concatenate([part.T.astype(BF) for part in (routes, order // 32, order % 32)])
    expert_numbers = jnp.arange(experts, dtype=jnp.int32)
    ids = jnp.stack([links.l, links.p]).astype(jnp.int32)
    tables = {}

    qkv_width = QW + 2 * HEAD_SIZE
    rider = jnp.concatenate([small, pairs], axis=0)
    rider_rows = rider.shape[0]

    def own_columns(b):
        cut = lambda array, width: lax.dynamic_slice_in_dim(array, b * width, width, 1)
        return jnp.concatenate(
            [
                cut(w_query, QW),
                cut(key_projection_weight, HEAD_SIZE),
                cut(value_projection_weight, HEAD_SIZE),
            ],
            axis=1,
        )

    def gather_qkv():
        blocks = [own_columns(links.b ^ k) for k in range(4)]
        if not links.square:
            blocks = yield from links.exchange(links.heads, blocks)
            pieces = yield from links.block_gather(jnp.concatenate(blocks, axis=0))
            others = yield [(links.twin, (piece,)) for piece in pieces]
            return pieces + others
        more = rider.reshape(-1, qkv_width)
        held = more.shape[0]
        more = jnp.pad(more, ((0, -held % 8), (0, 0)))
        blocks = [jnp.concatenate([block, more], axis=0) for block in blocks]
        blocks = yield from links.exchange(links.heads, blocks)
        wide = stack_rows(blocks, rows)

        def give(found):
            found = found.reshape(4, 4, -1, qkv_width)[:, :, :held]
            tables["riders"] = found.reshape(4, 4, rider_rows, lanes)

        pieces = yield from links.block_gather(wide, count=4 * rows, give=give)
        others = yield [(links.twin, (piece,)) for piece in pieces]
        return pieces + others

    def gather_small():
        if links.square:
            yield from hold(3)
            parts = tables["riders"]
            parts = jnp.stack(links.natural([parts[r] for r in range(4)], links.a))
            parts = jnp.stack(links.natural([parts[:, k] for k in range(4)], links.b), axis=1)
            parts = parts.reshape(2, 2, 2, 2, rider_rows, lanes).transpose(0, 3, 2, 1, 4, 5)
            parts = parts.reshape(experts, rider_rows, lanes)
        else:
            blocks = yield from links.exchange(links.places, [rider] * 4)
            line = jnp.stack(links.natural(blocks, links.p))
            came = yield [(shift, (line,)) for shift in links.shifts[1:]]
            parts = links.turned_line(jnp.stack([line] + came))
            parts = parts.reshape(experts, rider_rows, lanes)
            yield from hold(1)
        own_small = parts[:, :small_rows]
        (other_small,) = yield [(links.twin, (own_small,))]
        tables["pairs"] = parts[:, small_rows:]
        return (yield from work(sort_small, own_small, other_small, rounds.values[hidden_task]))

    def sort_small(own_small, other_small, block_hidden):
        swap = links.g == 1
        small_all = jnp.concatenate(
            [jnp.where(swap, other_small, own_small), jnp.where(swap, own_small, other_small)]
        )
        gains = small_all[:, router_rows:].reshape(devices, -1)
        head_gains = gains[:, 2 * rows : gain_count].reshape(devices, 2, head_part)
        values = block_hidden.astype(F32)
        scale = lax.rsqrt(jnp.mean(values * values, axis=-1, keepdims=True) + EPS)
        full_in = gains[:, :rows].reshape(MODEL_WIDTH).astype(F32)
        return (
            (values * scale * full_in).astype(BF),
            small_all[:, :router_rows].reshape(MODEL_WIDTH, experts),
            full_in,
            gains[:, rows : 2 * rows].reshape(MODEL_WIDTH).astype(F32),
            head_gains.swapaxes(0, 1).reshape(2, HEAD_SIZE).astype(F32),
        )

    def make_tables(pairs):
        pairs = pairs.astype(F32).reshape(planes, 4, 3, TOP, tokens)
        pairs = links.turned_line(pairs)
        near = [lax.dynamic_index_in_dim(pairs, links.p ^ k, 1, keepdims=False) for k in range(4)]
        return slot_tables(ids, jnp.stack(near, axis=1), capacity, experts)

    exchange_task = spread(hold(1))
    qkv_task = spread(gather_qkv())

    def gather_hidden():
        (value,) = yield from hold(1, hidden)
        return (yield from links.head_gather(value))

    hidden_task = spread(gather_hidden())
    small_task = spread(gather_small())

    aligned = capacity % 8 == 0

    def choose(piece, step, backs=()):
        found = choose_rows(tables["send"][step], piece, 4 if aligned else 1, as_blocks(backs))
        return found if aligned else by_place(found[0])

    def by_place(slot_rows):
        return [slot_rows[k * capacity : (k + 1) * capacity] for k in range(4)]

    def as_blocks(blocks):
        return blocks if aligned or not blocks else [jnp.concatenate(blocks, axis=0)]

    def collect(blocks, step, width, more=None, kind=BF):
        return collect_rows(tables["back"][step], as_blocks(blocks), width, more, kind)

    def in_places(own, came):
        return [own, came[0], came[1], came[2]]

    def to_places(blocks):
        return [(links.places[k], (blocks[k],)) for k in (1, 2, 3)]

    def gather_upstream():
        pieces, out = [cotangent], []
        yield from hold(2)
        found = yield from work(make_tables, tables["pairs"])
        tables["send"], tables["back"], tables["chooser"] = found
        plan = [(1, True, 0)] + [(0, s < planes - 1, s) for s in range(1, planes)]
        for idle, hop, step in plan:
            yield from hold(idle)
            asks = [(links.onward, (pieces[-1],))] if hop else []
            if step is not None:
                blocks = choose(pieces[step], step)
                asks += to_places(blocks)
            came = yield asks
            if hop:
                pieces.append(came[0])
            if step is not None:
                out.append(jnp.concatenate([blocks[0]] + came[-3:], axis=0))
        return out

    upstream_task = spread(gather_upstream())

    head_rows = w_out.shape[0]
    if links.square:
        pairs_of = [(g, i) for g in range(2) for i in range(experts)]
        line = lambda i: i & 3 | (i >> 3 & 1) << 2 | (i >> 2 & 1) << 3
        swap_line = [(g * experts + i, g * experts + line(i)) for g, i in pairs_of]
        swap_core = [
            (g * experts + i, (i >> 1 & 1) * experts + (i & 13 | g << 1)) for g, i in pairs_of
        ]
        bit = lambda k: links.index // (1 << k) % 2
        moves = bit(2) != bit(3), bit(1) != links.g
        back = ((swap_line, moves[0]), (swap_core, moves[1]))
        onto = dict(swap_core)
        there = ([(i, onto[j]) for i, j in swap_line], moves[0] | moves[1])
    else:
        to_block = [
            (b * 2 * planes + links.row_block(g, a), g * experts + links.device(a, b))
            for g in range(2)
            for a in range(planes)
            for b in range(4)
        ]
        there = (to_block, True)
        back = (([(to, of) for of, to in to_block], True), None)

    def moved(value, swap):
        if swap is None:
            return value
        pairs_of, moves = swap
        if moves is True:
            return lax.ppermute(value, ("dp", "expert"), pairs_of)
        came = lax.ppermute(value, ("dp", "expert"), [(i, j) for i, j in pairs_of if i != j])
        return jnp.where(moves, came, value)

    def gather_out():
        pieces = yield from links.block_gather(rounds.values[move_task], (1, 0))
        pieces = jnp.concatenate(pieces, axis=0)
        (others,) = yield [(links.twin, (pieces,))]
        return pieces, others

    move_task = spread(work(lambda value: moved(value, there), w_out))

    device_of = jnp.stack(
        [links.device(links.block(r), links.b ^ k) for r in range(planes) for k in range(4)]
    )
    starts = jnp.concatenate([(links.g ^ t) * experts + device_of for t in range(2)]) * rows
    all_slots = slots.reshape(experts, tokens)[device_of].reshape(experts * tokens)
    _, position = places(all_slots[:block_tokens], lengths[0])
    cosine, sine = rotary_tables(position)
    high = all_slots[:block_tokens]
    low = high - position

    rounds.until(exchange_task)
    found, block_hidden, qkv_pieces, _ = rounds.loosely(
        small_task, hidden_task, qkv_task, move_task, also=()
    )
    out_task = spread(gather_out())
    normalized, full_router, full_in, full_mid, head_gains = found
    w_qkv, projected, turned = rounds.run(
        work(
            lambda *args: project(rows, *args),
            starts,
            normalized,
            cosine,
            sine,
            head_gains,
            *qkv_pieces,
        )
    )
    keys_values = jnp.concatenate(
        rounds.run(links.block_gather_short(turned[:, QW:])), axis=0
    )
    keys_turned = keys_values[:, :HEAD_SIZE].T
    values_turned = keys_values[:, HEAD_SIZE:].T
    place_column = all_slots[:, None]
    low, high = low[None, :], high[None, :]

    def part_of(array, part, parts):
        width = array.shape[1] // parts
        return array[:, part * width : (part + 1) * width]

    def forward_part(query_rows):
        return attention_forward(query_rows, keys_values, values_turned, place_column, low, high)

    bounds = [0, PER_KV // 2, PER_KV]
    attended = [
        rounds.run(work(forward_part, turned[:, low_head * HEAD_SIZE : high_head * HEAD_SIZE]))
        for low_head, high_head in zip(bounds, bounds[1:])
    ]
    block_out = rounds.until(out_task)
    if head_rows == HEAD_SIZE:
        order_of = [
            links.row_block(links.g ^ t, links.block(r)) for t in range(2) for r in range(planes)
        ]
        order_of = jnp.stack(order_of).astype(jnp.int32)
    else:
        attended = jnp.concatenate(attended, axis=1)
        attended = [
            lax.dynamic_slice_in_dim(
                attended, links.row_block(links.g ^ t, links.block(r)) * head_rows, head_rows, 1
            )
            for t in range(2)
            for r in range(planes)
        ]
        attended = [jnp.concatenate(attended, axis=1)]
        order_of = jnp.arange(PER_KV, dtype=jnp.int32)
    branch, attended = rounds.run(
        work(lambda *parts: output_projection(order_of, parts, *block_out), *attended)
    )
    branch = rounds.loosely(spread(links.head_scatter(branch)))
    x_float = hidden.astype(F32)
    x_one = x_float + branch
    norm_two, norm_two_back = jax.vjp(rms_scale, x_one, full_mid)
    xn_two = norm_two.astype(BF)

    own_chooser = jnp.any(routes[:, :, None] == expert_numbers, axis=1)

    def masked_softmax(logits, chooser):
        top = jnp.max(jnp.where(chooser, logits, MASKED), axis=-1, keepdims=True)
        exponent = jnp.where(chooser, jnp.exp(jnp.where(chooser, logits - top, 0.0)), 0.0)
        total = jnp.sum(exponent, axis=-1, keepdims=True)
        return exponent / jnp.where(total > 0.0, total, 1.0)

    upstream_slots = rounds.until(upstream_task)
    me = links.index.astype(jnp.int32)[None]
    made = []

    def expert_step(step, *rows_in):
        found = expert_rows(
            me,
            as_blocks(list(rows_in)),
            upstream_slots[step],
            tables["chooser"][step],
            full_router,
            gate_full,
            up_full,
            down_full,
        )
        if aligned:
            return (found[:4], found[4:8], found[8:])
        return (by_place(found[0]), by_place(found[1]), found[2:])

    def return_mixture():
        def add(step, came, back, kind=BF):
            blocks = in_places(made[step][1][0], back)
            return collect(blocks, step, MODEL_WIDTH, came, kind)

        back = yield to_places(made[1][1])
        total = add(1, None, back)
        yield from hold(2)
        came, *back = yield [(links.onward, (total,))] + to_places(made[2][1])
        total = add(2, came, back)
        for step in range(3, planes):
            came, *back = yield [(links.onward, (total,))] + to_places(made[step][1])
            total = add(step, came, back)
        came, *back = yield [(links.onward, (total,))] + to_places(made[0][1])
        return add(0, came, back, F32)

    def experts_there_and_back():
        piece, ready, own_plane, total = xn_two, None, None, None
        wide = MODEL_WIDTH + lanes
        for step in range(planes + 3):
            asks = []
            back = made[step - 2][0] if 2 <= step < planes + 2 else []
            blocks = back
            if step < planes:
                blocks = choose(piece, step, back)
            if blocks:
                asks += to_places(blocks)
            if step < planes - 1:
                asks += [(links.onward, (piece,))]
            if step >= 4:
                asks += [(links.onward, (total,))]
            if 1 <= step <= planes:
                asks += [(lambda *v, s=step - 1: expert_step(s, *v), tuple(ready))]
            if step == planes + 2:
                tables["mixture"] = spread(return_mixture())
            came = yield asks
            if blocks:
                ready, came = in_places(blocks[0], came[:3]), came[3:]
            if step < planes - 1:
                piece, came = came[0], came[1:]
            if step >= 4:
                hop, came = came[0], came[1:]
            if 1 <= step <= planes:
                made.append(came[0])
            if step == 2:
                own_plane = collect(ready, 0, wide, None, F32)
            elif step == 3:
                total = collect(ready, 1, wide)
            elif step >= 4 and step < planes + 2:
                total = collect(ready, step - 2, wide, hop)
        return own_plane + hop.astype(F32)

    moe_grad = rounds.run(experts_there_and_back())
    gate_grads = moe_grad[:, MODEL_WIDTH : MODEL_WIDTH + experts]
    moe_grad = moe_grad[:, :MODEL_WIDTH]
    stacked = lambda place: jnp.concatenate([piece[2][place] for piece in made], axis=0)

    def by_rows(rows_in, grads_in):
        return jnp.einsum("rd,rf->df", rows_in, grads_in, preferred_element_type=F32)

    half_width = MODEL_WIDTH // 2

    def half_of(array, which):
        return lax.dynamic_slice_in_dim(array, which * half_width, half_width, 1)

    def gate_up_gradient(place, idle, rest):
        rows_in, grads_in = stacked(0), stacked(place)
        make = lambda which: by_rows(half_of(rows_in, which), grads_in)
        return links.twin_scatter(make, (links.g,), (1 - links.g,), idle=idle, rest=rest)

    def down_gradient():
        rows_in, grads_in = stacked(1), stacked(2)
        make = lambda which: by_rows(rows_in, half_of(grads_in, which))
        return links.twin_scatter(make, (links.g,), (1 - links.g,), idle=2)

    gate_task = spread(gate_up_gradient(3, 5, 0))
    up_task = spread(later(1, gate_up_gradient(4, 2, 3)))
    down_task = spread(later(5, down_gradient()))

    def route(rows_in):
        logits = jnp.dot(rows_in, full_router, preferred_element_type=F32)
        return masked_softmax(logits, own_chooser)

    own_probs = route(lax.optimization_barrier((xn_two, moe_grad))[0])

    upstream = cotangent.astype(F32)
    chosen_grad = own_probs * (
        gate_grads - jnp.sum(own_probs * gate_grads, axis=-1, keepdims=True)
    )
    logit_grad = chosen_grad.astype(BF)
    xn_two_grad = moe_grad + jnp.dot(logit_grad, full_router.T, preferred_element_type=F32)
    x_one_norm_grad, grad_mid = norm_two_back(xn_two_grad)
    x_one_grad = upstream + x_one_norm_grad
    branch_grad = x_one_grad.astype(BF)

    block_grad = rounds.loosely(spread(links.head_gather(branch_grad)))

    def head_gradients(block_grad):
        grad = [
            jnp.einsum("td,hd->th", block_grad, part, preferred_element_type=F32).astype(BF)
            for part in block_out
        ]
        grad = jnp.concatenate(grad, axis=1)
        parts = []
        where = {links.row_block(g, a): (g, a) for g in range(2) for a in range(planes)}
        for head in range(2 * planes):
            g, a = where[head]
            at = ((links.g ^ g) * planes + links.block(a)) * head_rows
            parts.append(lax.dynamic_slice_in_dim(grad, at, head_rows, 1))
        return jnp.concatenate(parts, axis=1)

    heads_task = spread(work(head_gradients, block_grad))

    def scatter_out():
        half = QW // 2
        grad = yield from links.twin_scatter(
            lambda rows_in, grads_in: jnp.einsum(
                "th,td->hd", rows_in, grads_in, preferred_element_type=F32
            ),
            (attended[:, :half], block_grad),
            (attended[:, half:], block_grad),
            now=True,
        )
        grad = grad.astype(BF)
        blocks = [grad[r * head_rows : (r + 1) * head_rows] for r in range(planes)]
        grad = yield from links.block_scatter(blocks, split=True)
        yield from hold(1)
        grad = yield from work(lambda value: moved(value, back[1]), grad.astype(BF))
        (grad,) = yield from hold(2, grad)
        return (yield from work(lambda value: moved(value, back[0]), grad))

    grad_out_task = spread(scatter_out())

    def owners_blocks(grad):
        blocks = []
        for r in range(planes):
            owners = [links.device(links.block(r), links.b ^ k) for k in range(4)]
            parts = [lax.dynamic_slice_in_dim(grad, owner * rows, rows, 0) for owner in owners]
            blocks.append(jnp.concatenate(parts, axis=0))
        return blocks

    def half_rows(array, which):
        return lax.dynamic_slice_in_dim(array, which * (MODEL_WIDTH // 2), MODEL_WIDTH // 2, 0)

    def query_gradient(grads_in, extra):
        def make(which):
            grad = by_rows(half_of(normalized, which), grads_in)
            if extra is not None:
                grad = jnp.concatenate([grad, half_rows(extra, which)], axis=1)
            return grad

        grad = yield from links.twin_scatter(make, (links.g,), (1 - links.g,))
        grad = yield from links.block_scatter(owners_blocks(grad.astype(BF)))
        return grad.astype(BF)

    def key_value_gradient(key_value_grad, proj_grad):
        sums = jnp.concatenate([grad_qgain, grad_kgain]).reshape(2, devices, head_part)
        sums = jnp.pad(sums, ((0, 0), (0, 0), (0, rows - head_part))).reshape(2, MODEL_WIDTH).T
        sums = jnp.pad(sums, ((0, 0), (0, lanes - sums.shape[1])))

        def half(which):
            grad = by_rows(half_of(normalized, which), key_value_grad)
            return jnp.concatenate([grad, half_rows(sums, which)], axis=1)

        came, xn_one_grad = yield [
            (links.twin, (half(1 - links.g).astype(BF),)),
            (lambda proj_grad: input_gradient(proj_grad, w_qkv), (proj_grad,)),
        ]
        tables["scatter"] = spread(links.head_scatter(xn_one_grad))
        grad = (half(links.g) + came.astype(F32)).astype(BF)
        grad = yield from links.block_scatter(owners_blocks(grad))
        return grad.astype(BF)

    attended_grad = rounds.until(heads_task)
    grad_router = jnp.dot(xn_two.T, logit_grad, preferred_element_type=F32)
    first = jnp.concatenate([grad_router, grad_mid[:, None]], axis=1)
    first = jnp.pad(first, ((0, 0), (0, lanes - first.shape[1])))
    query_low_grads, query_tasks, key_terms, grad_qgain = [], [], None, None

    parts = 2
    for part in range(parts):
        got = rounds.run(
            work(
                lambda *args: attention_backward(
                    *args,
                    keys_values,
                    keys_turned,
                    place_column,
                    low,
                    high,
                    cosine,
                    sine,
                    head_gains[0:1],
                ),
                part_of(turned[:, :QW], part, parts),
                part_of(attended_grad, part, parts),
                part_of(projected[:, :QW], part, parts),
            )
        )
        query_low_grads.append(got[0])
        key_terms = got[1] if part == 0 else key_terms + got[1]
        grad_qgain = got[2] if part == 0 else grad_qgain + got[2]
        query_tasks.append(spread(query_gradient(got[0], None if part else first)))
    key_terms = rounds.run(
        links.block_scatter(
            [key_terms[r * block_tokens : (r + 1) * block_tokens] for r in range(planes)]
        )
    )

    key_proj_grad, grad_kgain = unturn(
        key_terms[:, :HEAD_SIZE],
        projected[:, QW : QW + HEAD_SIZE],
        cosine,
        sine,
        head_gains[1:2],
    )
    key_value_grad = jnp.concatenate([key_proj_grad, key_terms[:, HEAD_SIZE:].astype(BF)], axis=1)
    proj_grad = jnp.concatenate(query_low_grads + [key_value_grad], axis=1)
    key_value_task = spread(key_value_gradient(key_value_grad, proj_grad))
    one, two, three = rounds.until(*query_tasks, key_value_task)
    xn_one_grad = rounds.until(tables["scatter"])
    query_task = spread(links.exchange(links.heads, pack_rows(one, two, three)))
    _, norm_one_back = jax.vjp(lambda values: rms_scale(values, full_in), x_float)
    (x_norm_grad,) = norm_one_back(xn_one_grad)
    input_grad = (x_one_grad + x_norm_grad).astype(BF)

    grad_gate, grad_up, grad_down, mixture, grad_out, owned = rounds.until(
        gate_task, up_task, down_task, tables["mixture"], grad_out_task, query_task
    )
    result = (x_one + mixture).astype(BF)
    weights = (w_query, key_projection_weight, value_projection_weight)
    found = finish(
        links.b, owned, gain_in.astype(F32)[None], grad_out, experts, head_part, *weights
    )
    grad_query, grad_key, grad_value, grad_router, grad_out = found[:5]
    grad_mid, grad_in, grad_qgain, grad_kgain = (row.reshape(-1) for row in found[5:])

    return (
        result,
        input_grad,
        grad_in,
        grad_query,
        grad_key,
        grad_value,
        grad_qgain,
        grad_kgain,
        grad_out,
        grad_mid,
        grad_router,
        grad_gate[None],
        grad_up[None],
        grad_down[None],
    )


def solution(mesh):
    every = ("dp", "expert")
    in_specs = (
        P(every, None),
        P("dp", None),
        P("dp"),
        P(every, None),
        P(every, None),
        P(every),
        P(every, None),
        P(every, None),
        P(every, None),
        P(every),
        P(every),
        P(every, None),
        P(every),
        P(every, None),
        P("expert", "dp", None),
        P("expert", "dp", None),
        P("expert", None, "dp"),
        P(every, None),
    )
    out_specs = (
        P(every, None),
        P(every, None),
        P(every),
        P(every, None),
        P(every, None),
        P(every, None),
        P(every),
        P(every),
        P(every, None),
        P(every),
        P(every, None),
        P("expert", "dp", None),
        P("expert", "dp", None),
        P("expert", None, "dp"),
    )
    return jax.shard_map(body, mesh=mesh, in_specs=in_specs, out_specs=out_specs, check_vma=False)
```

```python
import math

import jax
import jax.numpy as jnp
from jax import lax
from jax.experimental import pallas as pl
from jax.experimental.pallas import tpu as pltpu
from jax.sharding import PartitionSpec as P

MODEL_WIDTH = 2048
QUERY_HEADS = 32
KEY_VALUE_HEADS = 4
HEAD_SIZE = 128
TOP = 8
PER_KV = QUERY_HEADS // KEY_VALUE_HEADS
QW = PER_KV * HEAD_SIZE

EPS = 1e-06
THETA = 1000000.0
MASKED = -1e30
KEY_STEP = 1024
EXPONENT = HEAD_SIZE**-0.5 / math.log(2.0)
BF = jnp.bfloat16
F32 = jnp.float32


def rms_scale(values, scaling):
    return values * lax.rsqrt(jnp.mean(values * values, axis=-1, keepdims=True) + EPS) * scaling


def rotary_tables(position):
    half = HEAD_SIZE // 2
    index_float = jnp.arange(half, dtype=jnp.float32)
    freq = jnp.power(jnp.float32(THETA), -2.0 * index_float / HEAD_SIZE)
    angle = position.astype(jnp.float32)[:, None] * freq[None, :]
    cosine, sine = jnp.cos(angle), jnp.sin(angle)
    return (
        jnp.concatenate([cosine, cosine], axis=-1),
        jnp.concatenate([-sine, sine], axis=-1),
    )


def stack_kernel(rows, *refs):
    *block_refs, out_ref = refs
    blocks = [ref[...].astype(F32) for ref in block_refs]
    stack = [block[:rows] for block in blocks] + [block[rows:] for block in blocks]
    out_ref[...] = jnp.concatenate(stack, axis=0).astype(BF)


def stack_rows(blocks, rows):
    height, width = blocks[0].shape
    return pl.pallas_call(
        lambda *refs: stack_kernel(rows, *refs),
        out_shape=jax.ShapeDtypeStruct((height * len(blocks), width), BF),
    )(*blocks)


def project_kernel(starts_ref, x_ref, cos_ref, sin_ref, gains_ref, *refs):
    pieces, (w_ref, proj_ref, turned_ref) = refs[:-3], refs[-3:]
    last = pl.program_id(0) == pl.num_programs(0) - 1
    rows = pieces[0].shape[0] // 4
    for number, piece in enumerate(pieces):
        for k in range(4):
            at = pl.multiple_of(starts_ref[number * 4 + k], rows)
            w_ref[pl.ds(at, rows), :] = piece[k * rows : (k + 1) * rows, :]
    projected = jnp.dot(x_ref[...], w_ref[...], preferred_element_type=F32)
    proj_ref[...] = projected

    def turn(values, gain):
        scaled = (
            values * lax.rsqrt(jnp.mean(values * values, axis=-1, keepdims=True) + EPS) * gain
        )
        swapped = pltpu.roll(scaled, HEAD_SIZE // 2, 1)
        return scaled * cos_ref[...] + swapped * sin_ref[...]

    gain_q, gain_k = gains_ref[0:1], gains_ref[1:2]
    first, second = projected[:, :HEAD_SIZE], projected[:, HEAD_SIZE:]
    turned_ref[:, :HEAD_SIZE] = turn(first, jnp.where(last, gain_k, gain_q)).astype(BF)
    turned_ref[:, HEAD_SIZE:] = jnp.where(last, second, turn(second, gain_q)).astype(BF)


def project(rows, starts, rows_in, cosine, sine, gains, *pieces):
    count, width = rows_in.shape
    height, columns = 4 * rows, pieces[0].shape[1]
    step = 2 * HEAD_SIZE
    whole = lambda array: pl.BlockSpec(array.shape, lambda i: (0, 0))
    strip = lambda height: pl.BlockSpec((height, step), lambda i: (0, i))
    return pl.pallas_call(
        project_kernel,
        grid=(columns // step,),
        in_specs=[pl.BlockSpec(memory_space=pltpu.SMEM)]
        + [whole(rows_in), whole(cosine), whole(sine), whole(gains)]
        + [strip(height)] * len(pieces),
        out_specs=[strip(width), strip(count), strip(count)],
        out_shape=[
            jax.ShapeDtypeStruct((width, columns), BF),
            jax.ShapeDtypeStruct((count, columns), F32),
            jax.ShapeDtypeStruct((count, columns), BF),
        ],
        cost_estimate=pl.CostEstimate(
            flops=2 * count * width * columns,
            bytes_accessed=2 * (count + columns) * width,
            transcendentals=0,
        ),
        compiler_params=pltpu.CompilerParams(vmem_limit_bytes=60 * 2**20),
    )(starts, rows_in, cosine, sine, gains, *pieces)


def unturned(grad, values, cosine, sine, gain):
    grad = grad * cosine + pltpu.roll(grad * sine, HEAD_SIZE // 2, 1)
    scale = lax.rsqrt(jnp.mean(values * values, axis=-1, keepdims=True) + EPS)
    gain_grad = jnp.sum(grad * values * scale, axis=0, keepdims=True)
    grad = grad * gain
    inner = jnp.mean(grad * values, axis=-1, keepdims=True)
    return (scale * grad - values * (scale * scale * scale * inner)).astype(BF), gain_grad


def unturn_kernel(grad_ref, proj_ref, cos_ref, sin_ref, gain_ref, out_ref, gain_grad_ref):
    out_ref[...], gain_grad_ref[...] = unturned(
        grad_ref[...], proj_ref[...], cos_ref[...], sin_ref[...], gain_ref[...]
    )


def unturn(grad, projected, cosine, sine, gain):
    return pl.pallas_call(
        unturn_kernel,
        out_shape=[
            jax.ShapeDtypeStruct(grad.shape, BF),
            jax.ShapeDtypeStruct(gain.shape, F32),
        ],
    )(grad, projected, cosine, sine, gain)


def input_kernel(grad_ref, w_ref, out_ref):
    dims = (((1,), (1,)), ((), ()))
    out_ref[...] = lax.dot_general(grad_ref[...], w_ref[...], dims, preferred_element_type=F32)


def input_gradient(proj_grad, weights):
    count, columns = proj_grad.shape
    width = weights.shape[0]
    step = 256
    return pl.pallas_call(
        input_kernel,
        grid=(width // step,),
        in_specs=[
            pl.BlockSpec((count, columns), lambda i: (0, 0)),
            pl.BlockSpec((step, columns), lambda i: (i, 0)),
        ],
        out_specs=pl.BlockSpec((count, step), lambda i: (0, i)),
        out_shape=jax.ShapeDtypeStruct((count, width), F32),
        cost_estimate=pl.CostEstimate(
            flops=2 * count * width * columns,
            bytes_accessed=6 * (count + columns) * width,
            transcendentals=0,
        ),
        compiler_params=pltpu.CompilerParams(vmem_limit_bytes=24 * 2**20),
    )(proj_grad, weights)


def output_kernel(order_ref, *refs):
    *part_refs, own_ref, other_ref, out_ref, rows_ref, natural_ref = refs
    half = own_ref.shape[0]

    @pl.when(pl.program_id(0) == 0)
    def _():
        at = 0
        for part_ref in part_refs:
            width = part_ref.shape[1]
            natural_ref[:, at : at + width] = part_ref[...]
            at += width
        for head in range(at // HEAD_SIZE):
            start = pl.multiple_of(order_ref[head] * HEAD_SIZE, HEAD_SIZE)
            here = slice(head * HEAD_SIZE, (head + 1) * HEAD_SIZE)
            rows_ref[:, here] = natural_ref[:, pl.ds(start, HEAD_SIZE)]

    out_ref[...] = jnp.dot(
        rows_ref[:, :half], own_ref[...], preferred_element_type=F32
    ) + jnp.dot(rows_ref[:, half:], other_ref[...], preferred_element_type=F32)


def output_projection(order, parts, own, other):
    count = parts[0].shape[0]
    half, width = own.shape
    columns = 2 * half
    step = 256
    strip = lambda height: pl.BlockSpec((height, step), lambda i: (0, i))
    whole = lambda shape: pl.BlockSpec(shape, lambda i: (0, 0))
    return pl.pallas_call(
        output_kernel,
        grid=(width // step,),
        in_specs=[pl.BlockSpec(memory_space=pltpu.SMEM)]
        + [whole(part.shape) for part in parts]
        + [strip(half), strip(half)],
        out_specs=[strip(count), whole((count, columns))],
        out_shape=[
            jax.ShapeDtypeStruct((count, width), F32),
            jax.ShapeDtypeStruct((count, columns), BF),
        ],
        scratch_shapes=[pltpu.VMEM((count, columns), BF)],
        cost_estimate=pl.CostEstimate(
            flops=2 * count * width * columns,
            bytes_accessed=4 * (count + columns) * width,
            transcendentals=0,
        ),
        compiler_params=pltpu.CompilerParams(vmem_limit_bytes=24 * 2**20),
    )(order, *parts, own, other)


def fill_bias(place_ref, low_ref, high_ref, bias_ref):
    step = min(KEY_STEP, bias_ref.shape[0])

    def fill(i, carry):
        at = pl.ds(pl.multiple_of(i * step, step), step)
        place = place_ref[at, :]
        seen = (place >= low_ref[...]) & (place <= high_ref[...])
        bias_ref[at, :] = jnp.where(seen, 0.0, MASKED)
        return carry

    lax.fori_loop(0, bias_ref.shape[0] // step, fill, 0)


def forward_kernel(
    q_ref, kv_ref, vt_ref, place_ref, low_ref, high_ref, out_ref, p_ref, bias_ref, sum_ref
):
    count, queries = p_ref.shape
    step = min(KEY_STEP, count)
    part = lambda i: pl.ds(pl.multiple_of(i * step, step), step)
    q = q_ref[...]

    @pl.when((pl.program_id(0) == 0) | (pl.num_programs(1) > 1))
    def _():
        fill_bias(place_ref, low_ref, high_ref, bias_ref)

    def score(i, top):
        scores = lax.dot_general(
            kv_ref[part(i), :HEAD_SIZE], q, (((1,), (1,)), ((), ())), preferred_element_type=F32
        )
        scores = scores + bias_ref[part(i), :]
        p_ref[part(i), :] = scores
        return jnp.maximum(top, jnp.max(scores, axis=0, keepdims=True))

    top = lax.fori_loop(0, count // step, score, jnp.full((1, queries), MASKED, F32))

    def lift(i, total):
        exponent = jnp.exp2((p_ref[part(i), :] - top) * EXPONENT)
        p_ref[part(i), :] = exponent
        return total + jnp.sum(exponent, axis=0, keepdims=True)

    total = lax.fori_loop(0, count // step, lift, jnp.zeros((1, queries), F32))
    share = 1.0 / total
    sum_ref[...] = jnp.zeros_like(sum_ref)

    def mix(i, carry):
        probs = (p_ref[part(i), :] * share).astype(BF)
        sum_ref[...] += jnp.dot(vt_ref[:, part(i)], probs, preferred_element_type=F32)
        return carry

    lax.fori_loop(0, count // step, mix, 0)
    out_ref[...] = sum_ref[...].T.astype(BF)


def attention_blocks(rows, count):
    step = min(rows, 512 * 2048 // count)
    whole = lambda array: pl.BlockSpec(array.shape, lambda i, j: (0, 0))
    head = pl.BlockSpec((step, HEAD_SIZE), lambda i, j: (j, i))
    along = pl.BlockSpec((1, step), lambda i, j: (0, j))
    down = pl.BlockSpec((step, HEAD_SIZE), lambda i, j: (j, 0))
    limit = (32 if count <= 2048 else 60) * 2**20
    return step, whole, head, along, down, limit


def attention_forward(q, keys_values, values_turned, place, low, high):
    rows, columns = q.shape
    count = keys_values.shape[0]
    step, whole, head, along, _, limit = attention_blocks(rows, count)
    return pl.pallas_call(
        forward_kernel,
        grid=(columns // HEAD_SIZE, rows // step),
        in_specs=[head, whole(keys_values), whole(values_turned), whole(place), along, along],
        out_specs=head,
        out_shape=jax.ShapeDtypeStruct(q.shape, BF),
        scratch_shapes=[pltpu.VMEM((count, step), F32)] * 2
        + [pltpu.VMEM((HEAD_SIZE, step), F32)],
        cost_estimate=pl.CostEstimate(
            flops=8 * rows * columns * count, bytes_accessed=4 * rows * columns, transcendentals=0
        ),
        compiler_params=pltpu.CompilerParams(vmem_limit_bytes=limit),
    )(q, keys_values, values_turned, place, low, high)


def backward_kernel(
    q_ref, grad_ref, proj_ref, kv_ref, kt_ref, place_ref, low_ref, high_ref, cos_ref, sin_ref,
    gain_ref, out_ref, dkv_ref, gain_grad_ref, p_ref, dp_ref, bias_ref, dq_ref,
):
    @pl.when((pl.program_id(0) == 0) & (pl.program_id(1) == 0))
    def _():
        dkv_ref[...] = jnp.zeros_like(dkv_ref)
        gain_grad_ref[...] = jnp.zeros_like(gain_grad_ref)

    @pl.when((pl.program_id(0) == 0) | (pl.num_programs(1) > 1))
    def _():
        fill_bias(place_ref, low_ref, high_ref, bias_ref)

    count, queries = p_ref.shape
    step = min(KEY_STEP, count)
    part = lambda i: pl.ds(pl.multiple_of(i * step, step), step)
    scale = HEAD_SIZE**-0.5
    q, grad = q_ref[...], grad_ref[...]

    def across(left, right):
        dims = (((1,), (1,)), ((), ()))
        return lax.dot_general(left, right, dims, preferred_element_type=F32)

    def score(i, top):
        scores = across(kv_ref[part(i), :HEAD_SIZE], q) + bias_ref[part(i), :]
        p_ref[part(i), :] = scores
        return jnp.maximum(top, jnp.max(scores, axis=0, keepdims=True))

    top = lax.fori_loop(0, count // step, score, jnp.full((1, queries), MASKED, F32))

    def lift(i, sums):
        total, inner = sums
        exponent = jnp.exp2((p_ref[part(i), :] - top) * EXPONENT)
        p_ref[part(i), :] = exponent
        total = total + jnp.sum(exponent, axis=0, keepdims=True)
        prob_grad = across(kv_ref[part(i), HEAD_SIZE:], grad)
        dp_ref[part(i), :] = prob_grad
        return total, inner + jnp.sum(exponent * prob_grad, axis=0, keepdims=True)

    nothing = jnp.zeros((1, queries), F32)
    total, inner = lax.fori_loop(0, count // step, lift, (nothing, nothing))
    share = 1.0 / total
    inner = inner * share
    dq_ref[...] = jnp.zeros_like(dq_ref)

    def back(i, carry):
        probs = p_ref[part(i), :] * share
        score_grad = (probs * (dp_ref[part(i), :] - inner)).astype(BF)
        dkv_ref[part(i), HEAD_SIZE:] += jnp.dot(
            probs.astype(BF), grad, preferred_element_type=F32
        )
        dkv_ref[part(i), :HEAD_SIZE] += (
            jnp.dot(score_grad, q, preferred_element_type=F32) * scale
        )
        dq_ref[...] += jnp.dot(kt_ref[:, part(i)], score_grad, preferred_element_type=F32)
        return carry

    lax.fori_loop(0, count // step, back, 0)
    out_ref[...], gain_grad = unturned(
        dq_ref[...].T * scale, proj_ref[...], cos_ref[...], sin_ref[...], gain_ref[...]
    )
    gain_grad_ref[...] += gain_grad


def attention_backward(
    q, grad, projected, keys_values, keys_turned, place, low, high, cosine, sine, gain
):
    rows, columns = q.shape
    count = keys_values.shape[0]
    step, whole, head, along, down, limit = attention_blocks(rows, count)
    return pl.pallas_call(
        backward_kernel,
        grid=(columns // HEAD_SIZE, rows // step),
        in_specs=[head, head, head, whole(keys_values), whole(keys_turned), whole(place)]
        + [along, along, down, down, whole(gain)],
        out_specs=[head, whole(keys_values), whole(gain)],
        out_shape=[
            jax.ShapeDtypeStruct(q.shape, BF),
            jax.ShapeDtypeStruct(keys_values.shape, F32),
            jax.ShapeDtypeStruct(gain.shape, F32),
        ],
        scratch_shapes=[pltpu.VMEM((count, step), F32)] * 3
        + [pltpu.VMEM((HEAD_SIZE, step), F32)],
        cost_estimate=pl.CostEstimate(
            flops=10 * rows * columns * count, bytes_accessed=8 * rows * columns, transcendentals=0
        ),
        compiler_params=pltpu.CompilerParams(vmem_limit_bytes=60 * 2**20),
    )(q, grad, projected, keys_values, keys_turned, place, low, high, cosine, sine, gain)


def pack_kernel(*refs):
    *array_refs, out_0, out_1, out_2, out_3 = refs
    rows = out_0.shape[0]
    for k, out_ref in enumerate((out_0, out_1, out_2, out_3)):
        at = 0
        for array_ref in array_refs:
            width = array_ref.shape[1]
            out_ref[:, at : at + width] = array_ref[k * rows : (k + 1) * rows, :]
            at += width


def pack_rows(*arrays):
    rows = arrays[0].shape[0] // 4
    width = sum(array.shape[1] for array in arrays)
    return pl.pallas_call(
        pack_kernel,
        out_shape=[jax.ShapeDtypeStruct((rows, width), BF)] * 4,
    )(*arrays)


def finish_kernel(ids_ref, b0, b1, b2, b3, gain_ref, low_ref, wq_ref, wk_ref, wv_ref, *refs):
    gq_ref, gk_ref, gv_ref, router_ref, out_ref, mid_ref, in_ref, q_ref, k_ref = refs
    out_ref[...] = low_ref[...].astype(F32)
    half = QW // 2
    lanes = 128
    at = QW + lanes
    first = last = 0.0
    for k, ref in enumerate((b0, b1, b2, b3)):
        head = ids_ref[0] ^ k
        block = ref[...].astype(F32)
        wide = pl.multiple_of(head * QW, QW)
        thin = pl.multiple_of(head * HEAD_SIZE, HEAD_SIZE)
        gq_ref[:, pl.ds(wide, half)] = block[:, :half]
        gq_ref[:, pl.ds(wide + half, half)] = block[:, half + lanes : at]
        gk_ref[:, pl.ds(thin, HEAD_SIZE)] = block[:, at : at + HEAD_SIZE]
        gv_ref[:, pl.ds(thin, HEAD_SIZE)] = block[:, at + HEAD_SIZE : at + 2 * HEAD_SIZE]
        first = first + block[:, half : half + lanes]
        last = last + block[:, at + 2 * HEAD_SIZE :]
    inner = 0.0
    for w_ref, g_ref in ((wq_ref, gq_ref), (wk_ref, gk_ref), (wv_ref, gv_ref)):
        inner = inner + jnp.sum(w_ref[...].astype(F32) * g_ref[...], axis=1, keepdims=True)
    experts = router_ref.shape[1]
    router_ref[...] = first[:, :experts]
    first, last = first.T, last.T
    inner = jnp.broadcast_to(inner, (inner.shape[0], lanes)).T
    mid_ref[...] = first[experts : experts + 1]
    in_ref[...] = inner[0:1] / gain_ref[...]
    part = q_ref.shape[1]
    q_ref[...] = last[0:1, :part]
    k_ref[...] = last[1:2, :part]


def finish(b, blocks, gain, low, experts, head_part, *weights):
    rows = blocks[0].shape[0]
    shapes = [weight.shape for weight in weights] + [(rows, experts), low.shape]
    shapes += [(1, rows)] * 2 + [(1, head_part)] * 2
    return pl.pallas_call(
        finish_kernel,
        in_specs=[pl.BlockSpec(memory_space=pltpu.SMEM)]
        + [pl.BlockSpec(memory_space=pltpu.VMEM)] * 9,
        out_shape=[jax.ShapeDtypeStruct(shape, F32) for shape in shapes],
    )(b.astype(jnp.int32)[None], *blocks, gain, low, *weights)


def choose_kernel(blocks, table_ref, piece_ref, *refs):
    chosen = jnp.dot(table_ref[...], piece_ref[...], preferred_element_type=F32)
    back_refs, out_refs = refs[:-blocks], refs[-blocks:]
    count = out_refs[0].shape[0]
    width = piece_ref.shape[1]
    for k, out_ref in enumerate(out_refs):
        part = chosen[k * count : (k + 1) * count].astype(BF)
        if back_refs:
            out_ref[:, :width] = part
            out_ref[:, width:] = back_refs[k][...]
        else:
            out_ref[...] = part


def choose_rows(table, piece, blocks, backs=()):
    width = piece.shape[1] + (backs[0].shape[1] if backs else 0)
    shape = (table.shape[0] // blocks, width)
    return pl.pallas_call(
        lambda *refs: choose_kernel(blocks, *refs),
        out_shape=[jax.ShapeDtypeStruct(shape, BF)] * blocks,
        compiler_params=pltpu.CompilerParams(vmem_limit_bytes=16 * 2**20),
    )(table, piece, *backs)


def collect_kernel(blocks, table_ref, *refs):
    width = refs[-1].shape[1]
    rows_in = [ref[:, ref.shape[1] - width :].astype(F32) for ref in refs[:blocks]]
    stack = jnp.concatenate(rows_in, axis=0).astype(BF)
    total = jnp.dot(table_ref[...], stack, preferred_element_type=F32)
    if len(refs) > blocks + 1:
        total = total + refs[blocks][...].astype(F32)
    refs[-1][...] = total.astype(refs[-1].dtype)


def collect_rows(table, blocks, width, more=None, kind=BF):
    extra = [] if more is None else [more]
    return pl.pallas_call(
        lambda *refs: collect_kernel(len(blocks), *refs),
        out_shape=jax.ShapeDtypeStruct((table.shape[0], width), kind),
        compiler_params=pltpu.CompilerParams(vmem_limit_bytes=24 * 2**20),
    )(table, *blocks, *extra)


def expert_kernel(blocks, me_ref, *refs):
    rows_refs, refs = refs[:blocks], refs[blocks:]
    upstream_ref, chooser_ref, router_ref, gate_ref, up_ref, down_ref = refs[:6]
    back_refs, mixed_refs = refs[6 : 6 + blocks], refs[6 + blocks : 6 + 2 * blocks]
    refs = refs[6 + 2 * blocks :]
    rows_ref, act_ref, out_grad_ref, gate_low_ref, up_low_ref = refs[:5]
    share_ref, returned_ref, pair_ref = refs[5:]
    step = pl.program_id(0)
    across = (((1,), (1,)), ((), ()))

    @pl.when(step == 0)
    def _():
        rows_in = jnp.concatenate([ref[...].astype(F32) for ref in rows_refs], axis=0).astype(BF)
        upstream = upstream_ref[...].astype(F32)
        logits = jnp.dot(rows_in, router_ref[...], preferred_element_type=F32)
        chosen = chooser_ref[...] > 0.0
        top = jnp.max(jnp.where(chosen, logits, MASKED), axis=1, keepdims=True)
        exponent = jnp.where(chosen, jnp.exp(jnp.where(chosen, logits - top, 0.0)), 0.0)
        total = jnp.sum(exponent, axis=1, keepdims=True)
        number = lax.broadcasted_iota(jnp.int32, exponent.shape, 1)
        mine = jnp.sum(jnp.where(number == me_ref[0], exponent, 0.0), axis=1, keepdims=True)
        share = mine / jnp.where(total > 0.0, total, 1.0)
        rows_ref[...] = rows_in
        out_grad_ref[...] = (share * upstream).astype(BF)
        share_ref[...] = jnp.broadcast_to(share, share_ref.shape)
        returned_ref[...] = jnp.zeros_like(returned_ref)
        pair_ref[...] = jnp.zeros_like(pair_ref)

    rows_in, out_grad = rows_ref[...], out_grad_ref[...]
    gate, up, down = gate_ref[...], up_ref[...], down_ref[...]
    gate_pre = jnp.dot(rows_in, gate, preferred_element_type=F32)
    up_pre = jnp.dot(rows_in, up, preferred_element_type=F32)
    act_grad = lax.dot_general(out_grad, down, across, preferred_element_type=F32)
    logistic = jax.nn.sigmoid(gate_pre)
    silu = gate_pre * logistic
    act = (silu * up_pre).astype(BF)
    gate_low = (act_grad * up_pre * logistic * (1.0 + gate_pre * (1.0 - logistic))).astype(BF)
    up_low = (act_grad * silu).astype(BF)
    act_ref[...], gate_low_ref[...], up_low_ref[...] = act, gate_low, up_low
    returned_ref[...] += jnp.dot(act, down, preferred_element_type=F32)
    pair_ref[...] += lax.dot_general(
        gate_low, gate, across, preferred_element_type=F32
    ) + lax.dot_general(up_low, up, across, preferred_element_type=F32)

    @pl.when(step == pl.num_programs(0) - 1)
    def _():
        returned = returned_ref[...].astype(BF).astype(F32)
        upstream = upstream_ref[...].astype(F32)
        gate_grad = jnp.sum(upstream * returned, axis=1, keepdims=True)
        mixed = share_ref[:, :1] * returned
        pair = pair_ref[...]
        count = rows_refs[0].shape[0]
        width = pair.shape[1]
        number = lax.broadcasted_iota(jnp.int32, share_ref.shape, 1)
        gates = jnp.where(number == me_ref[0], gate_grad, 0.0)
        for k in range(blocks):
            part = slice(k * count, (k + 1) * count)
            back_refs[k][:, :width] = pair[part].astype(BF)
            back_refs[k][:, width:] = gates[part].astype(BF)
            mixed_refs[k][...] = mixed[part].astype(BF)


def expert_rows(me, rows_in, upstream, chooser, router, gate, up, down):
    blocks = len(rows_in)
    slots, width = upstream.shape
    block = (slots // blocks, width)
    ff = gate.shape[1]
    step = 256
    lanes = 128
    whole = lambda shape: pl.BlockSpec(shape, lambda i: (0, 0))
    columns = lambda height: pl.BlockSpec((height, step), lambda i: (0, i))
    shape = jax.ShapeDtypeStruct
    out = [((block[0], width + lanes), BF)] * blocks + [(block, BF)] * blocks
    out_specs = [whole(dims) for dims, _ in out]
    out_specs += [whole((slots, width)), columns(slots), whole((slots, width))]
    out_specs += [columns(slots)] * 2
    out += [((slots, width), BF), ((slots, ff), BF), ((slots, width), BF)]
    out += [((slots, ff), BF)] * 2
    return pl.pallas_call(
        lambda *refs: expert_kernel(blocks, *refs),
        grid=(ff // step,),
        in_specs=[pl.BlockSpec(memory_space=pltpu.SMEM)]
        + [whole(block)] * blocks
        + [whole(upstream.shape), whole(chooser.shape), whole(router.shape)]
        + [columns(width), columns(width), pl.BlockSpec((step, width), lambda i: (i, 0))],
        out_specs=out_specs,
        out_shape=[shape(dims, kind) for dims, kind in out],
        scratch_shapes=[
            pltpu.VMEM((slots, lanes), F32),
            pltpu.VMEM((slots, width), F32),
            pltpu.VMEM((slots, width), F32),
        ],
        cost_estimate=pl.CostEstimate(
            flops=12 * slots * width * ff, bytes_accessed=6 * width * ff, transcendentals=0
        ),
        compiler_params=pltpu.CompilerParams(vmem_limit_bytes=44 * 2**20),
    )(me, *rows_in, upstream, chooser, router, gate, up, down)


def table_kernel(capacity, ids_ref, pairs_ref, send_ref, back_ref, chosen_ref):
    mine_a, mine_b = ids_ref[0], ids_ref[1]
    slots, tokens = send_ref.shape[1:]
    experts = chosen_ref.shape[2]
    numbers = lax.broadcasted_iota(jnp.int32, (slots, tokens), 0).astype(F32)
    nowhere = 1e6

    def table(source, expert, k):
        hit = pairs_ref[0, source, 0] == expert.astype(F32)
        order = pairs_ref[0, source, 1] * 32.0 + pairs_ref[0, source, 2]
        place = jnp.min(jnp.where(hit, order, nowhere), axis=0, keepdims=True)
        across = jnp.broadcast_to(place, (tokens, tokens))
        before = jnp.where(across.T < across, 1.0, 0.0)
        rank = jnp.sum(before, axis=0, keepdims=True)
        inside = (place < nowhere) & (rank < capacity)
        rank = jnp.where(inside, rank + k * capacity, -1.0)
        return jnp.where(numbers == rank, 1.0, 0.0)

    send = chosen = 0.0
    for k in range(4):
        send = send + table(0, mine_a * 4 + (mine_b ^ k), k)
        kept = table(k, mine_a * 4 + mine_b, k)
        routes = pairs_ref[0, k, 0]
        expert_rows = lax.broadcasted_iota(jnp.int32, (experts, tokens), 0).astype(F32)
        chooser = sum(
            jnp.where(routes[j : j + 1] == expert_rows, 1.0, 0.0) for j in range(TOP)
        )
        chosen = chosen + lax.dot_general(
            kept.astype(BF),
            chooser.astype(BF),
            (((1,), (1,)), ((), ())),
            preferred_element_type=F32,
        )
    send_ref[0] = send.astype(BF)
    back_ref[0] = send.T.astype(BF)
    chosen_ref[0] = chosen


def slot_tables(ids, pairs, capacity, experts):
    planes, _, _, _, tokens = pairs.shape
    slots = 4 * capacity
    block = lambda *shape: pl.BlockSpec((1,) + shape, lambda i: (i,) + (0,) * len(shape))
    return pl.pallas_call(
        lambda *refs: table_kernel(capacity, *refs),
        grid=(planes,),
        in_specs=[pl.BlockSpec(memory_space=pltpu.SMEM), block(4, 3, TOP, tokens)],
        out_specs=[block(slots, tokens), block(tokens, slots), block(slots, experts)],
        out_shape=[
            jax.ShapeDtypeStruct((planes, slots, tokens), BF),
            jax.ShapeDtypeStruct((planes, tokens, slots), BF),
            jax.ShapeDtypeStruct((planes, slots, experts), F32),
        ],
    )(ids, pairs)


def places(slot_rows, lengths_row):
    seq_ends = jnp.cumsum(lengths_row)
    starts = seq_ends - lengths_row
    segment = jnp.sum((slot_rows[:, None] >= seq_ends[None, :]).astype(jnp.int32), axis=1)
    chosen = segment[:, None] == jnp.arange(lengths_row.shape[0], dtype=jnp.int32)[None, :]
    start_of = jnp.sum(jnp.where(chosen, starts[None, :], 0), axis=1)
    return (segment, slot_rows - start_of)


def pick(blocks, index):
    return lax.dynamic_index_in_dim(blocks, index, 0, keepdims=False)


class Rounds:
    def __init__(self):
        self.active = {}
        self.asked = {}
        self.values = {}
        self.count = 0
        self.strict = True
        self.alone = None

    def start(self, task):
        self.count += 1
        self.active[self.count] = (task, None)
        return self.count

    def until(self, *wanted):
        def waiting_now():
            ready = [n for n in self.active if n in self.alone] if self.alone else self.active
            return [number for number in ready if number not in self.asked]

        while True:
            while waiting := waiting_now():
                for number in waiting:
                    task, came = self.active[number]
                    try:
                        self.asked[number] = task.send(came)
                    except StopIteration as end:
                        self.values[number] = end.value
                        del self.active[number]
            if all(number in self.values for number in wanted):
                break
            asked = {n: c for n, c in self.asked.items() if not self.alone or n in self.alone}
            given = {number: [args for _, args in calls] for number, calls in asked.items()}
            if self.strict:
                given = lax.optimization_barrier(given)
            came = {
                number: [call(*args) for (call, _), args in zip(calls, given[number])]
                for number, calls in asked.items()
            }
            if self.strict:
                came = lax.optimization_barrier(came)
            for number, results in came.items():
                self.active[number] = (self.active[number][0], results)
            self.asked = {n: calls for n, calls in self.asked.items() if n not in asked}
        values = [self.values[number] for number in wanted]
        return values[0] if len(values) == 1 else values

    def run(self, task):
        return self.until(self.start(task))

    def loosely(self, *wanted, also=None):
        self.strict, self.alone = False, None if also is None else wanted + also
        values = self.until(*wanted)
        self.strict, self.alone = True, None
        return values


def hold(count, *values):
    for _ in range(count):
        (values,) = yield [(lambda *v: v, values)]
    return values


def later(count, task):
    yield from hold(count)
    return (yield from task)


def work(function, *args):
    (result,) = yield [(function, args)]
    return result


class Links:
    def __init__(self, n):
        self.n = n
        self.planes = n // 4
        index = lax.axis_index("expert")
        self.g = lax.axis_index("dp")
        self.index = index
        self.p = index % 4
        self.l = index // 4
        self.square = n == 16
        if self.square:
            self.a = index % 2 + index // 8 * 2
            self.b = index // 2 % 2 * 2 + index // 4 % 2
        else:
            self.a, self.b = self.l, self.p
        masks = (0, 4, 2, 6) if self.square else (0, 1, 2, 3)
        self.places = [lambda v, k=k: self.flip(v, k) for k in range(4)]
        self.heads = [lambda v, m=m: self.flip(v, m) for m in masks]
        self.shifts = [lambda v, s=s: self.shift(v, s) for s in range(self.planes)]
        self.backs = [lambda v, s=s: self.shift(v, -s) for s in range(self.planes)]

    def device(self, a, b):
        if not self.square:
            return a * 4 + b
        return a % 2 + b // 2 * 2 + b % 2 * 4 + a // 2 * 8

    def row_block(self, g, a):
        return a % 2 + g * 2 + a // 2 * 4 if self.square else g * self.planes + a

    def block(self, r):
        return self.a ^ r if self.square else (self.a - r) % self.planes

    def flip(self, value, mask):
        return lax.ppermute(value, "expert", [(i, i ^ mask) for i in range(self.n)])

    def shift(self, value, step):
        return lax.ppermute(
            value, "expert", [(i, (i + step * 4) % self.n) for i in range(self.n)]
        )

    def onward(self, value):
        return self.shift(value, 1)

    def twin(self, value):
        return lax.ppermute(value, "dp", [(0, 1), (1, 0)])

    def natural(self, blocks, mine):
        odd, high = mine % 2 == 1, mine >= 2
        pair = [jnp.where(odd, blocks[q ^ 1], blocks[q]) for q in range(4)]
        return [jnp.where(high, pair[q ^ 2], pair[q]) for q in range(4)]

    def turned_line(self, blocks):
        twice = jnp.concatenate([blocks[::-1], blocks[::-1]], axis=0)
        return lax.dynamic_slice_in_dim(twice, self.planes - 1 - self.l, self.planes, 0)

    def head_gather(self, own):
        half = own.shape[0] // 2
        near_x, near_y = yield [(self.heads[1], (own,)), (self.heads[2], (own,))]
        low, high = yield [(self.heads[2], (near_x[:half],)), (self.heads[1], (near_y[half:],))]
        return jnp.concatenate([own, near_x, near_y, low, high], axis=0)

    def exchange(self, flips, blocks):
        came = yield [(flips[k], (blocks[k],)) for k in (3, 1, 2)]
        return [blocks[0], came[1], came[2], came[0]]

    def head_scatter(self, total):
        count = total.shape[0] // 4
        half = count // 2
        cut = lambda k, low, high: total[k * count + low : k * count + high]
        low, high = yield [
            (self.heads[2], (cut(3, 0, half).astype(BF),)),
            (self.heads[1], (cut(3, half, count).astype(BF),)),
        ]
        to_x = jnp.concatenate([cut(1, 0, half) + low.astype(F32), cut(1, half, count)], axis=0)
        to_y = jnp.concatenate([cut(2, 0, half), cut(2, half, count) + high.astype(F32)], axis=0)
        got_x, got_y = yield [
            (self.heads[1], (to_x.astype(BF),)),
            (self.heads[2], (to_y.astype(BF),)),
        ]
        return cut(0, 0, count) + got_x.astype(F32) + got_y.astype(F32)

    def block_gather(self, own, idle=(0, 0), count=None, give=None):
        if not self.square:
            came = yield [(shift, (own,)) for shift in self.shifts[1:]]
            return [own] + came
        x, z = (lambda v: self.flip(v, 1)), (lambda v: self.flip(v, 8))
        count = count or own.shape[0]
        half = count // 2 + own.shape[0] - count
        near, low = yield [(x, (own,)), (z, (own[:half],))]
        near, low = yield from hold(idle[0], near, low)
        rest = count - half
        more = [own[half:]] if give is None else [own[half:], near[count:]]
        high, far_low = yield [(z, (jnp.concatenate(more),)), (x, (low,))]
        high, far_low = yield from hold(idle[1], high, far_low)
        if give is not None:
            give(jnp.concatenate([own[count:], near[count:], high[rest:]]))
        (far_high,) = yield [(x, (high[:rest],))]
        return [
            own,
            near,
            jnp.concatenate([low, high[:rest]], axis=0),
            jnp.concatenate([far_low, far_high], axis=0),
        ]

    def block_gather_short(self, own):
        if not self.square:
            came = yield [(shift, (own,)) for shift in self.shifts[1:]]
            return [own] + came
        x, z = (lambda v: self.flip(v, 1)), (lambda v: self.flip(v, 8))
        near, across = yield [(x, (own,)), (z, (own,))]
        (far,) = yield [(x, (across,))]
        return [own, near, across, far]

    def block_scatter(self, blocks, split=False, idle=0):
        if not self.square:
            came = yield [
                (back, (block.astype(BF),)) for back, block in zip(self.backs[1:], blocks[1:])
            ]
            return sum((block.astype(F32) for block in came), blocks[0].astype(F32))
        x, z = (lambda v: self.flip(v, 1)), (lambda v: self.flip(v, 8))
        (came,) = yield [(x, (blocks[3].astype(BF),))]
        (came,) = yield from hold(idle, came)
        across = (blocks[2].astype(F32) + came.astype(F32)).astype(BF)
        if split:
            half = across.shape[0] // 2
            (got,) = yield [(z, (across[:half],))]
            near, more = yield [(x, (blocks[1].astype(BF),)), (z, (across[half:],))]
            got = jnp.concatenate([got, more], axis=0)
        else:
            near, got = yield [(x, (blocks[1].astype(BF),)), (z, (across,))]
        return blocks[0].astype(F32) + near.astype(F32) + got.astype(F32)

    def twin_scatter(self, make, own, other, idle=None, now=False, rest=0):
        low = lambda *args: make(*args).astype(BF)
        if now:
            block = low(*other)
        else:
            (block,) = yield [(low, other)]
            (block,) = yield from hold(rest, block)
        if idle is None:
            came, total = yield [(self.twin, (block,)), (make, own)]
            return total + came.astype(F32)
        (came,) = yield [(self.twin, (block,))]
        (came,) = yield from hold(idle, came)
        (total,) = yield [(lambda came, *args: make(*args) + came.astype(F32), (came, *own))]
        return total


def body(
    hidden,
    lengths,
    slots,
    routes,
    order,
    gain_in,
    w_query,
    key_projection_weight,
    value_projection_weight,
    gain_q,
    gain_k,
    w_out,
    gain_mid,
    w_router,
    w_gate,
    w_up,
    w_down,
    cotangent,
):
    tokens = hidden.shape[0]
    experts = w_router.shape[1]
    links = Links(experts)
    planes = links.planes
    capacity = max(2, (tokens * TOP * 9 + 8 * experts - 1) // (8 * experts))
    block_tokens = 4 * tokens
    rows = gain_in.shape[0]
    head_part = gain_q.shape[0]
    devices = 2 * experts

    rounds = Rounds()
    spread = rounds.start
    slot_count = 4 * capacity

    gate_full = lax.all_gather(w_gate, "dp", axis=1, tiled=True)[0]
    up_full = lax.all_gather(w_up, "dp", axis=1, tiled=True)[0]
    down_full = lax.all_gather(w_down, "dp", axis=2, tiled=True)[0]

    lanes = 128
    gains = jnp.concatenate([gain_in, gain_mid, gain_q, gain_k], axis=0)
    gain_count = gains.shape[0]
    gains = jnp.pad(gains, (0, -gain_count % lanes)).reshape(-1, lanes)
    router_rows = rows * experts // lanes
    small = jnp.concatenate([w_router.reshape(-1, lanes), gains], axis=0)
    small = jnp.pad(small, ((0, -small.shape[0] % 8), (0, 0)))
    small_rows = small.shape[0]
    pairs = jnp.concatenate([part.T.astype(BF) for part in (routes, order // 32, order % 32)])
    expert_numbers = jnp.arange(experts, dtype=jnp.int32)
    ids = jnp.stack([links.l, links.p]).astype(jnp.int32)
    tables = {}

    qkv_width = QW + 2 * HEAD_SIZE
    rider = jnp.concatenate([small, pairs], axis=0)
    rider_rows = rider.shape[0]

    def own_columns(b):
        cut = lambda array, width: lax.dynamic_slice_in_dim(array, b * width, width, 1)
        return jnp.concatenate(
            [
                cut(w_query, QW),
                cut(key_projection_weight, HEAD_SIZE),
                cut(value_projection_weight, HEAD_SIZE),
            ],
            axis=1,
        )

    def gather_qkv():
        blocks = [own_columns(links.b ^ k) for k in range(4)]
        if not links.square:
            blocks = yield from links.exchange(links.heads, blocks)
            pieces = yield from links.block_gather(jnp.concatenate(blocks, axis=0))
            others = yield [(links.twin, (piece,)) for piece in pieces]
            return pieces + others
        more = rider.reshape(-1, qkv_width)
        held = more.shape[0]
        more = jnp.pad(more, ((0, -held % 8), (0, 0)))
        blocks = [jnp.concatenate([block, more], axis=0) for block in blocks]
        blocks = yield from links.exchange(links.heads, blocks)
        wide = stack_rows(blocks, rows)

        def give(found):
            found = found.reshape(4, 4, -1, qkv_width)[:, :, :held]
            tables["riders"] = found.reshape(4, 4, rider_rows, lanes)

        pieces = yield from links.block_gather(wide, count=4 * rows, give=give)
        others = yield [(links.twin, (piece,)) for piece in pieces]
        return pieces + others

    def gather_small():
        if links.square:
            yield from hold(3)
            parts = tables["riders"]
            parts = jnp.stack(links.natural([parts[r] for r in range(4)], links.a))
            parts = jnp.stack(links.natural([parts[:, k] for k in range(4)], links.b), axis=1)
            parts = parts.reshape(2, 2, 2, 2, rider_rows, lanes).transpose(0, 3, 2, 1, 4, 5)
            parts = parts.reshape(experts, rider_rows, lanes)
        else:
            blocks = yield from links.exchange(links.places, [rider] * 4)
            line = jnp.stack(links.natural(blocks, links.p))
            came = yield [(shift, (line,)) for shift in links.shifts[1:]]
            parts = links.turned_line(jnp.stack([line] + came))
            parts = parts.reshape(experts, rider_rows, lanes)
            yield from hold(1)
        own_small = parts[:, :small_rows]
        (other_small,) = yield [(links.twin, (own_small,))]
        tables["pairs"] = parts[:, small_rows:]
        return (yield from work(sort_small, own_small, other_small, rounds.values[hidden_task]))

    def sort_small(own_small, other_small, block_hidden):
        swap = links.g == 1
        small_all = jnp.concatenate(
            [jnp.where(swap, other_small, own_small), jnp.where(swap, own_small, other_small)]
        )
        gains = small_all[:, router_rows:].reshape(devices, -1)
        head_gains = gains[:, 2 * rows : gain_count].reshape(devices, 2, head_part)
        values = block_hidden.astype(F32)
        scale = lax.rsqrt(jnp.mean(values * values, axis=-1, keepdims=True) + EPS)
        full_in = gains[:, :rows].reshape(MODEL_WIDTH).astype(F32)
        return (
            (values * scale * full_in).astype(BF),
            small_all[:, :router_rows].reshape(MODEL_WIDTH, experts),
            full_in,
            gains[:, rows : 2 * rows].reshape(MODEL_WIDTH).astype(F32),
            head_gains.swapaxes(0, 1).reshape(2, HEAD_SIZE).astype(F32),
        )

    def make_tables(pairs):
        pairs = pairs.astype(F32).reshape(planes, 4, 3, TOP, tokens)
        pairs = links.turned_line(pairs)
        near = [lax.dynamic_index_in_dim(pairs, links.p ^ k, 1, keepdims=False) for k in range(4)]
        return slot_tables(ids, jnp.stack(near, axis=1), capacity, experts)

    exchange_task = spread(hold(1))
    qkv_task = spread(gather_qkv())

    def gather_hidden():
        (value,) = yield from hold(1, hidden)
        return (yield from links.head_gather(value))

    hidden_task = spread(gather_hidden())
    small_task = spread(gather_small())

    aligned = capacity % 8 == 0

    def choose(piece, step, backs=()):
        found = choose_rows(tables["send"][step], piece, 4 if aligned else 1, as_blocks(backs))
        return found if aligned else by_place(found[0])

    def by_place(slot_rows):
        return [slot_rows[k * capacity : (k + 1) * capacity] for k in range(4)]

    def as_blocks(blocks):
        return blocks if aligned or not blocks else [jnp.concatenate(blocks, axis=0)]

    def collect(blocks, step, width, more=None, kind=BF):
        return collect_rows(tables["back"][step], as_blocks(blocks), width, more, kind)

    def in_places(own, came):
        return [own, came[0], came[1], came[2]]

    def to_places(blocks):
        return [(links.places[k], (blocks[k],)) for k in (1, 2, 3)]

    def gather_upstream():
        pieces, out = [cotangent], []
        yield from hold(2)
        found = yield from work(make_tables, tables["pairs"])
        tables["send"], tables["back"], tables["chooser"] = found
        plan = [(1, True, 0)] + [(0, s < planes - 1, s) for s in range(1, planes)]
        for idle, hop, step in plan:
            yield from hold(idle)
            asks = [(links.onward, (pieces[-1],))] if hop else []
            if step is not None:
                blocks = choose(pieces[step], step)
                asks += to_places(blocks)
            came = yield asks
            if hop:
                pieces.append(came[0])
            if step is not None:
                out.append(jnp.concatenate([blocks[0]] + came[-3:], axis=0))
        return out

    upstream_task = spread(gather_upstream())

    head_rows = w_out.shape[0]
    if links.square:
        pairs_of = [(g, i) for g in range(2) for i in range(experts)]
        line = lambda i: i & 3 | (i >> 3 & 1) << 2 | (i >> 2 & 1) << 3
        swap_line = [(g * experts + i, g * experts + line(i)) for g, i in pairs_of]
        swap_core = [
            (g * experts + i, (i >> 1 & 1) * experts + (i & 13 | g << 1)) for g, i in pairs_of
        ]
        bit = lambda k: links.index // (1 << k) % 2
        moves = bit(2) != bit(3), bit(1) != links.g
        back = ((swap_line, moves[0]), (swap_core, moves[1]))
        onto = dict(swap_core)
        there = ([(i, onto[j]) for i, j in swap_line], moves[0] | moves[1])
    else:
        to_block = [
            (b * 2 * planes + links.row_block(g, a), g * experts + links.device(a, b))
            for g in range(2)
            for a in range(planes)
            for b in range(4)
        ]
        there = (to_block, True)
        back = (([(to, of) for of, to in to_block], True), None)

    def moved(value, swap):
        if swap is None:
            return value
        pairs_of, moves = swap
        if moves is True:
            return lax.ppermute(value, ("dp", "expert"), pairs_of)
        came = lax.ppermute(value, ("dp", "expert"), [(i, j) for i, j in pairs_of if i != j])
        return jnp.where(moves, came, value)

    def gather_out():
        pieces = yield from links.block_gather(rounds.values[move_task], (1, 0))
        pieces = jnp.concatenate(pieces, axis=0)
        (others,) = yield [(links.twin, (pieces,))]
        return pieces, others

    move_task = spread(work(lambda value: moved(value, there), w_out))

    device_of = jnp.stack(
        [links.device(links.block(r), links.b ^ k) for r in range(planes) for k in range(4)]
    )
    starts = jnp.concatenate([(links.g ^ t) * experts + device_of for t in range(2)]) * rows
    all_slots = slots.reshape(experts, tokens)[device_of].reshape(experts * tokens)
    _, position = places(all_slots[:block_tokens], lengths[0])
    cosine, sine = rotary_tables(position)
    high = all_slots[:block_tokens]
    low = high - position

    rounds.until(exchange_task)
    found, block_hidden, qkv_pieces, _ = rounds.loosely(
        small_task, hidden_task, qkv_task, move_task, also=()
    )
    out_task = spread(gather_out())
    normalized, full_router, full_in, full_mid, head_gains = found
    w_qkv, projected, turned = rounds.run(
        work(
            lambda *args: project(rows, *args),
            starts,
            normalized,
            cosine,
            sine,
            head_gains,
            *qkv_pieces,
        )
    )
    keys_values = jnp.concatenate(
        rounds.run(links.block_gather_short(turned[:, QW:])), axis=0
    )
    keys_turned = keys_values[:, :HEAD_SIZE].T
    values_turned = keys_values[:, HEAD_SIZE:].T
    place_column = all_slots[:, None]
    low, high = low[None, :], high[None, :]

    def part_of(array, part, parts):
        width = array.shape[1] // parts
        return array[:, part * width : (part + 1) * width]

    def forward_part(query_rows):
        return attention_forward(query_rows, keys_values, values_turned, place_column, low, high)

    bounds = [0, PER_KV // 2, PER_KV]
    attended = [
        rounds.run(work(forward_part, turned[:, low_head * HEAD_SIZE : high_head * HEAD_SIZE]))
        for low_head, high_head in zip(bounds, bounds[1:])
    ]
    block_out = rounds.until(out_task)
    if head_rows == HEAD_SIZE:
        order_of = [
            links.row_block(links.g ^ t, links.block(r)) for t in range(2) for r in range(planes)
        ]
        order_of = jnp.stack(order_of).astype(jnp.int32)
    else:
        attended = jnp.concatenate(attended, axis=1)
        attended = [
            lax.dynamic_slice_in_dim(
                attended, links.row_block(links.g ^ t, links.block(r)) * head_rows, head_rows, 1
            )
            for t in range(2)
            for r in range(planes)
        ]
        attended = [jnp.concatenate(attended, axis=1)]
        order_of = jnp.arange(PER_KV, dtype=jnp.int32)
    branch, attended = rounds.run(
        work(lambda *parts: output_projection(order_of, parts, *block_out), *attended)
    )
    branch = rounds.loosely(spread(links.head_scatter(branch)))
    x_float = hidden.astype(F32)
    x_one = x_float + branch
    norm_two, norm_two_back = jax.vjp(rms_scale, x_one, full_mid)
    xn_two = norm_two.astype(BF)

    own_chooser = jnp.any(routes[:, :, None] == expert_numbers, axis=1)

    def masked_softmax(logits, chooser):
        top = jnp.max(jnp.where(chooser, logits, MASKED), axis=-1, keepdims=True)
        exponent = jnp.where(chooser, jnp.exp(jnp.where(chooser, logits - top, 0.0)), 0.0)
        total = jnp.sum(exponent, axis=-1, keepdims=True)
        return exponent / jnp.where(total > 0.0, total, 1.0)

    upstream_slots = rounds.until(upstream_task)
    me = links.index.astype(jnp.int32)[None]
    made = []

    def expert_step(step, *rows_in):
        found = expert_rows(
            me,
            as_blocks(list(rows_in)),
            upstream_slots[step],
            tables["chooser"][step],
            full_router,
            gate_full,
            up_full,
            down_full,
        )
        if aligned:
            return (found[:4], found[4:8], found[8:])
        return (by_place(found[0]), by_place(found[1]), found[2:])

    def return_mixture():
        def add(step, came, back, kind=BF):
            blocks = in_places(made[step][1][0], back)
            return collect(blocks, step, MODEL_WIDTH, came, kind)

        back = yield to_places(made[1][1])
        total = add(1, None, back)
        yield from hold(2)
        came, *back = yield [(links.onward, (total,))] + to_places(made[2][1])
        total = add(2, came, back)
        for step in range(3, planes):
            came, *back = yield [(links.onward, (total,))] + to_places(made[step][1])
            total = add(step, came, back)
        came, *back = yield [(links.onward, (total,))] + to_places(made[0][1])
        return add(0, came, back, F32)

    def experts_there_and_back():
        piece, ready, own_plane, total = xn_two, None, None, None
        wide = MODEL_WIDTH + lanes
        for step in range(planes + 3):
            asks = []
            back = made[step - 2][0] if 2 <= step < planes + 2 else []
            blocks = back
            if step < planes:
                blocks = choose(piece, step, back)
            if blocks:
                asks += to_places(blocks)
            if step < planes - 1:
                asks += [(links.onward, (piece,))]
            if step >= 4:
                asks += [(links.onward, (total,))]
            if 1 <= step <= planes:
                asks += [(lambda *v, s=step - 1: expert_step(s, *v), tuple(ready))]
            if step == planes + 2:
                tables["mixture"] = spread(return_mixture())
            came = yield asks
            if blocks:
                ready, came = in_places(blocks[0], came[:3]), came[3:]
            if step < planes - 1:
                piece, came = came[0], came[1:]
            if step >= 4:
                hop, came = came[0], came[1:]
            if 1 <= step <= planes:
                made.append(came[0])
            if step == 2:
                own_plane = collect(ready, 0, wide, None, F32)
            elif step == 3:
                total = collect(ready, 1, wide)
            elif step >= 4 and step < planes + 2:
                total = collect(ready, step - 2, wide, hop)
        return own_plane + hop.astype(F32)

    moe_grad = rounds.run(experts_there_and_back())
    gate_grads = moe_grad[:, MODEL_WIDTH : MODEL_WIDTH + experts]
    moe_grad = moe_grad[:, :MODEL_WIDTH]
    stacked = lambda place: jnp.concatenate([piece[2][place] for piece in made], axis=0)

    def by_rows(rows_in, grads_in):
        return jnp.einsum("rd,rf->df", rows_in, grads_in, preferred_element_type=F32)

    half_width = MODEL_WIDTH // 2

    def half_of(array, which):
        return lax.dynamic_slice_in_dim(array, which * half_width, half_width, 1)

    def gate_up_gradient(place, idle, rest):
        rows_in, grads_in = stacked(0), stacked(place)
        make = lambda which: by_rows(half_of(rows_in, which), grads_in)
        return links.twin_scatter(make, (links.g,), (1 - links.g,), idle=idle, rest=rest)

    def down_gradient():
        rows_in, grads_in = stacked(1), stacked(2)
        make = lambda which: by_rows(rows_in, half_of(grads_in, which))
        return links.twin_scatter(make, (links.g,), (1 - links.g,), idle=2)

    gate_task = spread(gate_up_gradient(3, 5, 0))
    up_task = spread(later(1, gate_up_gradient(4, 2, 3)))
    down_task = spread(later(5, down_gradient()))

    def route(rows_in):
        logits = jnp.dot(rows_in, full_router, preferred_element_type=F32)
        return masked_softmax(logits, own_chooser)

    own_probs = route(lax.optimization_barrier((xn_two, moe_grad))[0])

    upstream = cotangent.astype(F32)
    chosen_grad = own_probs * (
        gate_grads - jnp.sum(own_probs * gate_grads, axis=-1, keepdims=True)
    )
    logit_grad = chosen_grad.astype(BF)
    xn_two_grad = moe_grad + jnp.dot(logit_grad, full_router.T, preferred_element_type=F32)
    x_one_norm_grad, grad_mid = norm_two_back(xn_two_grad)
    x_one_grad = upstream + x_one_norm_grad
    branch_grad = x_one_grad.astype(BF)

    block_grad = rounds.loosely(spread(links.head_gather(branch_grad)))

    def head_gradients(block_grad):
        grad = [
            jnp.einsum("td,hd->th", block_grad, part, preferred_element_type=F32).astype(BF)
            for part in block_out
        ]
        grad = jnp.concatenate(grad, axis=1)
        parts = []
        where = {links.row_block(g, a): (g, a) for g in range(2) for a in range(planes)}
        for head in range(2 * planes):
            g, a = where[head]
            at = ((links.g ^ g) * planes + links.block(a)) * head_rows
            parts.append(lax.dynamic_slice_in_dim(grad, at, head_rows, 1))
        return jnp.concatenate(parts, axis=1)

    heads_task = spread(work(head_gradients, block_grad))

    def scatter_out():
        half = QW // 2
        grad = yield from links.twin_scatter(
            lambda rows_in, grads_in: jnp.einsum(
                "th,td->hd", rows_in, grads_in, preferred_element_type=F32
            ),
            (attended[:, :half], block_grad),
            (attended[:, half:], block_grad),
            now=True,
        )
        grad = grad.astype(BF)
        blocks = [grad[r * head_rows : (r + 1) * head_rows] for r in range(planes)]
        grad = yield from links.block_scatter(blocks, split=True)
        yield from hold(1)
        grad = yield from work(lambda value: moved(value, back[1]), grad.astype(BF))
        (grad,) = yield from hold(2, grad)
        return (yield from work(lambda value: moved(value, back[0]), grad))

    grad_out_task = spread(scatter_out())

    def owners_blocks(grad):
        blocks = []
        for r in range(planes):
            owners = [links.device(links.block(r), links.b ^ k) for k in range(4)]
            parts = [lax.dynamic_slice_in_dim(grad, owner * rows, rows, 0) for owner in owners]
            blocks.append(jnp.concatenate(parts, axis=0))
        return blocks

    def half_rows(array, which):
        return lax.dynamic_slice_in_dim(array, which * (MODEL_WIDTH // 2), MODEL_WIDTH // 2, 0)

    def query_gradient(grads_in, extra):
        def make(which):
            grad = by_rows(half_of(normalized, which), grads_in)
            if extra is not None:
                grad = jnp.concatenate([grad, half_rows(extra, which)], axis=1)
            return grad

        grad = yield from links.twin_scatter(make, (links.g,), (1 - links.g,))
        grad = yield from links.block_scatter(owners_blocks(grad.astype(BF)))
        return grad.astype(BF)

    def key_value_gradient(key_value_grad, query_grads):
        sums = jnp.concatenate([grad_qgain, grad_kgain]).reshape(2, devices, head_part)
        sums = jnp.pad(sums, ((0, 0), (0, 0), (0, rows - head_part))).reshape(2, MODEL_WIDTH).T
        sums = jnp.pad(sums, ((0, 0), (0, lanes - sums.shape[1])))

        def half(which):
            grad = by_rows(half_of(normalized, which), key_value_grad)
            return jnp.concatenate([grad, half_rows(sums, which)], axis=1)

        came, xn_one_grad = yield [
            (links.twin, (half(1 - links.g).astype(BF),)),
            (
                lambda *parts: input_gradient(jnp.concatenate(parts, axis=1), w_qkv),
                (*query_grads, key_value_grad),
            ),
        ]
        tables["scatter"] = spread(links.head_scatter(xn_one_grad))
        grad = (half(links.g) + came.astype(F32)).astype(BF)
        grad = yield from links.block_scatter(owners_blocks(grad))
        return grad.astype(BF)

    attended_grad = rounds.until(heads_task)
    grad_router = jnp.dot(xn_two.T, logit_grad, preferred_element_type=F32)
    first = jnp.concatenate([grad_router, grad_mid[:, None]], axis=1)
    first = jnp.pad(first, ((0, 0), (0, lanes - first.shape[1])))
    query_low_grads, query_tasks, key_terms, grad_qgain = [], [], None, None

    parts = 2
    for part in range(parts):
        got = rounds.run(
            work(
                lambda *args: attention_backward(
                    *args,
                    keys_values,
                    keys_turned,
                    place_column,
                    low,
                    high,
                    cosine,
                    sine,
                    head_gains[0:1],
                ),
                part_of(turned[:, :QW], part, parts),
                part_of(attended_grad, part, parts),
                part_of(projected[:, :QW], part, parts),
            )
        )
        query_low_grads.append(got[0])
        key_terms = got[1] if part == 0 else key_terms + got[1]
        grad_qgain = got[2] if part == 0 else grad_qgain + got[2]
        query_tasks.append(spread(query_gradient(got[0], None if part else first)))
    key_terms = rounds.run(
        links.block_scatter(
            [key_terms[r * block_tokens : (r + 1) * block_tokens] for r in range(planes)]
        )
    )

    key_proj_grad, grad_kgain = unturn(
        key_terms[:, :HEAD_SIZE],
        projected[:, QW : QW + HEAD_SIZE],
        cosine,
        sine,
        head_gains[1:2],
    )
    key_value_grad = jnp.concatenate([key_proj_grad, key_terms[:, HEAD_SIZE:].astype(BF)], axis=1)
    key_value_task = spread(key_value_gradient(key_value_grad, query_low_grads))
    one, two, three = rounds.until(*query_tasks, key_value_task)
    xn_one_grad = rounds.until(tables["scatter"])
    query_task = spread(links.exchange(links.heads, pack_rows(one, two, three)))
    _, norm_one_back = jax.vjp(lambda values: rms_scale(values, full_in), x_float)
    (x_norm_grad,) = norm_one_back(xn_one_grad)
    input_grad = (x_one_grad + x_norm_grad).astype(BF)

    grad_gate, grad_up, grad_down, mixture, grad_out, owned = rounds.until(
        gate_task, up_task, down_task, tables["mixture"], grad_out_task, query_task
    )
    result = (x_one + mixture).astype(BF)
    weights = (w_query, key_projection_weight, value_projection_weight)
    found = finish(
        links.b, owned, gain_in.astype(F32)[None], grad_out, experts, head_part, *weights
    )
    grad_query, grad_key, grad_value, grad_router, grad_out = found[:5]
    grad_mid, grad_in, grad_qgain, grad_kgain = (row.reshape(-1) for row in found[5:])

    return (
        result,
        input_grad,
        grad_in,
        grad_query,
        grad_key,
        grad_value,
        grad_qgain,
        grad_kgain,
        grad_out,
        grad_mid,
        grad_router,
        grad_gate[None],
        grad_up[None],
        grad_down[None],
    )


def solution(mesh):
    every = ("dp", "expert")
    in_specs = (
        P(every, None),
        P("dp", None),
        P("dp"),
        P(every, None),
        P(every, None),
        P(every),
        P(every, None),
        P(every, None),
        P(every, None),
        P(every),
        P(every),
        P(every, None),
        P(every),
        P(every, None),
        P("expert", "dp", None),
        P("expert", "dp", None),
        P("expert", None, "dp"),
        P(every, None),
    )
    out_specs = (
        P(every, None),
        P(every, None),
        P(every),
        P(every, None),
        P(every, None),
        P(every, None),
        P(every),
        P(every),
        P(every, None),
        P(every),
        P(every, None),
        P("expert", "dp", None),
        P("expert", "dp", None),
        P("expert", None, "dp"),
    )
    return jax.shard_map(body, mesh=mesh, in_specs=in_specs, out_specs=out_specs, check_vma=False)
```
